32 devices in a mesh: lat: 4 (over y, core), lon: 8 (over z, x).
Axes of the slice: x: 2, y: 2, z: 4, core: 2. Of those that a mesh axis runs over, the one named last changes fastest.
Arguments:
- source_cells: bfloat16 [73, 16384], P(None, ('lat', 'lon')), may hold values from -6 to 6
- recv_src: int32 [131072], P(('lat', 'lon')), may hold values from 0 to 511
- recv_cell: int32 [131072], P(('lat', 'lon')), may hold values from 0 to 32399
- recv_weight: float32 [131072], P(('lat', 'lon')), may hold values from 0 to 1, as said below
- enc_w1: bfloat16 [256, 73], replicated, may hold values from -0.75 to 0.75
- enc_b1: float32 [256], replicated, may hold values from -3 to 3
- enc_w2: bfloat16 [256, 256], replicated, may hold values from -0.375 to 0.375
- enc_b2: float32 [256], replicated, may hold values from -3 to 3
- mix_weight: bfloat16 [2, 256, 256], replicated, may hold values from -0.25 to 0.25
- fwd_table: bfloat16 [512, 512, 720], P(('lat', 'lon')), may hold values from -0.21875 to 0.21875
- inv_table: bfloat16 [512, 720, 512], P(('lat', 'lon')), may hold values from -0.25 to 0.25
Outputs:
- layer_out: bfloat16 [256, 1036800], P(None, ('lat', 'lon'))
The draws below stay inside these ranges and needn't reach their ends.
Inputs may be any that keep to these rules, and one draw needn't show every extreme that they name: `recv_weight`: zero exactly on padding slots. For each target block and source device, the slots with nonzero weight come first; there are at most 512 of them, and for every target block one source device fills all 512.
All inputs are finite; a program needn't handle non-finite values.
Results may differ from the reference program's by a relative error of at most 0.011.
Values may be sent and summed in bfloat16 or wider, within the bound.
No kernel may reach another device: no remote copies, remote signals or barrier semaphores. Data moves between devices by JAX's collectives and lax.ppermute only.
A program may use at most 256 MiB of HBM per device.

```python
import math
import jax
import jax.numpy as jnp
from jax import lax

CIN = 73
E = 256
NLAT = 720
NLON = 1440
ORDERS = 512
DEGREES = 512
SRC_DEV = 512
CAP = 512
CELLS_DEV = 32400
N_LAT = 4
N_LON = 8


def draw_recv_weight(key, part):
    key = jax.random.fold_in(key, 11)
    key_count, key_full, key_value = jax.random.split(key, 3)
    devices = N_LAT * N_LON
    counts = jax.random.randint(key_count, (devices, N_LON), max(1, CAP // 4), CAP + 1)
    filled = jax.random.randint(key_full, (devices, 1), 0, N_LON)
    counts = jnp.where(jnp.arange(N_LON)[None, :] == filled, CAP, counts)
    live = jnp.arange(CAP)[None, None, :] < counts[:, :, None]
    values = jnp.exp(jax.random.uniform(key_value, (devices, N_LON, CAP), jnp.float32, math.log(0.05), 0.0))
    return jnp.where(live, values, 0.0).reshape(-1).astype(jnp.float32)


def set_ends(values, own_key, least, top_value):
    longest = values.shape.index(max(values.shape))
    spots = []
    for shift in (0, 1):
        where = [jax.random.randint(jax.random.fold_in(own_key, axis), (), 0, length) for axis, length in enumerate(values.shape)]
        where[longest] = (where[longest] + shift) % values.shape[longest]
        spots.append(tuple(where))
    return values.at[spots[0]].set(least).at[spots[1]].set(top_value)


def block_scale(rng, extent, cuts, least, high):
    def one(position, shards_of):
        draws = jax.random.uniform(jax.random.fold_in(jax.random.fold_in(rng, 6), position), (shards_of,), jnp.float32, least / len(cuts), high / len(cuts))
        return jnp.repeat(jnp.exp(draws), extent[position] // shards_of).reshape((-1,) + (1,) * (len(extent) - position - 1))

    loudness = one(*cuts[0])
    for cut in cuts[1:]:
        loudness = loudness * one(*cut)
    return loudness


def noise(own_key, extent, spread, most, cuts=(), held_as=jnp.bfloat16):
    level = block_scale(own_key, extent, cuts, -0.22, 0.18) if cuts else 1.0
    entries = jax.random.normal(own_key, extent, jnp.float32) * spread * level
    return jnp.minimum(jnp.maximum(entries, -most), most).astype(held_as)


def setup_inputs(seed: int = 0) -> dict:
    key_list = jax.random.split(jax.random.key(seed), 12)
    return {
        "source_cells": noise(key_list[0], (CIN, N_LAT * N_LON * SRC_DEV), 1.0, 6.0, ((1, 32),)),
        "recv_src": set_ends(jax.random.randint(key_list[1], (N_LAT * N_LON * N_LON * CAP,), 0, SRC_DEV), jax.random.fold_in(key_list[1], 1), 0, SRC_DEV - 1).astype(jnp.int32),
        "recv_cell": set_ends(jax.random.randint(key_list[2], (N_LAT * N_LON * N_LON * CAP,), 0, CELLS_DEV), jax.random.fold_in(key_list[2], 1), 0, CELLS_DEV - 1).astype(jnp.int32),
        "recv_weight": draw_recv_weight(jax.random.fold_in(key_list[11], 71), 0),
        "enc_w1": noise(key_list[4], (E, CIN), CIN ** -0.5, 0.75),
        "enc_b1": noise(key_list[5], (E,), 0.5, 3.0, (), jnp.float32),
        "enc_w2": noise(key_list[6], (E, E), E ** -0.5, 0.375),
        "enc_b2": noise(key_list[7], (E,), 0.5, 3.0, (), jnp.float32),
        "mix_weight": noise(key_list[8], (2, E, E), (2 * E) ** -0.5, 0.25),
        "fwd_table": noise(key_list[9], (ORDERS, DEGREES, NLAT), NLAT ** -0.5, 0.21875, ((0, 32),)),
        "inv_table": noise(key_list[10], (ORDERS, NLAT, DEGREES), DEGREES ** -0.5, 0.25, ((0, 32),)),
    }


def build_basis(order_list):
    points = jnp.arange(NLON, dtype=jnp.int32)
    angles = (order_list[:, None] * points[None, :] % NLON).astype(jnp.float32) * (2.0 * math.pi / NLON)
    factor = math.sqrt(2.0 / NLON)
    stacked = jnp.stack([factor * jnp.cos(angles), -factor * jnp.sin(angles)], axis=1)
    return stacked.astype(jnp.bfloat16).reshape(2 * order_list.shape[0], NLON)

def reference(source_cells, recv_src, recv_cell, recv_weight, enc_w1, enc_b1, enc_w2, enc_b2, mix_weight, fwd_table, inv_table):
    lat_dev = NLAT // N_LAT
    lon_dev = NLON // N_LON
    cells_dev = lat_dev * lon_dev
    band_cells = source_cells.reshape(CIN, N_LAT, N_LON * SRC_DEV).transpose(1, 0, 2)
    band_src = recv_src.reshape(N_LAT, N_LON, N_LON, CAP)
    band_cell = recv_cell.reshape(N_LAT, N_LON, N_LON, CAP)
    band_weight = recv_weight.reshape(N_LAT, N_LON, N_LON, CAP)
    lon_ids = jnp.arange(N_LON, dtype=jnp.int32)

    def band_regrid(members):
        cells_here, src_here, cell_here, weight_here = members
        global_rows = (lon_ids[None, :, None] * SRC_DEV + src_here).reshape(-1)
        target_rows = (lon_ids[:, None, None] * cells_dev + cell_here).reshape(-1)
        values = jnp.take(cells_here, global_rows, axis=1).astype(jnp.float32) * weight_here.reshape(-1)[None, :]
        return jnp.zeros((CIN, N_LON * cells_dev), jnp.float32).at[:, target_rows].add(values)
    regridded = lax.map(band_regrid, (band_cells, band_src, band_cell, band_weight))
    regridded = regridded.transpose(1, 0, 2).reshape(CIN, N_LAT * N_LON * cells_dev).astype(jnp.bfloat16)
    hidden = jnp.dot(enc_w1, regridded, preferred_element_type=jnp.float32) + enc_b1[:, None]
    hidden = jax.nn.gelu(hidden, approximate=False).astype(jnp.bfloat16)
    encoded = (jnp.dot(enc_w2, hidden, preferred_element_type=jnp.float32) + enc_b2[:, None]).astype(jnp.bfloat16)
    natural = encoded.reshape(E, N_LAT, N_LON, lat_dev, lon_dev).transpose(0, 1, 3, 2, 4).reshape(E * NLAT, NLON)
    dft_basis = build_basis(jnp.arange(ORDERS, dtype=jnp.int32))
    spectra = lax.dot_general(dft_basis, natural, (((1,), (1,)), ((), ())), preferred_element_type=jnp.float32)
    spectra = spectra.astype(jnp.bfloat16).reshape(ORDERS, 2 * E, NLAT)
    real_part = mix_weight[0]
    imag_part = mix_weight[1]
    mix_block = jnp.concatenate([jnp.concatenate([real_part, -imag_part], axis=1), jnp.concatenate([imag_part, real_part], axis=1)], axis=0)

    def per_order(members):
        spectrum, forward, inverse = members
        coeffs = jnp.dot(spectrum, forward.T, preferred_element_type=jnp.float32).astype(jnp.bfloat16)
        mixed = jnp.dot(mix_block, coeffs, preferred_element_type=jnp.float32).astype(jnp.bfloat16)
        return jnp.dot(mixed, inverse.T, preferred_element_type=jnp.float32).astype(jnp.bfloat16)
    synth_in = lax.map(per_order, (spectra, fwd_table, inv_table))
    spectral = lax.dot_general(synth_in.reshape(2 * ORDERS, E * NLAT), dft_basis, (((0,), (0,)), ((), ())), preferred_element_type=jnp.float32)
    spectral = spectral.astype(jnp.bfloat16).reshape(E, N_LAT, lat_dev, N_LON, lon_dev).transpose(0, 1, 3, 2, 4)
    spectral = spectral.reshape(E, N_LAT * N_LON * cells_dev)
    return (encoded.astype(jnp.float32) + spectral.astype(jnp.float32)).astype(jnp.bfloat16)
```

```python
import functools
import math

import jax
import jax.numpy as jnp
from jax import lax
from jax.experimental import pallas as pl
from jax.experimental.pallas import tpu as pltpu
from jax.sharding import PartitionSpec as P

NLON = 1440
ORDERS = 512
LANES = 128
TILE = 16
WINDOW = 48
VMEM_BYTES = 60 * 1024 * 1024

F32 = jnp.float32
BF16 = jnp.bfloat16


def build_basis(order_list, points_total):
    points = jnp.arange(points_total, dtype=jnp.int32)
    angles = (order_list[:, None] * points[None, :] % points_total).astype(jnp.float32) * (
        2.0 * math.pi / points_total
    )
    factor = math.sqrt(2.0 / points_total)
    stacked = jnp.stack([factor * jnp.cos(angles), -factor * jnp.sin(angles)], axis=1)
    return stacked.astype(jnp.bfloat16).reshape(2 * order_list.shape[0], points_total)


def basis_by_point(order_list, points):
    shape = points.shape + order_list.shape
    angles = (points[..., None] * order_list % NLON).astype(F32) * (2.0 * math.pi / NLON)
    factor = math.sqrt(2.0 / NLON)
    stacked = jnp.stack([factor * jnp.cos(angles), -factor * jnp.sin(angles)], axis=-1)
    return stacked.astype(BF16).reshape(shape[:-1] + (2 * shape[-1],))


def spread(running, values, weights, targets):
    channels = values.shape[-1]
    contrib = values.astype(jnp.float32) * weights[:, :, None]
    return running.at[targets.reshape(-1)].add(contrib.reshape(-1, channels))


def mixing_matrix(mix_weight):
    real_part = mix_weight[0]
    imag_part = mix_weight[1]
    return jnp.concatenate(
        [
            jnp.concatenate([real_part, -imag_part], axis=1),
            jnp.concatenate([imag_part, real_part], axis=1),
        ],
        axis=0,
    )


def dense_encoder(piece, sources, targets, weights, cells_dev, enc_w1, enc_b1, enc_w2, enc_b2):
    shard_count, slot_count = sources.shape
    channels = piece.shape[0]
    src_rows = piece.shape[1] // shard_count
    piece_rows = piece.T
    offsets = jnp.arange(shard_count, dtype=jnp.int32)[:, None] * src_rows
    picked = jnp.take(piece_rows, (offsets + sources).reshape(-1), axis=0)
    picked = picked.reshape(shard_count, slot_count, channels)
    empty = jnp.zeros((cells_dev, channels), jnp.float32)
    regridded = spread(empty, picked, weights, targets).T.astype(jnp.bfloat16)
    hidden = jnp.dot(enc_w1, regridded, preferred_element_type=jnp.float32) + enc_b1[:, None]
    hidden = jax.nn.gelu(hidden, approximate=False).astype(jnp.bfloat16)
    return (
        jnp.dot(enc_w2, hidden, preferred_element_type=jnp.float32) + enc_b2[:, None]
    ).astype(jnp.bfloat16)


def regrid_kernel(src_ref, cols_ref, row_ref, out_ref, contrib, *, channels, shards, slots, src_rows):
    step = pl.program_id(0)
    rows = out_ref.shape[0]

    @pl.when(step == 0)
    def _():
        contrib[...] = jnp.zeros_like(contrib)
        lane = lax.broadcasted_iota(jnp.int32, (slots, src_rows), 1).astype(F32)

        def one(j, carry):
            at = pl.ds(pl.multiple_of(j * slots, slots), slots)
            index = cols_ref[at, 0:1]
            weight = cols_ref[at, 1:2]
            hot = (index == lane).astype(BF16)
            picked = lax.dot_general(
                hot, src_ref[j], (((1,), (1,)), ((), ())), preferred_element_type=F32
            )
            value = picked * weight
            upper = value.astype(BF16)
            lower = (value - upper.astype(F32)).astype(BF16)
            contrib[at, 0:channels] = upper
            contrib[at, LANES : LANES + channels] = lower
            return carry

        lax.fori_loop(0, shards, one, 0)

    here = pl.ds(pl.multiple_of(step * rows, rows), rows)
    cell = cols_ref[here, 2:3]
    total = jnp.zeros((rows, 2 * LANES), F32)
    for s in range(shards):
        same = (cell == row_ref[:, s * slots : (s + 1) * slots]).astype(BF16)
        total += jnp.dot(same, contrib[s * slots : (s + 1) * slots, :], preferred_element_type=F32)
    merged = total[:, :LANES] + total[:, LANES:]
    lane = lax.broadcasted_iota(jnp.int32, (rows, LANES), 1)
    for place in range(4):
        merged = jnp.where(lane == channels + place, cols_ref[here, 3 + place : 4 + place], merged)
    out_ref[...] = merged.astype(BF16)


def regrid_listed(source_all, recv_src, recv_cell, recv_weight, lat_dev, lon_dev, slot_count):
    shards, channels, src_rows = source_all.shape
    total = recv_src.shape[0]
    ordered = jnp.sort(recv_cell)
    lead = jnp.concatenate([jnp.ones((1,), jnp.bool_), ordered[1:] != ordered[:-1]])
    bounds = jnp.arange(total, dtype=jnp.int32) * lon_dev
    limits = jnp.arange(lat_dev + 1, dtype=jnp.int32) * lon_dev
    starts = jnp.sum((recv_cell[None, :] < limits[:, None]).astype(jnp.int32), axis=1)
    starts = jnp.zeros((total,), jnp.int32).at[: lat_dev + 1].set(starts)
    del bounds
    cols = jnp.stack(
        [
            recv_src.astype(F32),
            recv_weight,
            ordered.astype(F32),
            (ordered % lon_dev).astype(F32),
            lead.astype(F32),
            (starts // 128).astype(F32),
            (starts % 128).astype(F32),
            jnp.zeros((total,), F32),
        ],
        axis=1,
    )
    rows = min(512, total)
    return pl.pallas_call(
        functools.partial(
            regrid_kernel, channels=channels, shards=shards, slots=slot_count, src_rows=src_rows
        ),
        grid=(total // rows,),
        out_shape=jax.ShapeDtypeStruct((total, LANES), BF16),
        in_specs=[
            pl.BlockSpec((shards, channels, src_rows), lambda i: (0, 0, 0)),
            pl.BlockSpec((total, 8), lambda i: (0, 0)),
            pl.BlockSpec((1, total), lambda i: (0, 0)),
        ],
        out_specs=pl.BlockSpec((rows, LANES), lambda i: (i, 0)),
        scratch_shapes=[pltpu.VMEM((total, 2 * LANES), BF16)],
        compiler_params=pltpu.CompilerParams(vmem_limit_bytes=VMEM_BYTES),
    )(source_all, cols, recv_cell.astype(F32)[None, :])


def zonal_kernel(
    starts,
    rows_ref,
    w1_ref,
    b1_ref,
    w2_ref,
    b2_ref,
    basis_ref,
    sums_ref,
    out_ref,
    delta,
    hots,
    base,
    *,
    channels,
    blocks,
    block_rows,
):
    step = pl.program_id(0)
    total = blocks * block_rows
    groups, lats, height, width = out_ref.shape
    columns = groups * height
    chunk = min(512, block_rows)

    def encode(values):
        hidden = jnp.dot(values, w1_ref[...], preferred_element_type=F32) + b1_ref[...]
        hidden = 0.5 * hidden * (1.0 + lax.erf(hidden * math.sqrt(0.5)))
        encoded = jnp.dot(hidden.astype(BF16), w2_ref[...], preferred_element_type=F32)
        return (encoded + b2_ref[...]).astype(BF16).astype(F32)

    @pl.when(step == 0)
    def _():
        empty = encode(jnp.zeros((16, LANES), BF16))[0:1]
        base[...] = sums_ref[...] * empty
        delta[pl.ds(total, WINDOW), :] = jnp.zeros((WINDOW, width), BF16)
        hots[pl.ds(total, WINDOW), :] = jnp.zeros((WINDOW, columns), BF16)
        points = basis_ref.shape[1]
        lane = lax.broadcasted_iota(jnp.int32, (chunk, points), 1).astype(F32)

        def one(j, carry):
            at = pl.ds(pl.multiple_of(j * chunk, chunk), chunk)
            values = rows_ref[at, :]
            delta[at, :] = (encode(values) - empty).astype(BF16)
            point = values[:, channels : channels + 1].astype(F32)
            lead = values[:, channels + 1 : channels + 2].astype(F32)
            point = jnp.where(lead > 0.5, point, -1.0)
            hot = (point == lane).astype(BF16)
            block = basis_ref[j // (block_rows // chunk)]
            hots[at, :] = jnp.dot(hot, block, preferred_element_type=F32).astype(BF16)
            return carry

        lax.fori_loop(0, total // chunk, one, 0)

    place = lax.broadcasted_iota(jnp.int32, (WINDOW, columns), 0)

    def latitude(tt, carry):
        t = step * lats + tt
        lows, highs, firsts = [], [], []
        most = jnp.int32(1)
        for k in range(blocks):
            low = starts[k, t] + k * block_rows
            high = starts[k, t + 1] + k * block_rows
            first = (low // TILE) * TILE
            most = jnp.maximum(most, (high - first + WINDOW - 1) // WINDOW)
            lows.append(low)
            highs.append(high)
            firsts.append(first)

        def window(j, running):
            left, right = [], []
            for k in range(blocks):
                first = jnp.minimum(firsts[k] + j * WINDOW, total)
                first = pl.multiple_of(first, TILE)
                at = pl.ds(first, WINDOW)
                inside = (place >= lows[k] - first) & (place < highs[k] - first)
                left.append(jnp.where(inside, hots[at, :].astype(F32), 0.0).astype(BF16))
                right.append(delta[at, :])
            return running + lax.dot_general(
                jnp.concatenate(left, axis=0),
                jnp.concatenate(right, axis=0),
                (((0,), (0,)), ((), ())),
                preferred_element_type=F32,
            )

        result = window(0, base[...])
        result = lax.fori_loop(1, most, window, result).astype(BF16)
        for g in range(groups):
            out_ref[g, tt] = result[g * height : (g + 1) * height, :]
        return carry

    lax.fori_loop(0, lats, latitude, 0)


def zonal_transform(
    rows, starts, w1, b1, w2, b2, basis, sums, lat_dev, groups, channels, lats=15
):
    blocks, block_rows, _ = rows.shape
    width = w2.shape[1]
    columns = basis.shape[2]
    height = columns // groups
    total = blocks * block_rows
    whole = lambda shape: pl.BlockSpec(
        shape, lambda i, s: (0,) * len(shape), pipeline_mode=pl.Buffered(1)
    )
    return pl.pallas_call(
        functools.partial(
            zonal_kernel, channels=channels, blocks=blocks, block_rows=block_rows
        ),
        grid_spec=pltpu.PrefetchScalarGridSpec(
            num_scalar_prefetch=1,
            grid=(lat_dev // lats,),
            in_specs=[
                whole((total, LANES)),
                whole(w1.shape),
                whole(b1.shape),
                whole(w2.shape),
                whole(b2.shape),
                whole(basis.shape),
                whole(sums.shape),
            ],
            out_specs=pl.BlockSpec((groups, lats, height, width), lambda i, s: (0, i, 0, 0)),
            scratch_shapes=[
                pltpu.VMEM((total + WINDOW, width), BF16),
                pltpu.VMEM((total + WINDOW, columns), BF16),
                pltpu.VMEM((columns, width), F32),
            ],
        ),
        out_shape=jax.ShapeDtypeStruct((groups, lat_dev, height, width), BF16),
        compiler_params=pltpu.CompilerParams(vmem_limit_bytes=VMEM_BYTES),
    )(starts, rows.reshape(total, LANES), w1, b1, w2, b2, basis, sums)


def orders_kernel(spec_ref, fwd_ref, inv_ref, mix_ref, swap_ref, out_ref, taken, made, *, group):
    order = lax.rem(pl.program_id(0), group)
    lat_total, _, width = spec_ref.shape
    parts, halves, part_lats, _, lanes = out_ref.shape
    side = 2 * group

    @pl.when(order == 0)
    def _():
        def one(j, carry):
            at = pl.ds(pl.multiple_of(j * side, side), side)
            block = spec_ref[at].reshape(side * side, width)
            turned = jnp.dot(swap_ref[...], block, preferred_element_type=F32).astype(BF16)
            taken[:, at, :] = turned.reshape(side, side, width)
            return carry

        lax.fori_loop(0, lat_total // side, one, 0)

    spectrum = jnp.concatenate([taken[2 * order], taken[2 * order + 1]], axis=1)
    coeffs = jnp.dot(fwd_ref[0], spectrum, preferred_element_type=F32).astype(BF16)
    mixed = jnp.dot(coeffs, mix_ref[...], preferred_element_type=F32).astype(BF16)
    made[order] = jnp.dot(inv_ref[0], mixed, preferred_element_type=F32).astype(BF16)

    @pl.when(order == group - 1)
    def _():
        def one(j, carry):
            first = pl.multiple_of(j * side, side)
            at = pl.ds(first, side)
            columns = []
            for h in range(halves):
                pieces = []
                for r in range(group):
                    for c in range(2):
                        low = (c * halves + h) * lanes
                        pieces.append(made[r, at, low : low + lanes])
                columns.append(jnp.concatenate(pieces, axis=0))
            block = jnp.concatenate(columns, axis=1)
            turned = jnp.dot(swap_ref[...], block, preferred_element_type=F32).astype(BF16)
            for i in range(side):
                lat = first + i
                for h in range(halves):
                    out_ref[lat // part_lats, h, lat % part_lats] = turned[
                        i * side : (i + 1) * side, h * lanes : (h + 1) * lanes
                    ]
            return carry

        lax.fori_loop(0, lat_total // side, one, 0)


def order_steps(spectra, fwd_table, inv_table, mix_t, parts, halves):
    lat_total, height, width = spectra.shape
    ord_dev, degrees, _ = fwd_table.shape
    group = 8
    side = 2 * group
    index = jnp.arange(side * side, dtype=jnp.int32)
    swapped = (index % side) * side + index // side
    swap = (swapped[:, None] == index[None, :]).astype(BF16)
    both = 2 * width
    part_lats = lat_total // parts
    return pl.pallas_call(
        functools.partial(orders_kernel, group=group),
        grid=(ord_dev,),
        in_specs=[
            pl.BlockSpec((lat_total, side, width), lambda r: (0, r // group, 0)),
            pl.BlockSpec((1, degrees, lat_total), lambda r: (r, 0, 0)),
            pl.BlockSpec((1, lat_total, degrees), lambda r: (r, 0, 0)),
            pl.BlockSpec((both, both), lambda r: (0, 0)),
            pl.BlockSpec((side * side, side * side), lambda r: (0, 0)),
        ],
        out_specs=pl.BlockSpec(
            (parts, halves, part_lats, side, width // halves),
            lambda r: (0, 0, 0, r // group, 0),
        ),
        out_shape=jax.ShapeDtypeStruct(
            (parts, halves, part_lats, height, width // halves), BF16
        ),
        scratch_shapes=[
            pltpu.VMEM((side, lat_total, width), BF16),
            pltpu.VMEM((group, lat_total, both), BF16),
        ],
        compiler_params=pltpu.CompilerParams(vmem_limit_bytes=VMEM_BYTES),
    )(spectra, fwd_table, inv_table, mix_t, swap)


def synthesis_kernel(modes_ref, basis_ref, out_ref):
    sources, lats, height, lanes = modes_ref.shape
    blocks, _, points, _ = out_ref.shape
    right = jnp.concatenate(
        [modes_ref[:, t].reshape(sources * height, lanes) for t in range(lats)], axis=1
    )

    def one(k, carry):
        value = jnp.dot(basis_ref[k], right, preferred_element_type=F32).astype(BF16)
        for t in range(lats):
            out_ref[k, t] = value[:points, t * lanes : (t + 1) * lanes]
        return carry

    lax.fori_loop(0, blocks, one, 0)


def synthesis_steps(modes, basis, points, lats):
    sources, lat_part, height, lanes = modes.shape
    blocks = basis.shape[0]
    return pl.pallas_call(
        synthesis_kernel,
        grid=(lat_part // lats,),
        in_specs=[
            pl.BlockSpec((sources, lats, height, lanes), lambda i: (0, i, 0, 0)),
            pl.BlockSpec(basis.shape, lambda i: (0, 0, 0)),
        ],
        out_specs=pl.BlockSpec((blocks, lats, points, lanes), lambda i: (0, i, 0, 0)),
        out_shape=jax.ShapeDtypeStruct((blocks, lat_part, points, lanes), BF16),
        compiler_params=pltpu.CompilerParams(vmem_limit_bytes=VMEM_BYTES),
    )(modes, basis)


def listed_plan(
    source_cells,
    recv_src,
    recv_cell,
    recv_weight,
    enc_w1,
    enc_b1,
    enc_w2,
    enc_b2,
    mix_weight,
    fwd_table,
    inv_table,
):
    lon_count = lax.axis_size("lon")
    lat_count = lax.axis_size("lat")
    channels = source_cells.shape[0]
    slot_count = recv_src.shape[0] // lon_count
    lat_total = fwd_table.shape[2]
    lat_dev = lat_total // lat_count
    lon_dev = NLON // lon_count
    cells_dev = lat_dev * lon_dev
    width = enc_w1.shape[0]
    ord_dev = fwd_table.shape[0]
    halves = width // LANES
    quarters = lon_count // halves
    part_lats = lat_dev // quarters

    source_all = lax.all_gather(source_cells, "lon", axis=0, tiled=False)
    listed = regrid_listed(
        source_all, recv_src, recv_cell, recv_weight, lat_dev, lon_dev, slot_count
    )
    band = lax.all_gather(listed, "lon", axis=0, tiled=False)
    coded = band[:, : lat_dev + 1, channels + 2 : channels + 4].astype(jnp.int32)
    starts = coded[:, :, 0] * 128 + coded[:, :, 1]

    mine = lax.axis_index("lon")
    owned = (
        (jnp.arange(lat_count, dtype=jnp.int32)[:, None] * lon_count + mine) * ord_dev
        + jnp.arange(ord_dev, dtype=jnp.int32)[None, :]
    ).reshape(-1)
    point_rows = -(-lon_dev // LANES) * LANES
    at = jnp.arange(lon_count, dtype=jnp.int32)[:, None] * lon_dev + jnp.arange(
        point_rows, dtype=jnp.int32
    )
    inside = (jnp.arange(point_rows) < lon_dev)[None, :, None]
    basis_in = jnp.where(inside, basis_by_point(owned, at), 0)
    sums = jnp.sum(basis_in.astype(F32), axis=(0, 1))[:, None]
    w1 = jnp.zeros((LANES, width), BF16).at[:channels].set(enc_w1.T)
    spectra = zonal_transform(
        band,
        starts,
        w1,
        enc_b1[None, :],
        enc_w2.T,
        enc_b2[None, :],
        basis_in,
        sums,
        lat_dev,
        lat_count,
        channels,
    )
    spectra = lax.all_to_all(spectra, "lat", split_axis=0, concat_axis=0, tiled=True)
    spectra = spectra.reshape(lat_total, 2 * ord_dev, width)
    made = order_steps(
        spectra,
        fwd_table,
        inv_table,
        mixing_matrix(mix_weight).T,
        lat_count * quarters,
        halves,
    )
    made = made.reshape(lat_count * lon_count, part_lats, 2 * ord_dev, LANES)
    modes = lax.all_to_all(made, ("lat", "lon"), split_axis=0, concat_axis=0, tiled=True)

    pad_points = -(-lon_dev // TILE) * TILE
    at = jnp.arange(lon_count, dtype=jnp.int32)[:, None] * lon_dev + jnp.arange(
        pad_points, dtype=jnp.int32
    )
    inside = (jnp.arange(pad_points) < lon_dev)[None, :, None]
    basis_out = basis_by_point(jnp.arange(ORDERS, dtype=jnp.int32), at)
    basis_out = jnp.where(inside, basis_out, 0)
    grid_part = synthesis_steps(modes, basis_out, lon_dev, 9)
    grid_part = lax.all_to_all(grid_part, "lon", split_axis=0, concat_axis=0, tiled=True)
    spectral = (
        grid_part.reshape(quarters, halves, part_lats, lon_dev, LANES)
        .transpose(1, 4, 0, 2, 3)
        .reshape(width, cells_dev)
    )
    piece = source_all.transpose(1, 0, 2).reshape(channels, -1)
    encoded = dense_encoder(
        piece,
        recv_src.reshape(lon_count, slot_count),
        recv_cell.reshape(lon_count, slot_count),
        recv_weight.reshape(lon_count, slot_count),
        cells_dev,
        enc_w1,
        enc_b1,
        enc_w2,
        enc_b2,
    )
    return (encoded.astype(F32) + spectral.astype(F32)).astype(BF16)


def dense_plan(
    source_cells,
    recv_src,
    recv_cell,
    recv_weight,
    enc_w1,
    enc_b1,
    enc_w2,
    enc_b2,
    mix_weight,
    fwd_table,
    inv_table,
):
    lon_count = lax.axis_size("lon")
    lat_count = lax.axis_size("lat")
    slot_count = recv_src.shape[0] // lon_count
    sources = recv_src.reshape(lon_count, slot_count)
    targets = recv_cell.reshape(lon_count, slot_count)
    weights = recv_weight.reshape(lon_count, slot_count)
    lat_total = fwd_table.shape[2]
    lat_dev = lat_total // lat_count
    lon_dev = NLON // lon_count
    cells_dev = lat_dev * lon_dev
    width = enc_w1.shape[0]
    ch_dev = width // lon_count
    orders_total = ORDERS
    ord_dev = fwd_table.shape[0]
    piece = lax.all_gather(source_cells, "lon", axis=1, tiled=True)
    encoded = dense_encoder(
        piece, sources, targets, weights, cells_dev, enc_w1, enc_b1, enc_w2, enc_b2
    )
    blocked = encoded.reshape(width, lat_dev, 1, lon_dev)
    circles = lax.all_to_all(blocked, "lon", split_axis=0, concat_axis=2, tiled=True).reshape(
        ch_dev * lat_dev, NLON
    )
    natural_order = jnp.arange(orders_total, dtype=jnp.int32)
    dft_basis = build_basis(natural_order, NLON)
    spectra = lax.dot_general(
        dft_basis, circles, (((1,), (1,)), ((), ())), preferred_element_type=jnp.float32
    )
    spectra = spectra.astype(jnp.bfloat16).reshape(orders_total, 2, ch_dev, lat_dev)
    by_order = lax.all_to_all(
        lax.all_to_all(spectra, "lat", split_axis=0, concat_axis=3, tiled=True),
        "lon",
        split_axis=0,
        concat_axis=2,
        tiled=True,
    )
    by_order = by_order.reshape(ord_dev, 2 * width, lat_total)
    coeffs = jnp.einsum(
        "mrt,mlt->mrl", by_order, fwd_table, preferred_element_type=jnp.float32
    ).astype(jnp.bfloat16)
    mix_block = mixing_matrix(mix_weight)
    mixed = jnp.einsum("gr,mrl->mgl", mix_block, coeffs, preferred_element_type=jnp.float32).astype(
        jnp.bfloat16
    )
    synth_in = jnp.einsum(
        "mrl,mtl->mrt", mixed, inv_table, preferred_element_type=jnp.float32
    ).astype(jnp.bfloat16)
    synth_in = synth_in.reshape(ord_dev, 2, width, lat_total)
    returned_modes = lax.all_to_all(
        lax.all_to_all(synth_in, "lon", split_axis=2, concat_axis=0, tiled=True),
        "lat",
        split_axis=3,
        concat_axis=0,
        tiled=True,
    )
    returned_modes = returned_modes.reshape(2 * orders_total, ch_dev * lat_dev)
    synthesis = lax.dot_general(
        returned_modes, dft_basis, (((0,), (0,)), ((), ())), preferred_element_type=jnp.float32
    )
    synthesis = synthesis.astype(jnp.bfloat16).reshape(ch_dev, lat_dev, lon_count, lon_dev)
    regained = lax.all_to_all(synthesis, "lon", split_axis=2, concat_axis=0, tiled=True).reshape(
        width, cells_dev
    )
    return (encoded.astype(jnp.float32) + regained.astype(jnp.float32)).astype(jnp.bfloat16)


def solution(mesh):
    in_specs = (
        P(None, ("lat", "lon")),
        P(("lat", "lon")),
        P(("lat", "lon")),
        P(("lat", "lon")),
        P(),
        P(),
        P(),
        P(),
        P(),
        P(("lat", "lon"), None, None),
        P(("lat", "lon"), None, None),
    )
    out_specs = P(None, ("lat", "lon"))
    lon_count = mesh.shape["lon"]
    lat_count = mesh.shape["lat"]

    def on_device(*arrays):
        slots = arrays[1].shape[0]
        width = arrays[4].shape[0]
        ord_dev, _, lat_total = arrays[9].shape
        lat_dev = lat_total // lat_count
        cells_dev = lat_dev * (NLON // lon_count)
        halves = max(1, width // LANES)
        fits = (
            slots * 4 <= cells_dev
            and width % LANES == 0
            and lon_count % halves == 0
            and lat_dev % (9 * lon_count // halves) == 0
            and ord_dev % 8 == 0
            and lat_total % TILE == 0
        )
        return listed_plan(*arrays) if fits else dense_plan(*arrays)

    return jax.shard_map(
        on_device, mesh=mesh, in_specs=in_specs, out_specs=out_specs, check_vma=False
    )
```

```python
import functools
import math

import jax
import jax.numpy as jnp
import numpy as np
from jax import lax
from jax.experimental import pallas as pl
from jax.experimental.pallas import tpu as pltpu
from jax.sharding import PartitionSpec as P

NLON = 1440
ORDERS = 512
LANES = 128
TILE = 16
WINDOW = 48
LATS = 8
CHUNK_RUNS = 2
ORDER_GROUP = 8
VMEM_BYTES = 60 * 1024 * 1024

F32 = jnp.float32
BF16 = jnp.bfloat16


def work(flops, bytes_moved):
    return pl.CostEstimate(flops=flops, bytes_accessed=bytes_moved, transcendentals=0)


def build_basis(order_list, points_total):
    points = jnp.arange(points_total, dtype=jnp.int32)
    angles = (order_list[:, None] * points[None, :] % points_total).astype(jnp.float32) * (
        2.0 * math.pi / points_total
    )
    factor = math.sqrt(2.0 / points_total)
    stacked = jnp.stack([factor * jnp.cos(angles), -factor * jnp.sin(angles)], axis=1)
    return stacked.astype(jnp.bfloat16).reshape(2 * order_list.shape[0], points_total)


def basis_by_point(order_list, points):
    shape = points.shape + order_list.shape
    angles = (points[..., None] * order_list % NLON).astype(F32) * (2.0 * math.pi / NLON)
    factor = math.sqrt(2.0 / NLON)
    stacked = jnp.stack([factor * jnp.cos(angles), -factor * jnp.sin(angles)], axis=-1)
    return stacked.astype(BF16).reshape(shape[:-1] + (2 * shape[-1],))


def spread(running, values, weights, targets):
    channels = values.shape[-1]
    contrib = values.astype(jnp.float32) * weights[:, :, None]
    return running.at[targets.reshape(-1)].add(contrib.reshape(-1, channels))


def mixing_matrix(mix_weight):
    real_part = mix_weight[0]
    imag_part = mix_weight[1]
    return jnp.concatenate(
        [
            jnp.concatenate([real_part, -imag_part], axis=1),
            jnp.concatenate([imag_part, real_part], axis=1),
        ],
        axis=0,
    )


def dense_encoder(piece, sources, targets, weights, cells_dev, enc_w1, enc_b1, enc_w2, enc_b2):
    shard_count, slot_count = sources.shape
    channels = piece.shape[0]
    src_rows = piece.shape[1] // shard_count
    piece_rows = piece.T
    offsets = jnp.arange(shard_count, dtype=jnp.int32)[:, None] * src_rows
    picked = jnp.take(piece_rows, (offsets + sources).reshape(-1), axis=0)
    picked = picked.reshape(shard_count, slot_count, channels)
    empty = jnp.zeros((cells_dev, channels), jnp.float32)
    regridded = spread(empty, picked, weights, targets).T.astype(jnp.bfloat16)
    hidden = jnp.dot(enc_w1, regridded, preferred_element_type=jnp.float32) + enc_b1[:, None]
    hidden = jax.nn.gelu(hidden, approximate=False).astype(jnp.bfloat16)
    return (
        jnp.dot(enc_w2, hidden, preferred_element_type=jnp.float32) + enc_b2[:, None]
    ).astype(jnp.bfloat16)


def regrid_kernel(src_ref, cols_ref, row_ref, out_ref, contrib, *, channels, shards, slots, src_rows):
    step = pl.program_id(0)
    height, rows = out_ref.shape

    @pl.when(step == 0)
    def _():
        contrib[...] = jnp.zeros_like(contrib)
        lane = lax.broadcasted_iota(jnp.int32, (slots, src_rows), 1).astype(F32)

        def one(j, carry):
            at = pl.ds(pl.multiple_of(j * slots, slots), slots)
            index = cols_ref[at, 0:1]
            weight = cols_ref[at, 1:2]
            hot = (index == lane).astype(BF16)
            picked = lax.dot_general(
                hot, src_ref[j], (((1,), (1,)), ((), ())), preferred_element_type=F32
            )
            value = picked * weight
            upper = value.astype(BF16)
            lower = (value - upper.astype(F32)).astype(BF16)
            contrib[at, 0:channels] = upper
            contrib[at, LANES : LANES + channels] = lower
            return carry

        lax.fori_loop(0, shards, one, 0)

    here = pl.ds(pl.multiple_of(step * rows, rows), rows)
    cell = cols_ref[here, 2:3]
    total = jnp.zeros((rows, 2 * LANES), F32)
    for s in range(shards):
        same = (cell == row_ref[:, s * slots : (s + 1) * slots]).astype(BF16)
        total += jnp.dot(same, contrib[s * slots : (s + 1) * slots, :], preferred_element_type=F32)
    merged = total[:, :LANES] + total[:, LANES:]
    lane = lax.broadcasted_iota(jnp.int32, (rows, LANES), 1)
    for place in range(4):
        merged = jnp.where(lane == channels + place, cols_ref[here, 3 + place : 4 + place], merged)
    out_ref[...] = merged.T[:height].astype(BF16)


def regrid_listed(source_all, recv_src, recv_cell, recv_weight, lat_dev, lon_dev, slot_count):
    shards, channels, src_rows = source_all.shape
    total = recv_src.shape[0]
    ordered = jnp.sort(recv_cell)
    lead = jnp.concatenate([jnp.ones((1,), jnp.bool_), ordered[1:] != ordered[:-1]])
    limits = jnp.arange(lat_dev + 1, dtype=jnp.int32) * lon_dev
    starts = jnp.sum((recv_cell[None, :] < limits[:, None]).astype(jnp.int32), axis=1)
    starts = jnp.zeros((total,), jnp.int32).at[: lat_dev + 1].set(starts)
    cols = jnp.stack(
        [
            recv_src.astype(F32),
            recv_weight,
            ordered.astype(F32),
            (ordered % lon_dev).astype(F32),
            lead.astype(F32),
            (starts // 128).astype(F32),
            (starts % 128).astype(F32),
            jnp.zeros((total,), F32),
        ],
        axis=1,
    )
    rows = min(512, total)
    height = -(-(channels + 4) // TILE) * TILE
    return pl.pallas_call(
        functools.partial(
            regrid_kernel, channels=channels, shards=shards, slots=slot_count, src_rows=src_rows
        ),
        grid=(total // rows,),
        out_shape=jax.ShapeDtypeStruct((height, total), BF16),
        in_specs=[
            pl.BlockSpec((shards, channels, src_rows), lambda i: (0, 0, 0)),
            pl.BlockSpec((total, 8), lambda i: (0, 0)),
            pl.BlockSpec((1, total), lambda i: (0, 0)),
        ],
        out_specs=pl.BlockSpec((height, rows), lambda i: (0, i)),
        scratch_shapes=[pltpu.VMEM((total, 2 * LANES), BF16)],
        compiler_params=pltpu.CompilerParams(vmem_limit_bytes=VMEM_BYTES),
        cost_estimate=work(4 * total * total * LANES, 2 * total * LANES),
    )(source_all, cols, recv_cell.astype(F32)[None, :])


def zonal_kernel(
    starts,
    rows_ref,
    w1_ref,
    b1_ref,
    w2_ref,
    b2_ref,
    basis_ref,
    sums_ref,
    *rest,
    channels,
    blocks,
    block_rows,
):
    *out_refs, delta, hots, base = rest
    step = pl.program_id(0)
    total = blocks * block_rows
    groups, lats, height, width = out_refs[0].shape
    columns = groups * height * len(out_refs)
    chunk = min(512, block_rows)

    def encode(values):
        hidden = jnp.dot(values, w1_ref[...], preferred_element_type=F32) + b1_ref[...]
        hidden = 0.5 * hidden * (1.0 + lax.erf(hidden * math.sqrt(0.5)))
        encoded = jnp.dot(hidden.astype(BF16), w2_ref[...], preferred_element_type=F32)
        return (encoded + b2_ref[...]).astype(BF16).astype(F32)

    @pl.when(step == 0)
    def _():
        empty = encode(jnp.zeros((TILE, rows_ref.shape[1]), BF16))[0:1]
        base[...] = sums_ref[...] * empty
        delta[pl.ds(total, WINDOW), :] = jnp.zeros((WINDOW, width), BF16)
        hots[pl.ds(total, WINDOW), :] = jnp.zeros((WINDOW, columns), BF16)
        points = basis_ref.shape[1]
        lane = lax.broadcasted_iota(jnp.int32, (chunk, points), 1).astype(F32)

        def one(j, carry):
            at = pl.ds(pl.multiple_of(j * chunk, chunk), chunk)
            per_block = block_rows // chunk
            part = pl.ds(pl.multiple_of((j % per_block) * chunk, chunk), chunk)
            values = rows_ref[j // per_block, :, part].astype(F32).T
            delta[at, :] = (encode(values.astype(BF16)) - empty).astype(BF16)
            point = values[:, channels : channels + 1]
            lead = values[:, channels + 1 : channels + 2]
            point = jnp.where(lead > 0.5, point, -1.0)
            hot = (point == lane).astype(BF16)
            block = basis_ref[j // per_block]
            hots[at, :] = jnp.dot(hot, block, preferred_element_type=F32).astype(BF16)
            return carry

        lax.fori_loop(0, total // chunk, one, 0)

    place = lax.broadcasted_iota(jnp.int32, (WINDOW, columns), 0)

    def latitude(tt, carry):
        t = step * lats + tt
        lows, highs, firsts = [], [], []
        most = jnp.int32(1)
        for k in range(blocks):
            low = starts[k, t] + k * block_rows
            high = starts[k, t + 1] + k * block_rows
            first = (low // TILE) * TILE
            most = jnp.maximum(most, (high - first + WINDOW - 1) // WINDOW)
            lows.append(low)
            highs.append(high)
            firsts.append(first)

        def window(j, running):
            left, right = [], []
            for k in range(blocks):
                first = jnp.minimum(firsts[k] + j * WINDOW, total)
                first = pl.multiple_of(first, TILE)
                at = pl.ds(first, WINDOW)
                inside = (place >= lows[k] - first) & (place < highs[k] - first)
                left.append(jnp.where(inside, hots[at, :].astype(F32), 0.0).astype(BF16))
                right.append(delta[at, :])
            return running + lax.dot_general(
                jnp.concatenate(left, axis=0),
                jnp.concatenate(right, axis=0),
                (((0,), (0,)), ((), ())),
                preferred_element_type=F32,
            )

        result = window(0, base[...])
        result = lax.fori_loop(1, most, window, result).astype(BF16)
        for g in range(groups):
            for h, out_ref in enumerate(out_refs):
                low = (g * len(out_refs) + h) * height
                out_ref[g, tt] = result[low : low + height, :]
        return carry

    lax.fori_loop(0, lats, latitude, 0)


def zonal_transform(
    rows, starts, w1, b1, w2, b2, basis, sums, lat_dev, groups, sets, channels, lats=15
):
    blocks, depth, block_rows = rows.shape
    width = w2.shape[1]
    columns = basis.shape[2]
    height = columns // (groups * sets)
    total = blocks * block_rows
    whole = lambda shape: pl.BlockSpec(
        shape, lambda i, s: (0,) * len(shape), pipeline_mode=pl.Buffered(1)
    )
    return pl.pallas_call(
        functools.partial(
            zonal_kernel, channels=channels, blocks=blocks, block_rows=block_rows
        ),
        grid_spec=pltpu.PrefetchScalarGridSpec(
            num_scalar_prefetch=1,
            grid=(lat_dev // lats,),
            in_specs=[
                whole(rows.shape),
                whole(w1.shape),
                whole(b1.shape),
                whole(w2.shape),
                whole(b2.shape),
                whole(basis.shape),
                whole(sums.shape),
            ],
            out_specs=[pl.BlockSpec((groups, lats, height, width), lambda i, s: (0, i, 0, 0))]
            * sets,
            scratch_shapes=[
                pltpu.VMEM((total + WINDOW, width), BF16),
                pltpu.VMEM((total + WINDOW, columns), BF16),
                pltpu.VMEM((columns, width), F32),
            ],
        ),
        out_shape=[jax.ShapeDtypeStruct((groups, lat_dev, height, width), BF16)] * sets,
        compiler_params=pltpu.CompilerParams(vmem_limit_bytes=VMEM_BYTES),
        cost_estimate=work(50 * total * width * 2 * columns, 2 * total * width),
    )(starts, rows, w1, b1, w2, b2, basis, sums)


def orders_kernel(place, spec_ref, fwd_ref, inv_ref, mix_ref, swap_ref, out_ref, taken, made, *, group):
    order = pl.program_id(0)
    lat_total, _, width = spec_ref.shape
    parts, halves, part_lats, _, lanes = out_ref.shape
    side = 2 * group

    @pl.when(order == 0)
    def _():
        def one(j, carry):
            at = pl.ds(pl.multiple_of(j * side, side), side)
            block = spec_ref[at].reshape(side * side, width)
            turned = jnp.dot(swap_ref[...], block, preferred_element_type=F32).astype(BF16)
            taken[:, at, :] = turned.reshape(side, side, width)
            return carry

        lax.fori_loop(0, lat_total // side, one, 0)

    spectrum = jnp.concatenate([taken[2 * order], taken[2 * order + 1]], axis=1)
    coeffs = jnp.dot(fwd_ref[0], spectrum, preferred_element_type=F32).astype(BF16)
    mixed = jnp.dot(coeffs, mix_ref[...], preferred_element_type=F32).astype(BF16)
    made[order] = jnp.dot(inv_ref[0], mixed, preferred_element_type=F32).astype(BF16)

    @pl.when(order == group - 1)
    def _():
        def one(j, carry):
            first = pl.multiple_of(j * side, side)
            at = pl.ds(first, side)
            columns = []
            for h in range(halves):
                pieces = []
                for r in range(group):
                    for c in range(2):
                        low = (c * halves + h) * lanes
                        pieces.append(made[r, at, low : low + lanes])
                columns.append(jnp.concatenate(pieces, axis=0))
            block = jnp.concatenate(columns, axis=1)
            turned = jnp.dot(swap_ref[...], block, preferred_element_type=F32).astype(BF16)
            for i in range(side):
                spot = place[first + i]
                for h in range(halves):
                    out_ref[spot // 64, h, spot % 64] = turned[
                        i * side : (i + 1) * side, h * lanes : (h + 1) * lanes
                    ]
            return carry

        lax.fori_loop(0, lat_total // side, one, 0)


def order_steps(place, spectra, fwd_table, inv_table, mix_t, first, parts, halves):
    lat_total, side, width = spectra.shape
    degrees = fwd_table.shape[1]
    group = side // 2
    index = jnp.arange(side * side, dtype=jnp.int32)
    swapped = (index % side) * side + index // side
    swap = (swapped[:, None] == index[None, :]).astype(BF16)
    both = 2 * width
    part_lats = lat_total // parts
    out_shape = (parts, halves, part_lats, side, width // halves)
    return pl.pallas_call(
        functools.partial(orders_kernel, group=group),
        grid_spec=pltpu.PrefetchScalarGridSpec(
            num_scalar_prefetch=1,
            grid=(group,),
            in_specs=[
                pl.BlockSpec((lat_total, side, width), lambda r, s: (0, 0, 0)),
                pl.BlockSpec((1, degrees, lat_total), lambda r, s: (first + r, 0, 0)),
                pl.BlockSpec((1, lat_total, degrees), lambda r, s: (first + r, 0, 0)),
                pl.BlockSpec((both, both), lambda r, s: (0, 0)),
                pl.BlockSpec((side * side, side * side), lambda r, s: (0, 0)),
            ],
            out_specs=pl.BlockSpec(out_shape, lambda r, s: (0, 0, 0, 0, 0)),
            scratch_shapes=[
                pltpu.VMEM((side, lat_total, width), BF16),
                pltpu.VMEM((group, lat_total, both), BF16),
            ],
        ),
        out_shape=jax.ShapeDtypeStruct(out_shape, BF16),
        compiler_params=pltpu.CompilerParams(vmem_limit_bytes=VMEM_BYTES),
        cost_estimate=work(
            group * 2 * both * degrees * (2 * lat_total + both), 8 * group * degrees * lat_total
        ),
    )(place, spectra, fwd_table, inv_table, mix_t, swap)


def synthesis_kernel(*refs):
    *mode_refs, basis_ref, out_ref = refs
    sources, lats, height, lanes = mode_refs[0].shape
    blocks, _, points, _ = out_ref.shape
    right = jnp.concatenate(
        [
            jnp.concatenate(
                [ref[:, t].reshape(sources * height, lanes) for ref in mode_refs], axis=0
            )
            for t in range(lats)
        ],
        axis=1,
    )

    def one(k, carry):
        value = jnp.dot(basis_ref[k], right, preferred_element_type=F32).astype(BF16)
        for t in range(lats):
            out_ref[k, t] = value[:points, t * lanes : (t + 1) * lanes]
        return carry

    lax.fori_loop(0, blocks, one, 0)


def synthesis_steps(modes, basis, points, lats, first, count):
    sources, _, height, lanes = modes[0].shape
    blocks = basis.shape[0]
    offset = first // lats
    return pl.pallas_call(
        synthesis_kernel,
        grid=(-(-count // lats),),
        in_specs=[
            pl.BlockSpec((sources, lats, height, lanes), lambda i: (0, i + offset, 0, 0))
            for _ in modes
        ]
        + [pl.BlockSpec(basis.shape, lambda i: (0, 0, 0))],
        out_specs=pl.BlockSpec((blocks, lats, points, lanes), lambda i: (0, i, 0, 0)),
        out_shape=jax.ShapeDtypeStruct((blocks, count, points, lanes), BF16),
        compiler_params=pltpu.CompilerParams(vmem_limit_bytes=VMEM_BYTES),
        cost_estimate=work(2 * count * lanes * basis.size, 4 * blocks * count * points * lanes),
    )(*modes, basis)


def finish_kernel(part_ref, enc_ref, out_ref, flat, *, first, whole_groups, rest):
    quarters, _, lats, points, lanes = part_ref.shape
    group = pl.program_id(1) + first

    def fill(count):
        for q in range(quarters):
            for t in range(count):
                row = (q * count + t) * points
                flat[row : row + points, :] = part_ref[q, 0, t].astype(F32)

    @pl.when(group < whole_groups)
    def _():
        fill(lats)

    @pl.when(group >= whole_groups)
    def _():
        fill(rest)

    def one(j, carry):
        at = pl.ds(pl.multiple_of(j * lanes, lanes), lanes)
        out_ref[:, at] = (enc_ref[:, at].astype(F32) + flat[at, :].T).astype(BF16)
        return carry

    lax.fori_loop(0, out_ref.shape[1] // lanes, one, 0)


def finish_steps(part, running, lats, first, whole_groups, rest):
    quarters, halves, count, points, lanes = part.shape
    span = quarters * lats * points
    return pl.pallas_call(
        functools.partial(
            finish_kernel, first=first, whole_groups=whole_groups, rest=rest
        ),
        grid=(halves, -(-count // lats)),
        in_specs=[
            pl.BlockSpec((quarters, 1, lats, points, lanes), lambda h, i: (0, h, i, 0, 0)),
            pl.BlockSpec((lanes, span), lambda h, i: (h, i + first)),
        ],
        out_specs=pl.BlockSpec((lanes, span), lambda h, i: (h, i + first)),
        out_shape=jax.ShapeDtypeStruct(running.shape, BF16),
        scratch_shapes=[pltpu.VMEM((span, lanes), F32)],
        input_output_aliases={1: 0},
        compiler_params=pltpu.CompilerParams(vmem_limit_bytes=VMEM_BYTES),
        cost_estimate=work(part.size * 40, 6 * part.size),
    )(part, running)


def listed_plan(
    source_cells,
    recv_src,
    recv_cell,
    recv_weight,
    enc_w1,
    enc_b1,
    enc_w2,
    enc_b2,
    mix_weight,
    fwd_table,
    inv_table,
):
    lon_count = lax.axis_size("lon")
    lat_count = lax.axis_size("lat")
    channels = source_cells.shape[0]
    slot_count = recv_src.shape[0] // lon_count
    lat_total = fwd_table.shape[2]
    lat_dev = lat_total // lat_count
    lon_dev = NLON // lon_count
    cells_dev = lat_dev * lon_dev
    width = enc_w1.shape[0]
    ord_dev = fwd_table.shape[0]
    halves = width // LANES
    quarters = lon_count // halves
    part_lats = lat_dev // quarters

    source_all = lax.all_gather(source_cells, "lon", axis=0, tiled=False)
    listed = regrid_listed(
        source_all, recv_src, recv_cell, recv_weight, lat_dev, lon_dev, slot_count
    )
    band = lax.all_gather(listed, "lon", axis=0, tiled=False)
    coded = band[:, channels + 2 : channels + 4, : lat_dev + 1].astype(jnp.int32)
    starts = coded[:, 0] * 128 + coded[:, 1]

    mine = lax.axis_index("lon")
    owned = (
        (jnp.arange(lat_count, dtype=jnp.int32)[:, None] * lon_count + mine) * ord_dev
        + jnp.arange(ord_dev, dtype=jnp.int32)[None, :]
    ).reshape(-1)
    point_rows = -(-lon_dev // LANES) * LANES
    at = jnp.arange(lon_count, dtype=jnp.int32)[:, None] * lon_dev + jnp.arange(
        point_rows, dtype=jnp.int32
    )
    inside = (jnp.arange(point_rows) < lon_dev)[None, :, None]
    basis_in = jnp.where(inside, basis_by_point(owned, at), 0)
    sums = jnp.sum(basis_in.astype(F32), axis=(0, 1))[:, None]
    w1 = jnp.zeros((band.shape[1], width), BF16).at[:channels].set(enc_w1.T)
    sets = ord_dev // ORDER_GROUP
    spectra = zonal_transform(
        band,
        starts,
        w1,
        enc_b1[None, :],
        enc_w2.T,
        enc_b2[None, :],
        basis_in,
        sums,
        lat_dev,
        lat_count,
        sets,
        channels,
    )

    run = quarters * LATS
    whole_groups = lat_dev // run
    rest = (lat_dev - whole_groups * run) // quarters
    lat = np.arange(lat_dev)
    tail = lat - whole_groups * run
    to_part = np.where(tail < 0, lat % run // LATS, tail // max(rest, 1))
    to_row = np.where(tail < 0, lat // run * LATS + lat % LATS, whole_groups * LATS + tail % max(rest, 1))
    place = (np.arange(lat_count)[:, None] * quarters + to_part) * 64 + to_row
    place = jnp.asarray(place.reshape(-1), jnp.int32)

    mix_t = mixing_matrix(mix_weight).T
    modes = []
    for g in range(sets):
        got = lax.all_to_all(spectra[g], "lat", split_axis=0, concat_axis=0, tiled=True)
        made = order_steps(
            place,
            got.reshape(lat_total, 2 * ORDER_GROUP, width),
            fwd_table,
            inv_table,
            mix_t,
            g * ORDER_GROUP,
            lat_count * quarters,
            halves,
        )
        made = made.reshape(lat_count * lon_count, part_lats, 2 * ORDER_GROUP, LANES)
        modes.append(
            lax.all_to_all(made, ("lat", "lon"), split_axis=0, concat_axis=0, tiled=True)
        )

    pad_points = -(-lon_dev // TILE) * TILE
    at = jnp.arange(lon_count, dtype=jnp.int32)[:, None] * lon_dev + jnp.arange(
        pad_points, dtype=jnp.int32
    )
    inside = (jnp.arange(pad_points) < lon_dev)[None, :, None]
    listing = jnp.arange(ORDERS, dtype=jnp.int32).reshape(-1, sets, ORDER_GROUP)
    basis_out = basis_by_point(listing.transpose(1, 0, 2).reshape(-1), at)
    basis_out = jnp.where(inside, basis_out, 0)

    piece = source_all.transpose(1, 0, 2).reshape(channels, -1)
    encoded = dense_encoder(
        piece,
        recv_src.reshape(lon_count, slot_count),
        recv_cell.reshape(lon_count, slot_count),
        recv_weight.reshape(lon_count, slot_count),
        cells_dev,
        enc_w1,
        enc_b1,
        enc_w2,
        enc_b2,
    )
    running = encoded
    step = CHUNK_RUNS * LATS
    for first in range(0, part_lats, step):
        count = min(step, part_lats - first)
        part = synthesis_steps(modes, basis_out, lon_dev, LATS, first, count)
        part = lax.all_to_all(part, "lon", split_axis=0, concat_axis=0, tiled=True)
        part = part.reshape(quarters, halves, count, lon_dev, LANES)
        running = finish_steps(part, running, LATS, first // LATS, whole_groups, rest)
    return running


def dense_plan(
    source_cells,
    recv_src,
    recv_cell,
    recv_weight,
    enc_w1,
    enc_b1,
    enc_w2,
    enc_b2,
    mix_weight,
    fwd_table,
    inv_table,
):
    lon_count = lax.axis_size("lon")
    lat_count = lax.axis_size("lat")
    slot_count = recv_src.shape[0] // lon_count
    sources = recv_src.reshape(lon_count, slot_count)
    targets = recv_cell.reshape(lon_count, slot_count)
    weights = recv_weight.reshape(lon_count, slot_count)
    lat_total = fwd_table.shape[2]
    lat_dev = lat_total // lat_count
    lon_dev = NLON // lon_count
    cells_dev = lat_dev * lon_dev
    width = enc_w1.shape[0]
    ch_dev = width // lon_count
    orders_total = ORDERS
    ord_dev = fwd_table.shape[0]
    piece = lax.all_gather(source_cells, "lon", axis=1, tiled=True)
    encoded = dense_encoder(
        piece, sources, targets, weights, cells_dev, enc_w1, enc_b1, enc_w2, enc_b2
    )
    blocked = encoded.reshape(width, lat_dev, 1, lon_dev)
    circles = lax.all_to_all(blocked, "lon", split_axis=0, concat_axis=2, tiled=True).reshape(
        ch_dev * lat_dev, NLON
    )
    natural_order = jnp.arange(orders_total, dtype=jnp.int32)
    dft_basis = build_basis(natural_order, NLON)
    spectra = lax.dot_general(
        dft_basis, circles, (((1,), (1,)), ((), ())), preferred_element_type=jnp.float32
    )
    spectra = spectra.astype(jnp.bfloat16).reshape(orders_total, 2, ch_dev, lat_dev)
    by_order = lax.all_to_all(
        lax.all_to_all(spectra, "lat", split_axis=0, concat_axis=3, tiled=True),
        "lon",
        split_axis=0,
        concat_axis=2,
        tiled=True,
    )
    by_order = by_order.reshape(ord_dev, 2 * width, lat_total)
    coeffs = jnp.einsum(
        "mrt,mlt->mrl", by_order, fwd_table, preferred_element_type=jnp.float32
    ).astype(jnp.bfloat16)
    mix_block = mixing_matrix(mix_weight)
    mixed = jnp.einsum("gr,mrl->mgl", mix_block, coeffs, preferred_element_type=jnp.float32).astype(
        jnp.bfloat16
    )
    synth_in = jnp.einsum(
        "mrl,mtl->mrt", mixed, inv_table, preferred_element_type=jnp.float32
    ).astype(jnp.bfloat16)
    synth_in = synth_in.reshape(ord_dev, 2, width, lat_total)
    returned_modes = lax.all_to_all(
        lax.all_to_all(synth_in, "lon", split_axis=2, concat_axis=0, tiled=True),
        "lat",
        split_axis=3,
        concat_axis=0,
        tiled=True,
    )
    returned_modes = returned_modes.reshape(2 * orders_total, ch_dev * lat_dev)
    synthesis = lax.dot_general(
        returned_modes, dft_basis, (((0,), (0,)), ((), ())), preferred_element_type=jnp.float32
    )
    synthesis = synthesis.astype(jnp.bfloat16).reshape(ch_dev, lat_dev, lon_count, lon_dev)
    regained = lax.all_to_all(synthesis, "lon", split_axis=2, concat_axis=0, tiled=True).reshape(
        width, cells_dev
    )
    return (encoded.astype(jnp.float32) + regained.astype(jnp.float32)).astype(jnp.bfloat16)


def solution(mesh):
    in_specs = (
        P(None, ("lat", "lon")),
        P(("lat", "lon")),
        P(("lat", "lon")),
        P(("lat", "lon")),
        P(),
        P(),
        P(),
        P(),
        P(),
        P(("lat", "lon"), None, None),
        P(("lat", "lon"), None, None),
    )
    out_specs = P(None, ("lat", "lon"))
    lon_count = mesh.shape["lon"]
    lat_count = mesh.shape["lat"]

    def on_device(*arrays):
        slots = arrays[1].shape[0]
        width = arrays[4].shape[0]
        ord_dev, _, lat_total = arrays[9].shape
        lat_dev = lat_total // lat_count
        cells_dev = lat_dev * (NLON // lon_count)
        halves = max(1, width // LANES)
        fits = (
            slots * 4 <= cells_dev
            and width % LANES == 0
            and lon_count % halves == 0
            and lat_dev % (lon_count // halves) == 0
            and lat_dev % 15 == 0
            and (lon_count // halves) * LATS * (NLON // lon_count) % LANES == 0
            and lat_dev // (lon_count // halves) < 64
            and ord_dev % ORDER_GROUP == 0
            and lat_total % TILE == 0
        )
        return listed_plan(*arrays) if fits else dense_plan(*arrays)

    return jax.shard_map(
        on_device, mesh=mesh, in_specs=in_specs, out_specs=out_specs, check_vma=False
    )
```

```python
import functools
import math

import jax
import jax.numpy as jnp
import numpy as np
from jax import lax
from jax.experimental import pallas as pl
from jax.experimental.pallas import tpu as pltpu
from jax.sharding import PartitionSpec as P

NLON = 1440
ORDERS = 512
LANES = 128
TILE = 16
WINDOW = 32
LATS = 8
CHUNK_RUNS = 2
ORDER_GROUP = 8
VMEM_BYTES = 60 * 1024 * 1024

F32 = jnp.float32
BF16 = jnp.bfloat16


def work(flops, bytes_moved):
    return pl.CostEstimate(flops=flops, bytes_accessed=bytes_moved, transcendentals=0)


def build_basis(order_list, points_total):
    points = jnp.arange(points_total, dtype=jnp.int32)
    angles = (order_list[:, None] * points[None, :] % points_total).astype(jnp.float32) * (
        2.0 * math.pi / points_total
    )
    factor = math.sqrt(2.0 / points_total)
    stacked = jnp.stack([factor * jnp.cos(angles), -factor * jnp.sin(angles)], axis=1)
    return stacked.astype(jnp.bfloat16).reshape(2 * order_list.shape[0], points_total)


def basis_by_point(order_list, points):
    shape = points.shape + order_list.shape
    angles = (points[..., None] * order_list % NLON).astype(F32) * (2.0 * math.pi / NLON)
    factor = math.sqrt(2.0 / NLON)
    stacked = jnp.stack([factor * jnp.cos(angles), -factor * jnp.sin(angles)], axis=-1)
    return stacked.astype(BF16).reshape(shape[:-1] + (2 * shape[-1],))


def spread(running, values, weights, targets):
    channels = values.shape[-1]
    contrib = values.astype(jnp.float32) * weights[:, :, None]
    return running.at[targets.reshape(-1)].add(contrib.reshape(-1, channels))


def mixing_matrix(mix_weight):
    real_part = mix_weight[0]
    imag_part = mix_weight[1]
    return jnp.concatenate(
        [
            jnp.concatenate([real_part, -imag_part], axis=1),
            jnp.concatenate([imag_part, real_part], axis=1),
        ],
        axis=0,
    )


def regrid_all(piece, sources, targets, weights, cells_dev):
    shard_count, slot_count = sources.shape
    channels = piece.shape[0]
    src_rows = piece.shape[1] // shard_count
    piece_rows = piece.T
    offsets = jnp.arange(shard_count, dtype=jnp.int32)[:, None] * src_rows
    picked = jnp.take(piece_rows, (offsets + sources).reshape(-1), axis=0)
    picked = picked.reshape(shard_count, slot_count, channels)
    empty = jnp.zeros((cells_dev, channels), jnp.float32)
    return spread(empty, picked, weights, targets).astype(jnp.bfloat16)


def dense_encoder(regridded, enc_w1, enc_b1, enc_w2, enc_b2):
    hidden = jnp.dot(enc_w1, regridded, preferred_element_type=jnp.float32) + enc_b1[:, None]
    hidden = jax.nn.gelu(hidden, approximate=False).astype(jnp.bfloat16)
    return (
        jnp.dot(enc_w2, hidden, preferred_element_type=jnp.float32) + enc_b2[:, None]
    ).astype(jnp.bfloat16)


def encoder_by_cell(regridded, enc_w1, enc_b1, enc_w2, enc_b2):
    hidden = jnp.dot(regridded, enc_w1.T, preferred_element_type=F32) + enc_b1
    hidden = jax.nn.gelu(hidden, approximate=False).astype(BF16)
    return (jnp.dot(hidden, enc_w2.T, preferred_element_type=F32) + enc_b2).astype(BF16)


def regrid_kernel(live, src_ref, cols_ref, row_ref, out_ref, contrib, *, channels, shards, slots, src_rows):
    step = pl.program_id(0)
    height, rows = out_ref.shape

    @pl.when(step == 0)
    def _():
        contrib[...] = jnp.zeros_like(contrib)
        lane = lax.broadcasted_iota(jnp.int32, (slots, src_rows), 1).astype(F32)

        def one(j, carry):
            at = pl.ds(pl.multiple_of(j * slots, slots), slots)
            index = cols_ref[at, 0:1]
            weight = cols_ref[at, 1:2]
            hot = (index == lane).astype(BF16)
            picked = lax.dot_general(
                hot, src_ref[j], (((1,), (1,)), ((), ())), preferred_element_type=F32
            )
            value = picked * weight
            upper = value.astype(BF16)
            lower = (value - upper.astype(F32)).astype(BF16)
            contrib[at, 0:channels] = upper
            contrib[at, LANES : LANES + channels] = lower
            return carry

        lax.fori_loop(0, shards, one, 0)

    here = pl.ds(pl.multiple_of(step * rows, rows), rows)
    used = jnp.logical_or(step == 0, step * rows < live[0])

    @pl.when(used)
    def _():
        cell = cols_ref[here, 2:3]
        total = jnp.zeros((rows, 2 * LANES), F32)
        for s in range(shards):
            same = (cell == row_ref[:, s * slots : (s + 1) * slots]).astype(BF16)
            total += jnp.dot(
                same, contrib[s * slots : (s + 1) * slots, :], preferred_element_type=F32
            )
        merged = total[:, :LANES] + total[:, LANES:]
        lane = lax.broadcasted_iota(jnp.int32, (rows, LANES), 1)
        for place in range(4):
            merged = jnp.where(
                lane == channels + place, cols_ref[here, 3 + place : 4 + place], merged
            )
        out_ref[...] = merged.T[:height].astype(BF16)

    @pl.when(jnp.logical_not(used))
    def _():
        out_ref[...] = jnp.zeros_like(out_ref)


def regrid_listed(source_all, recv_src, recv_cell, recv_weight, lat_dev, lon_dev, slot_count):
    shards, channels, src_rows = source_all.shape
    total = recv_src.shape[0]
    keys = jnp.where(recv_weight != 0, recv_cell, lat_dev * lon_dev)
    ordered = jnp.sort(keys)
    lead = jnp.concatenate([jnp.ones((1,), jnp.bool_), ordered[1:] != ordered[:-1]])
    limits = jnp.arange(lat_dev + 1, dtype=jnp.int32) * lon_dev
    starts = jnp.sum((keys[None, :] < limits[:, None]).astype(jnp.int32), axis=1)
    live = starts[lat_dev:]
    starts = jnp.zeros((total,), jnp.int32).at[: lat_dev + 1].set(starts)
    cols = jnp.stack(
        [
            recv_src.astype(F32),
            recv_weight,
            ordered.astype(F32),
            (ordered % lon_dev).astype(F32),
            lead.astype(F32),
            (starts // 128).astype(F32),
            (starts % 128).astype(F32),
            jnp.zeros((total,), F32),
        ],
        axis=1,
    )
    rows = min(512, total)
    height = -(-(channels + 4) // TILE) * TILE
    return pl.pallas_call(
        functools.partial(
            regrid_kernel, channels=channels, shards=shards, slots=slot_count, src_rows=src_rows
        ),
        grid_spec=pltpu.PrefetchScalarGridSpec(
            num_scalar_prefetch=1,
            grid=(total // rows,),
            in_specs=[
                pl.BlockSpec((shards, channels, src_rows), lambda i, n: (0, 0, 0)),
                pl.BlockSpec((total, 8), lambda i, n: (0, 0)),
                pl.BlockSpec((1, total), lambda i, n: (0, 0)),
            ],
            out_specs=pl.BlockSpec((height, rows), lambda i, n: (0, i)),
            scratch_shapes=[pltpu.VMEM((total, 2 * LANES), BF16)],
        ),
        out_shape=jax.ShapeDtypeStruct((height, total), BF16),
        compiler_params=pltpu.CompilerParams(vmem_limit_bytes=VMEM_BYTES),
        cost_estimate=work(4 * total * total * LANES, 2 * total * LANES),
    )(live, source_all, cols, keys.astype(F32)[None, :])


def zonal_kernel(
    starts,
    rows_ref,
    w1_ref,
    b1_ref,
    w2_ref,
    b2_ref,
    basis_ref,
    sums_ref,
    *rest,
    channels,
    blocks,
    block_rows,
    lat_dev,
):
    *out_refs, delta, hots, base = rest
    step = pl.program_id(0)
    total = blocks * block_rows
    lats, height, width = out_refs[0].shape
    columns = height * len(out_refs)
    chunk = min(512, block_rows)

    def encode(values):
        hidden = jnp.dot(values, w1_ref[...], preferred_element_type=F32) + b1_ref[...]
        hidden = 0.5 * hidden * (1.0 + lax.erf(hidden * math.sqrt(0.5)))
        encoded = jnp.dot(hidden.astype(BF16), w2_ref[...], preferred_element_type=F32)
        return (encoded + b2_ref[...]).astype(BF16).astype(F32)

    @pl.when(step == 0)
    def _():
        empty = encode(jnp.zeros((TILE, rows_ref.shape[1]), BF16))[0:1]
        base[...] = sums_ref[...] * empty
        delta[pl.ds(total, WINDOW), :] = jnp.zeros((WINDOW, width), BF16)
        hots[pl.ds(total, WINDOW), :] = jnp.zeros((WINDOW, columns), BF16)
        points = basis_ref.shape[1]
        lane = lax.broadcasted_iota(jnp.int32, (chunk, points), 1).astype(F32)

        per_block = block_rows // chunk

        def one_block(k, carry):
            used = starts[k, lat_dev] + TILE + WINDOW
            count = jnp.minimum((used + chunk - 1) // chunk, per_block)

            def one(j, inner):
                at = pl.ds(pl.multiple_of(k * block_rows + j * chunk, chunk), chunk)
                part = pl.ds(pl.multiple_of(j * chunk, chunk), chunk)
                values = rows_ref[k, :, part].astype(F32).T
                delta[at, :] = (encode(values.astype(BF16)) - empty).astype(BF16)
                point = values[:, channels : channels + 1]
                lead = values[:, channels + 1 : channels + 2]
                point = jnp.where(lead > 0.5, point, -1.0)
                hot = (point == lane).astype(BF16)
                hots[at, :] = jnp.dot(hot, basis_ref[k], preferred_element_type=F32).astype(BF16)
                return inner

            return lax.fori_loop(0, count, one, carry)

        lax.fori_loop(0, blocks, one_block, 0)

    place = lax.broadcasted_iota(jnp.int32, (WINDOW, columns), 0)

    def latitude(tt, carry):
        t = step * lats + tt
        lows, highs, firsts = [], [], []
        most = jnp.int32(1)
        for k in range(blocks):
            low = starts[k, t] + k * block_rows
            high = starts[k, t + 1] + k * block_rows
            first = (low // TILE) * TILE
            most = jnp.maximum(most, (high - first + WINDOW - 1) // WINDOW)
            lows.append(low)
            highs.append(high)
            firsts.append(first)

        def window(j, running):
            left, right = [], []
            for k in range(blocks):
                ceiling = (highs[k] + TILE - 1) // TILE * TILE
                first = jnp.minimum(firsts[k] + j * WINDOW, ceiling)
                first = pl.multiple_of(first, TILE)
                at = pl.ds(first, WINDOW)
                inside = (place >= lows[k] - first) & (place < highs[k] - first)
                left.append(jnp.where(inside, hots[at, :].astype(F32), 0.0).astype(BF16))
                right.append(delta[at, :])
            return running + lax.dot_general(
                jnp.concatenate(left, axis=0),
                jnp.concatenate(right, axis=0),
                (((0,), (0,)), ((), ())),
                preferred_element_type=F32,
            )

        result = window(0, base[...])
        result = lax.fori_loop(1, most, window, result).astype(BF16)
        for g, out_ref in enumerate(out_refs):
            out_ref[tt] = result[g * height : (g + 1) * height, :]
        return carry

    lax.fori_loop(0, lats, latitude, 0)


def zonal_transform(
    rows, starts, w1, b1, w2, b2, basis, sums, lat_dev, pieces, channels, lats=15
):
    blocks, depth, block_rows = rows.shape
    width = w2.shape[1]
    columns = basis.shape[2]
    height = columns // pieces
    total = blocks * block_rows
    whole = lambda shape: pl.BlockSpec(
        shape, lambda i, s: (0,) * len(shape), pipeline_mode=pl.Buffered(1)
    )
    return pl.pallas_call(
        functools.partial(
            zonal_kernel,
            channels=channels,
            blocks=blocks,
            block_rows=block_rows,
            lat_dev=lat_dev,
        ),
        grid_spec=pltpu.PrefetchScalarGridSpec(
            num_scalar_prefetch=1,
            grid=(lat_dev // lats,),
            in_specs=[
                whole(rows.shape),
                whole(w1.shape),
                whole(b1.shape),
                whole(w2.shape),
                whole(b2.shape),
                whole(basis.shape),
                whole(sums.shape),
            ],
            out_specs=[pl.BlockSpec((lats, height, width), lambda i, s: (i, 0, 0))] * pieces,
            scratch_shapes=[
                pltpu.VMEM((total + WINDOW, width), BF16),
                pltpu.VMEM((total + WINDOW, columns), BF16),
                pltpu.VMEM((columns, width), F32),
            ],
        ),
        out_shape=[jax.ShapeDtypeStruct((lat_dev, height, width), BF16)] * pieces,
        compiler_params=pltpu.CompilerParams(vmem_limit_bytes=VMEM_BYTES),
        cost_estimate=work(50 * total * width * 2 * columns, 2 * total * width),
    )(starts, rows, w1, b1, w2, b2, basis, sums)


def orders_kernel(place, bands, *refs, group, pieces):
    spec_refs = refs[:pieces]
    fwd_ref, inv_ref, mix_ref, swap_ref, out_ref, arrived, taken, made, sems = refs[pieces:]
    order = pl.program_id(0)
    lats = spec_refs[0].shape[0]
    lat_total, _, width = arrived.shape
    halves, lanes = out_ref.shape[1], out_ref.shape[4]
    side = 2 * group

    @pl.when(order == 0)
    def _():
        copies = [
            pltpu.make_async_copy(ref, arrived.at[pl.ds(bands[d] * lats, lats)], sems.at[d])
            for d, ref in enumerate(spec_refs)
        ]
        for copy in copies:
            copy.start()
        for copy in copies:
            copy.wait()

        def one(j, carry):
            at = pl.ds(pl.multiple_of(j * side, side), side)
            block = arrived[at].reshape(side * side, width)
            turned = jnp.dot(swap_ref[...], block, preferred_element_type=F32).astype(BF16)
            taken[:, at, :] = turned.reshape(side, side, width)
            return carry

        lax.fori_loop(0, lat_total // side, one, 0)

    spectrum = jnp.concatenate([taken[2 * order], taken[2 * order + 1]], axis=1)
    coeffs = lax.dot_general(
        fwd_ref[0], spectrum, (((0,), (0,)), ((), ())), preferred_element_type=F32
    ).astype(BF16)
    mixed = jnp.dot(coeffs, mix_ref[...], preferred_element_type=F32).astype(BF16)
    made[order] = jnp.dot(inv_ref[0], mixed, preferred_element_type=F32).astype(BF16)

    @pl.when(order == group - 1)
    def _():
        def one(j, carry):
            first = pl.multiple_of(j * side, side)
            at = pl.ds(first, side)
            columns = []
            for h in range(halves):
                pieces = []
                for r in range(group):
                    for c in range(2):
                        low = (c * halves + h) * lanes
                        pieces.append(made[r, at, low : low + lanes])
                columns.append(jnp.concatenate(pieces, axis=0))
            block = jnp.concatenate(columns, axis=1)
            turned = jnp.dot(swap_ref[...], block, preferred_element_type=F32).astype(BF16)
            for i in range(side):
                spot = place[first + i]
                for h in range(halves):
                    out_ref[spot // 64, h, spot % 64] = turned[
                        i * side : (i + 1) * side, h * lanes : (h + 1) * lanes
                    ]
            return carry

        lax.fori_loop(0, lat_total // side, one, 0)


def order_steps(place, bands, spectra, fwd_table, inv_table, mix_t, first, parts, halves):
    pieces = len(spectra)
    lats, side, width = spectra[0].shape
    lat_total = lats * pieces
    degrees = fwd_table.shape[2]
    group = side // 2
    index = jnp.arange(side * side, dtype=jnp.int32)
    swapped = (index % side) * side + index // side
    swap = (swapped[:, None] == index[None, :]).astype(BF16)
    both = 2 * width
    part_lats = lat_total // parts
    out_shape = (parts, halves, part_lats, side, width // halves)
    return pl.pallas_call(
        functools.partial(orders_kernel, group=group, pieces=pieces),
        grid_spec=pltpu.PrefetchScalarGridSpec(
            num_scalar_prefetch=2,
            grid=(group,),
            in_specs=[pl.BlockSpec(memory_space=pl.ANY)] * pieces
            + [
                pl.BlockSpec((1, lat_total, degrees), lambda r, s, b: (first + r, 0, 0)),
                pl.BlockSpec((1, lat_total, degrees), lambda r, s, b: (first + r, 0, 0)),
                pl.BlockSpec((both, both), lambda r, s, b: (0, 0)),
                pl.BlockSpec((side * side, side * side), lambda r, s, b: (0, 0)),
            ],
            out_specs=pl.BlockSpec(out_shape, lambda r, s, b: (0, 0, 0, 0, 0)),
            scratch_shapes=[
                pltpu.VMEM((lat_total, side, width), BF16),
                pltpu.VMEM((side, lat_total, width), BF16),
                pltpu.VMEM((group, lat_total, both), BF16),
                pltpu.SemaphoreType.DMA((pieces,)),
            ],
        ),
        out_shape=jax.ShapeDtypeStruct(out_shape, BF16),
        compiler_params=pltpu.CompilerParams(vmem_limit_bytes=VMEM_BYTES),
        cost_estimate=work(
            group * 2 * both * degrees * (2 * lat_total + both), 8 * group * degrees * lat_total
        ),
    )(place, bands, *spectra, fwd_table, inv_table, mix_t, swap)


def synthesis_kernel(*refs):
    *mode_refs, basis_ref, out_ref = refs
    sources, _, height, lanes = mode_refs[0].shape
    blocks = out_ref.shape[0]
    lats = mode_refs[0].shape[1]
    points = out_ref.shape[1] // lats
    right = jnp.concatenate(
        [
            jnp.concatenate(
                [ref[:, t].reshape(sources * height, lanes) for ref in mode_refs], axis=0
            )
            for t in range(lats)
        ],
        axis=1,
    )

    def one(k, carry):
        value = jnp.dot(basis_ref[k], right, preferred_element_type=F32)
        span = 4 * points
        for t in range(0, lats, 4):
            rows = [value[:points, (t + i) * lanes : (t + i + 1) * lanes] for i in range(4)]
            low = t * points
            out_ref[k, low : low + span, :] = jnp.concatenate(rows, axis=0).astype(BF16)
        return carry

    lax.fori_loop(0, blocks, one, 0)


def synthesis_steps(modes, basis, points, lats, first, count):
    sources, _, height, lanes = modes[0].shape
    blocks = basis.shape[0]
    offset = first // lats
    return pl.pallas_call(
        synthesis_kernel,
        grid=(-(-count // lats),),
        in_specs=[
            pl.BlockSpec((sources, lats, height, lanes), lambda i: (0, i + offset, 0, 0))
            for _ in modes
        ]
        + [pl.BlockSpec(basis.shape, lambda i: (0, 0, 0))],
        out_specs=pl.BlockSpec((blocks, lats * points, lanes), lambda i: (0, i, 0)),
        out_shape=jax.ShapeDtypeStruct((blocks, count * points, lanes), BF16),
        compiler_params=pltpu.CompilerParams(vmem_limit_bytes=VMEM_BYTES),
        cost_estimate=work(2 * count * lanes * basis.size, 4 * blocks * count * points * lanes),
    )(*modes, basis)


def finish_kernel(part_ref, enc_ref, out_ref, *, first, whole_groups, rest_rows):
    quarters, halves, rows, lanes = part_ref.shape
    group = pl.program_id(0) + first

    @pl.when(group < whole_groups)
    def _():
        for q in range(quarters):
            at = pl.ds(q * rows, rows)
            for h in range(halves):
                across = pl.ds(h * lanes, lanes)
                total = enc_ref[at, across].astype(F32) + part_ref[q, h].astype(F32)
                out_ref[at, across] = total.astype(BF16)

    @pl.when(group >= whole_groups)
    def _():
        count = quarters * rest_rows
        for h in range(halves):
            across = pl.ds(h * lanes, lanes)
            pieces = [part_ref[q, h].astype(F32)[:rest_rows] for q in range(quarters)]
            total = enc_ref[:count, across].astype(F32) + jnp.concatenate(pieces, axis=0)
            out_ref[:count, across] = total.astype(BF16)


def finish_steps(part, running, lats, points, first, whole_groups, rest):
    quarters, halves, count, lanes = part.shape
    rows = lats * points
    return pl.pallas_call(
        functools.partial(
            finish_kernel, first=first, whole_groups=whole_groups, rest_rows=rest * points
        ),
        grid=(-(-count // rows),),
        in_specs=[
            pl.BlockSpec((quarters, halves, rows, lanes), lambda i: (0, 0, i, 0)),
            pl.BlockSpec((quarters * rows, halves * lanes), lambda i: (i + first, 0)),
        ],
        out_specs=pl.BlockSpec((quarters * rows, halves * lanes), lambda i: (i + first, 0)),
        out_shape=jax.ShapeDtypeStruct(running.shape, BF16),
        input_output_aliases={1: 0},
        compiler_params=pltpu.CompilerParams(vmem_limit_bytes=VMEM_BYTES),
        cost_estimate=work(part.size * 4, 6 * part.size),
    )(part, running)


def listed_plan(
    source_cells,
    recv_src,
    recv_cell,
    recv_weight,
    enc_w1,
    enc_b1,
    enc_w2,
    enc_b2,
    mix_weight,
    fwd_table,
    inv_table,
):
    lon_count = lax.axis_size("lon")
    lat_count = lax.axis_size("lat")
    channels = source_cells.shape[0]
    slot_count = recv_src.shape[0] // lon_count
    lat_total = fwd_table.shape[2]
    lat_dev = lat_total // lat_count
    lon_dev = NLON // lon_count
    cells_dev = lat_dev * lon_dev
    width = enc_w1.shape[0]
    ord_dev = fwd_table.shape[0]
    halves = width // LANES
    quarters = lon_count // halves
    part_lats = lat_dev // quarters

    source_all = jnp.broadcast_to(source_cells[None], (lon_count,) + source_cells.shape)
    source_all = lax.all_to_all(source_all, "lon", split_axis=0, concat_axis=0, tiled=True)
    listed = regrid_listed(
        source_all, recv_src, recv_cell, recv_weight, lat_dev, lon_dev, slot_count
    )
    band = lax.all_gather(listed, "lon", axis=0, tiled=False)
    coded = band[:, channels + 2 : channels + 4, : lat_dev + 1].astype(jnp.int32)
    starts = coded[:, 0] * 128 + coded[:, 1]

    mine = lax.axis_index("lon")
    sets = ord_dev // ORDER_GROUP
    bands = lax.axis_index("lat") ^ jnp.arange(lat_count, dtype=jnp.int32)
    owned = (
        (bands[None, :, None] * lon_count + mine) * ord_dev
        + jnp.arange(ord_dev, dtype=jnp.int32).reshape(sets, 1, ORDER_GROUP)
    ).reshape(-1)
    point_rows = -(-lon_dev // LANES) * LANES
    at = jnp.arange(lon_count, dtype=jnp.int32)[:, None] * lon_dev + jnp.arange(
        point_rows, dtype=jnp.int32
    )
    inside = (jnp.arange(point_rows) < lon_dev)[None, :, None]
    basis_in = jnp.where(inside, basis_by_point(owned, at), 0)
    sums = jnp.sum(basis_in.astype(F32), axis=(0, 1))[:, None]
    w1 = jnp.zeros((band.shape[1], width), BF16).at[:channels].set(enc_w1.T)
    spectra = zonal_transform(
        band,
        starts,
        w1,
        enc_b1[None, :],
        enc_w2.T,
        enc_b2[None, :],
        basis_in,
        sums,
        lat_dev,
        sets * lat_count,
        channels,
    )

    run = quarters * LATS
    whole_groups = lat_dev // run
    rest = (lat_dev - whole_groups * run) // quarters
    lat = np.arange(lat_dev)
    tail = lat - whole_groups * run
    to_part = np.where(tail < 0, lat % run // LATS, tail // max(rest, 1))
    to_row = np.where(tail < 0, lat // run * LATS + lat % LATS, whole_groups * LATS + tail % max(rest, 1))
    place = (np.arange(lat_count)[:, None] * quarters + to_part) * 64 + to_row
    place = jnp.asarray(place.reshape(-1), jnp.int32)

    mix_t = mixing_matrix(mix_weight).T
    fwd_by_lat = fwd_table.transpose(0, 2, 1)
    modes, waiting, got = [], [], []
    for g in range(sets):
        sent = spectra[g * lat_count : (g + 1) * lat_count]
        if got:
            sent, got[1:] = lax.optimization_barrier((list(sent), got[1:]))
        got = [sent[0]] + [
            lax.ppermute(sent[d], "lat", [(i, i ^ d) for i in range(lat_count)])
            for d in range(1, lat_count)
        ]
        waiting.append(got)
    for g in range(sets):
        made = order_steps(
            place,
            bands,
            waiting[g],
            fwd_by_lat,
            inv_table,
            mix_t,
            g * ORDER_GROUP,
            lat_count * quarters,
            halves,
        )
        made = made.reshape(lat_count * lon_count, part_lats, 2 * ORDER_GROUP, LANES)
        modes.append(
            lax.all_to_all(made, ("lat", "lon"), split_axis=0, concat_axis=0, tiled=True)
        )

    pad_points = -(-lon_dev // TILE) * TILE
    at = jnp.arange(lon_count, dtype=jnp.int32)[:, None] * lon_dev + jnp.arange(
        pad_points, dtype=jnp.int32
    )
    inside = (jnp.arange(pad_points) < lon_dev)[None, :, None]
    listing = jnp.arange(ORDERS, dtype=jnp.int32).reshape(-1, sets, ORDER_GROUP)
    basis_out = basis_by_point(listing.transpose(1, 0, 2).reshape(-1), at)
    basis_out = jnp.where(inside, basis_out, 0)

    piece = source_all.transpose(1, 0, 2).reshape(channels, -1)
    regridded = regrid_all(
        piece,
        recv_src.reshape(lon_count, slot_count),
        recv_cell.reshape(lon_count, slot_count),
        recv_weight.reshape(lon_count, slot_count),
        cells_dev,
    )
    encoded = encoder_by_cell(regridded, enc_w1, enc_b1, enc_w2, enc_b2)
    modes[-1], encoded = lax.optimization_barrier((modes[-1], encoded))
    running = encoded
    step = CHUNK_RUNS * LATS
    for first in range(0, part_lats, step):
        count = min(step, part_lats - first)
        part = synthesis_steps(modes, basis_out, lon_dev, LATS, first, count)
        part = lax.all_to_all(part, "lon", split_axis=0, concat_axis=0, tiled=True)
        part = part.reshape(quarters, halves, count * lon_dev, LANES)
        running = finish_steps(part, running, LATS, lon_dev, first // LATS, whole_groups, rest)
    return running.T


def dense_plan(
    source_cells,
    recv_src,
    recv_cell,
    recv_weight,
    enc_w1,
    enc_b1,
    enc_w2,
    enc_b2,
    mix_weight,
    fwd_table,
    inv_table,
):
    lon_count = lax.axis_size("lon")
    lat_count = lax.axis_size("lat")
    slot_count = recv_src.shape[0] // lon_count
    sources = recv_src.reshape(lon_count, slot_count)
    targets = recv_cell.reshape(lon_count, slot_count)
    weights = recv_weight.reshape(lon_count, slot_count)
    lat_total = fwd_table.shape[2]
    lat_dev = lat_total // lat_count
    lon_dev = NLON // lon_count
    cells_dev = lat_dev * lon_dev
    width = enc_w1.shape[0]
    ch_dev = width // lon_count
    orders_total = ORDERS
    ord_dev = fwd_table.shape[0]
    piece = lax.all_gather(source_cells, "lon", axis=1, tiled=True)
    regridded = regrid_all(piece, sources, targets, weights, cells_dev).T
    encoded = dense_encoder(regridded, enc_w1, enc_b1, enc_w2, enc_b2)
    blocked = encoded.reshape(width, lat_dev, 1, lon_dev)
    circles = lax.all_to_all(blocked, "lon", split_axis=0, concat_axis=2, tiled=True).reshape(
        ch_dev * lat_dev, NLON
    )
    natural_order = jnp.arange(orders_total, dtype=jnp.int32)
    dft_basis = build_basis(natural_order, NLON)
    spectra = lax.dot_general(
        dft_basis, circles, (((1,), (1,)), ((), ())), preferred_element_type=jnp.float32
    )
    spectra = spectra.astype(jnp.bfloat16).reshape(orders_total, 2, ch_dev, lat_dev)
    by_order = lax.all_to_all(
        lax.all_to_all(spectra, "lat", split_axis=0, concat_axis=3, tiled=True),
        "lon",
        split_axis=0,
        concat_axis=2,
        tiled=True,
    )
    by_order = by_order.reshape(ord_dev, 2 * width, lat_total)
    coeffs = jnp.einsum(
        "mrt,mlt->mrl", by_order, fwd_table, preferred_element_type=jnp.float32
    ).astype(jnp.bfloat16)
    mix_block = mixing_matrix(mix_weight)
    mixed = jnp.einsum("gr,mrl->mgl", mix_block, coeffs, preferred_element_type=jnp.float32).astype(
        jnp.bfloat16
    )
    synth_in = jnp.einsum(
        "mrl,mtl->mrt", mixed, inv_table, preferred_element_type=jnp.float32
    ).astype(jnp.bfloat16)
    synth_in = synth_in.reshape(ord_dev, 2, width, lat_total)
    returned_modes = lax.all_to_all(
        lax.all_to_all(synth_in, "lon", split_axis=2, concat_axis=0, tiled=True),
        "lat",
        split_axis=3,
        concat_axis=0,
        tiled=True,
    )
    returned_modes = returned_modes.reshape(2 * orders_total, ch_dev * lat_dev)
    synthesis = lax.dot_general(
        returned_modes, dft_basis, (((0,), (0,)), ((), ())), preferred_element_type=jnp.float32
    )
    synthesis = synthesis.astype(jnp.bfloat16).reshape(ch_dev, lat_dev, lon_count, lon_dev)
    regained = lax.all_to_all(synthesis, "lon", split_axis=2, concat_axis=0, tiled=True).reshape(
        width, cells_dev
    )
    return (encoded.astype(jnp.float32) + regained.astype(jnp.float32)).astype(jnp.bfloat16)


def solution(mesh):
    in_specs = (
        P(None, ("lat", "lon")),
        P(("lat", "lon")),
        P(("lat", "lon")),
        P(("lat", "lon")),
        P(),
        P(),
        P(),
        P(),
        P(),
        P(("lat", "lon"), None, None),
        P(("lat", "lon"), None, None),
    )
    out_specs = P(None, ("lat", "lon"))
    lon_count = mesh.shape["lon"]
    lat_count = mesh.shape["lat"]

    def on_device(*arrays):
        slots = arrays[1].shape[0]
        width = arrays[4].shape[0]
        ord_dev, _, lat_total = arrays[9].shape
        lat_dev = lat_total // lat_count
        cells_dev = lat_dev * (NLON // lon_count)
        halves = max(1, width // LANES)
        fits = (
            slots * 4 <= cells_dev
            and width % LANES == 0
            and lon_count % halves == 0
            and lat_dev % (lon_count // halves) == 0
            and lat_dev % 15 == 0
            and lat_count & (lat_count - 1) == 0
            and 4 * (NLON // lon_count) % TILE == 0
            and lat_dev // (lon_count // halves) < 64
            and ord_dev % ORDER_GROUP == 0
            and lat_total % TILE == 0
        )
        return listed_plan(*arrays) if fits else dense_plan(*arrays)

    return jax.shard_map(
        on_device, mesh=mesh, in_specs=in_specs, out_specs=out_specs, check_vma=False
    )
```

```python
import functools
import math

import jax
import jax.numpy as jnp
import numpy as np
from jax import lax
from jax.experimental import pallas as pl
from jax.experimental.pallas import tpu as pltpu
from jax.sharding import PartitionSpec as P

NLON = 1440
ORDERS = 512
LANES = 128
TILE = 16
WINDOW = 48
UNROLL = 3
LATS = 8
CHUNK_RUNS = 2
ORDER_GROUP = 8
VMEM_BYTES = 60 * 1024 * 1024

F32 = jnp.float32
BF16 = jnp.bfloat16


def work(flops, bytes_moved):
    return pl.CostEstimate(flops=flops, bytes_accessed=bytes_moved, transcendentals=0)


def build_basis(order_list, points_total):
    points = jnp.arange(points_total, dtype=jnp.int32)
    angles = (order_list[:, None] * points[None, :] % points_total).astype(jnp.float32) * (
        2.0 * math.pi / points_total
    )
    factor = math.sqrt(2.0 / points_total)
    stacked = jnp.stack([factor * jnp.cos(angles), -factor * jnp.sin(angles)], axis=1)
    return stacked.astype(jnp.bfloat16).reshape(2 * order_list.shape[0], points_total)


def basis_by_point(order_list, points):
    shape = points.shape + order_list.shape
    angles = (points[..., None] * order_list % NLON).astype(F32) * (2.0 * math.pi / NLON)
    factor = math.sqrt(2.0 / NLON)
    stacked = jnp.stack([factor * jnp.cos(angles), -factor * jnp.sin(angles)], axis=-1)
    return stacked.astype(BF16).reshape(shape[:-1] + (2 * shape[-1],))


def spread(running, values, weights, targets):
    channels = values.shape[-1]
    contrib = values.astype(jnp.float32) * weights[:, :, None]
    return running.at[targets.reshape(-1)].add(contrib.reshape(-1, channels))


def mixing_matrix(mix_weight):
    real_part = mix_weight[0]
    imag_part = mix_weight[1]
    return jnp.concatenate(
        [
            jnp.concatenate([real_part, -imag_part], axis=1),
            jnp.concatenate([imag_part, real_part], axis=1),
        ],
        axis=0,
    )


def regrid_all(piece, sources, targets, weights, cells_dev):
    shard_count, slot_count = sources.shape
    channels = piece.shape[0]
    src_rows = piece.shape[1] // shard_count
    piece_rows = piece.T
    offsets = jnp.arange(shard_count, dtype=jnp.int32)[:, None] * src_rows
    picked = jnp.take(piece_rows, (offsets + sources).reshape(-1), axis=0)
    picked = picked.reshape(shard_count, slot_count, channels)
    empty = jnp.zeros((cells_dev, channels), jnp.float32)
    return spread(empty, picked, weights, targets).astype(jnp.bfloat16)


def dense_encoder(regridded, enc_w1, enc_b1, enc_w2, enc_b2):
    hidden = jnp.dot(enc_w1, regridded, preferred_element_type=jnp.float32) + enc_b1[:, None]
    hidden = jax.nn.gelu(hidden, approximate=False).astype(jnp.bfloat16)
    return (
        jnp.dot(enc_w2, hidden, preferred_element_type=jnp.float32) + enc_b2[:, None]
    ).astype(jnp.bfloat16)


def encoder_by_cell(regridded, enc_w1, enc_b1, enc_w2, enc_b2):
    hidden = jnp.dot(regridded, enc_w1.T, preferred_element_type=F32) + enc_b1
    hidden = jax.nn.gelu(hidden, approximate=False).astype(BF16)
    return (jnp.dot(hidden, enc_w2.T, preferred_element_type=F32) + enc_b2).astype(BF16)


def regrid_kernel(live, src_ref, cols_ref, row_ref, out_ref, contrib, *, channels, shards, slots, src_rows):
    step = pl.program_id(0)
    height, rows = out_ref.shape

    @pl.when(step == 0)
    def _():
        contrib[...] = jnp.zeros_like(contrib)
        lane = lax.broadcasted_iota(jnp.int32, (slots, src_rows), 1).astype(F32)

        def one(j, carry):
            at = pl.ds(pl.multiple_of(j * slots, slots), slots)
            index = cols_ref[at, 0:1]
            weight = cols_ref[at, 1:2]
            hot = (index == lane).astype(BF16)
            picked = lax.dot_general(
                hot, src_ref[j], (((1,), (1,)), ((), ())), preferred_element_type=F32
            )
            value = picked * weight
            upper = value.astype(BF16)
            lower = (value - upper.astype(F32)).astype(BF16)
            contrib[at, 0:channels] = upper
            contrib[at, LANES : LANES + channels] = lower
            return carry

        lax.fori_loop(0, shards, one, 0)

    here = pl.ds(pl.multiple_of(step * rows, rows), rows)
    used = jnp.logical_or(step == 0, step * rows < live[0])

    @pl.when(used)
    def _():
        cell = cols_ref[here, 2:3]
        total = jnp.zeros((rows, 2 * LANES), F32)
        for s in range(shards):
            same = (cell == row_ref[:, s * slots : (s + 1) * slots]).astype(BF16)
            total += jnp.dot(
                same, contrib[s * slots : (s + 1) * slots, :], preferred_element_type=F32
            )
        merged = total[:, :LANES] + total[:, LANES:]
        lane = lax.broadcasted_iota(jnp.int32, (rows, LANES), 1)
        for place in range(4):
            merged = jnp.where(
                lane == channels + place, cols_ref[here, 3 + place : 4 + place], merged
            )
        out_ref[...] = merged.T[:height].astype(BF16)

    @pl.when(jnp.logical_not(used))
    def _():
        out_ref[...] = jnp.zeros_like(out_ref)


def regrid_listed(source_all, recv_src, recv_cell, recv_weight, lat_dev, lon_dev, slot_count):
    shards, channels, src_rows = source_all.shape
    total = recv_src.shape[0]
    keys = jnp.where(recv_weight != 0, recv_cell, lat_dev * lon_dev)
    ordered = jnp.sort(keys)
    lead = jnp.concatenate([jnp.ones((1,), jnp.bool_), ordered[1:] != ordered[:-1]])
    limits = jnp.arange(lat_dev + 1, dtype=jnp.int32) * lon_dev
    starts = jnp.sum((keys[None, :] < limits[:, None]).astype(jnp.int32), axis=1)
    live = starts[lat_dev:]
    starts = jnp.zeros((total,), jnp.int32).at[: lat_dev + 1].set(starts)
    cols = jnp.stack(
        [
            recv_src.astype(F32),
            recv_weight,
            ordered.astype(F32),
            (ordered % lon_dev).astype(F32),
            lead.astype(F32),
            (starts // 128).astype(F32),
            (starts % 128).astype(F32),
            jnp.zeros((total,), F32),
        ],
        axis=1,
    )
    rows = min(512, total)
    height = -(-(channels + 4) // TILE) * TILE
    return pl.pallas_call(
        functools.partial(
            regrid_kernel, channels=channels, shards=shards, slots=slot_count, src_rows=src_rows
        ),
        grid_spec=pltpu.PrefetchScalarGridSpec(
            num_scalar_prefetch=1,
            grid=(total // rows,),
            in_specs=[
                pl.BlockSpec((shards, channels, src_rows), lambda i, n: (0, 0, 0)),
                pl.BlockSpec((total, 8), lambda i, n: (0, 0)),
                pl.BlockSpec((1, total), lambda i, n: (0, 0)),
            ],
            out_specs=pl.BlockSpec((height, rows), lambda i, n: (0, i)),
            scratch_shapes=[pltpu.VMEM((total, 2 * LANES), BF16)],
        ),
        out_shape=jax.ShapeDtypeStruct((height, total), BF16),
        compiler_params=pltpu.CompilerParams(vmem_limit_bytes=VMEM_BYTES),
        cost_estimate=work(4 * total * total * LANES, 2 * total * LANES),
    )(live, source_all, cols, keys.astype(F32)[None, :])


def transform_latitudes(starts, hots, delta, base, out_refs, first_lat, blocks):
    step = pl.program_id(0)
    groups, lats, _, _ = out_refs[0].shape
    columns = hots.shape[1]
    block_rows = (hots.shape[0] - WINDOW) // blocks
    place = lax.broadcasted_iota(jnp.int32, (WINDOW, columns), 0)

    def bounds(t):
        lows = [starts[k, t] + k * block_rows for k in range(blocks)]
        highs = [starts[k, t + 1] + k * block_rows for k in range(blocks)]
        firsts = [(low // TILE) * TILE for low in lows]
        most = jnp.int32(1)
        for k in range(blocks):
            most = jnp.maximum(most, (highs[k] - firsts[k] + WINDOW - 1) // WINDOW)
        return lows, highs, firsts, most

    def window(lows, highs, firsts):
        left, right = [], []
        for k in range(blocks):
            first = pl.multiple_of(firsts[k], TILE)
            at = pl.ds(first, WINDOW)
            inside = (place >= lows[k] - first) & (place < highs[k] - first)
            left.append(jnp.where(inside, hots[at, :].astype(F32), 0.0).astype(BF16))
            right.append(delta[at, :])
        return lax.dot_general(
            jnp.concatenate(left, axis=0),
            jnp.concatenate(right, axis=0),
            (((0,), (0,)), ((), ())),
            preferred_element_type=F32,
        )

    def store(tt, result):
        result = result.astype(BF16)
        low = 0
        for g in range(groups):
            for out_ref in out_refs:
                height = out_ref.shape[2]
                out_ref[g, tt] = result[low : low + height, :]
                low += height

    def several(b, carry):
        chosen = [b * UNROLL + u for u in range(UNROLL)]
        limits = [bounds(first_lat + step * lats + tt) for tt in chosen]
        most = limits[0][3]
        for limit in limits[1:]:
            most = jnp.maximum(most, limit[3])

        @pl.when(most == 1)
        def _():
            for tt, (lows, highs, firsts, _) in zip(chosen, limits):
                store(tt, base[...] + window(lows, highs, firsts))

        @pl.when(most > 1)
        def _():
            for tt, (lows, highs, firsts, count) in zip(chosen, limits):

                def more(j, running):
                    moved = [
                        jnp.minimum(firsts[k] + j * WINDOW, (highs[k] + TILE - 1) // TILE * TILE)
                        for k in range(blocks)
                    ]
                    return running + window(lows, highs, moved)

                store(tt, lax.fori_loop(0, count, more, base[...]))

        return carry

    lax.fori_loop(0, lats // UNROLL, several, 0)


def zonal_first_kernel(
    starts,
    rows_ref,
    w1_ref,
    b1_ref,
    w2_ref,
    b2_ref,
    basis_ref,
    sums_ref,
    *rest,
    channels,
    blocks,
    block_rows,
    lat_dev,
):
    *out_refs, delta_out, hots_out, base, delta, hots, sems = rest
    step = pl.program_id(0)
    total = blocks * block_rows
    width = delta.shape[1]
    columns = hots.shape[1]
    chunk = min(512, block_rows)
    copies = [
        pltpu.make_async_copy(delta, delta_out, sems.at[0]),
        pltpu.make_async_copy(hots, hots_out, sems.at[1]),
    ]

    def encode(values):
        hidden = jnp.dot(values, w1_ref[...], preferred_element_type=F32) + b1_ref[...]
        hidden = 0.5 * hidden * (1.0 + lax.erf(hidden * math.sqrt(0.5)))
        encoded = jnp.dot(hidden.astype(BF16), w2_ref[...], preferred_element_type=F32)
        return (encoded + b2_ref[...]).astype(BF16).astype(F32)

    @pl.when(step == 0)
    def _():
        empty = encode(jnp.zeros((TILE, rows_ref.shape[1]), BF16))[0:1]
        base[...] = sums_ref[...] * empty
        delta[pl.ds(total, WINDOW), :] = jnp.zeros((WINDOW, width), BF16)
        hots[pl.ds(total, WINDOW), :] = jnp.zeros((WINDOW, columns), BF16)
        points = basis_ref.shape[1]
        lane = lax.broadcasted_iota(jnp.int32, (chunk, points), 1).astype(F32)
        per_block = block_rows // chunk

        def one_block(k, carry):
            used = starts[k, lat_dev] + TILE + WINDOW
            count = jnp.minimum((used + chunk - 1) // chunk, per_block)

            def one(j, inner):
                at = pl.ds(pl.multiple_of(k * block_rows + j * chunk, chunk), chunk)
                part = pl.ds(pl.multiple_of(j * chunk, chunk), chunk)
                values = rows_ref[k, :, part].astype(F32).T
                delta[at, :] = (encode(values.astype(BF16)) - empty).astype(BF16)
                point = values[:, channels : channels + 1]
                lead = values[:, channels + 1 : channels + 2]
                point = jnp.where(lead > 0.5, point, -1.0)
                hot = (point == lane).astype(BF16)
                hots[at, :] = jnp.dot(hot, basis_ref[k], preferred_element_type=F32).astype(BF16)
                return inner

            return lax.fori_loop(0, count, one, carry)

        lax.fori_loop(0, blocks, one_block, 0)
        for copy in copies:
            copy.start()

    transform_latitudes(starts, hots, delta, base, out_refs, 0, blocks)

    @pl.when(step == pl.num_programs(0) - 1)
    def _():
        for copy in copies:
            copy.wait()


def zonal_second_kernel(starts, delta, hots, base, *out_refs, first_lat, blocks):
    transform_latitudes(starts, hots, delta, base, out_refs, first_lat, blocks)


def whole_block(shape):
    return pl.BlockSpec(shape, lambda i, *_: (0,) * len(shape), pipeline_mode=pl.Buffered(1))


def zonal_outputs(groups, lat_count, heights, lats, width):
    shapes = [jax.ShapeDtypeStruct((groups, lat_count, h, width), BF16) for h in heights]
    specs = [pl.BlockSpec((groups, lats, h, width), lambda i, *_: (0, i, 0, 0)) for h in heights]
    return shapes, specs


def zonal_transform(rows, starts, w1, b1, w2, b2, basis, sums, lat_dev, groups, sets, channels):
    blocks, _, block_rows = rows.shape
    width = w2.shape[1]
    columns = basis.shape[2]
    height = columns // groups
    total = blocks * block_rows
    lats = 15
    early = lat_dev // 3 // lats * lats
    late = lat_dev - early
    flops = 25 * total * width * 2 * columns
    shapes, specs = zonal_outputs(groups, early, [height], lats, width)
    kept = [
        jax.ShapeDtypeStruct((total + WINDOW, width), BF16),
        jax.ShapeDtypeStruct((total + WINDOW, columns), BF16),
        jax.ShapeDtypeStruct((columns, width), F32),
    ]
    inputs = (rows, w1, b1, w2, b2, basis, sums)
    first, delta, hots, base = pl.pallas_call(
        functools.partial(
            zonal_first_kernel,
            channels=channels,
            blocks=blocks,
            block_rows=block_rows,
            lat_dev=lat_dev,
        ),
        grid_spec=pltpu.PrefetchScalarGridSpec(
            num_scalar_prefetch=1,
            grid=(early // lats,),
            in_specs=[whole_block(a.shape) for a in inputs],
            out_specs=specs
            + [pl.BlockSpec(memory_space=pl.ANY)] * 2
            + [whole_block((columns, width))],
            scratch_shapes=[
                pltpu.VMEM((total + WINDOW, width), BF16),
                pltpu.VMEM((total + WINDOW, columns), BF16),
                pltpu.SemaphoreType.DMA((2,)),
            ],
        ),
        out_shape=shapes + kept,
        compiler_params=pltpu.CompilerParams(vmem_limit_bytes=VMEM_BYTES),
        cost_estimate=work(flops, 4 * total * width),
    )(starts, *inputs)
    shapes, specs = zonal_outputs(groups, late, [height // sets] * sets, lats, width)
    second = pl.pallas_call(
        functools.partial(zonal_second_kernel, first_lat=early, blocks=blocks),
        grid_spec=pltpu.PrefetchScalarGridSpec(
            num_scalar_prefetch=1,
            grid=(late // lats,),
            in_specs=[whole_block(a.shape) for a in (delta, hots, base)],
            out_specs=specs,
        ),
        out_shape=shapes,
        compiler_params=pltpu.CompilerParams(vmem_limit_bytes=VMEM_BYTES),
        cost_estimate=work(flops, 4 * total * width),
    )(starts, delta, hots, base)
    return first, second


def orders_kernel(place, *refs, group, pieces, rows):
    spec_refs = refs[:pieces]
    fwd_ref, inv_ref, mix_ref, swap_ref, out_ref, arrived, taken, made, sems = refs[pieces:]
    order = pl.program_id(0)
    lat_total, _, width = arrived.shape
    halves, lanes = out_ref.shape[1], out_ref.shape[4]
    side = 2 * group
    count = spec_refs[0].shape[0]

    @pl.when(order == 0)
    def _():
        copies = []
        for i in range(count):
            low = i * lat_total // count
            for ref, row in zip(spec_refs, rows):
                lats = ref.shape[1]
                copies.append(
                    pltpu.make_async_copy(
                        ref.at[i, :, pl.ds(row, side)],
                        arrived.at[pl.ds(low, lats)],
                        sems.at[len(copies)],
                    )
                )
                low += lats
        for copy in copies:
            copy.start()
        for copy in copies:
            copy.wait()

        def one(j, carry):
            at = pl.ds(pl.multiple_of(j * side, side), side)
            block = arrived[at].reshape(side * side, width)
            turned = jnp.dot(swap_ref[...], block, preferred_element_type=F32).astype(BF16)
            taken[:, at, :] = turned.reshape(side, side, width)
            return carry

        lax.fori_loop(0, lat_total // side, one, 0)

    spectrum = jnp.concatenate([taken[2 * order], taken[2 * order + 1]], axis=1)
    coeffs = lax.dot_general(
        fwd_ref[0], spectrum, (((0,), (0,)), ((), ())), preferred_element_type=F32
    ).astype(BF16)
    mixed = jnp.dot(coeffs, mix_ref[...], preferred_element_type=F32).astype(BF16)
    made[order] = jnp.dot(inv_ref[0], mixed, preferred_element_type=F32).astype(BF16)

    @pl.when(order == group - 1)
    def _():
        def one(j, carry):
            first = pl.multiple_of(j * side, side)
            at = pl.ds(first, side)
            columns = []
            for h in range(halves):
                pieces = []
                for r in range(group):
                    for c in range(2):
                        low = (c * halves + h) * lanes
                        pieces.append(made[r, at, low : low + lanes])
                columns.append(jnp.concatenate(pieces, axis=0))
            block = jnp.concatenate(columns, axis=1)
            turned = jnp.dot(swap_ref[...], block, preferred_element_type=F32).astype(BF16)
            for i in range(side):
                spot = place[first + i]
                for h in range(halves):
                    out_ref[spot // 64, h, spot % 64] = turned[
                        i * side : (i + 1) * side, h * lanes : (h + 1) * lanes
                    ]
            return carry

        lax.fori_loop(0, lat_total // side, one, 0)


def order_steps(place, spectra, rows, fwd_table, inv_table, mix_t, first, parts, halves):
    pieces = len(spectra)
    count, width = spectra[0].shape[0], spectra[0].shape[3]
    side = 2 * ORDER_GROUP
    lat_total = fwd_table.shape[1]
    degrees = fwd_table.shape[2]
    group = side // 2
    index = jnp.arange(side * side, dtype=jnp.int32)
    swapped = (index % side) * side + index // side
    swap = (swapped[:, None] == index[None, :]).astype(BF16)
    both = 2 * width
    part_lats = lat_total // parts
    out_shape = (parts, halves, part_lats, side, width // halves)
    return pl.pallas_call(
        functools.partial(orders_kernel, group=group, pieces=pieces, rows=rows),
        grid_spec=pltpu.PrefetchScalarGridSpec(
            num_scalar_prefetch=1,
            grid=(group,),
            in_specs=[pl.BlockSpec(memory_space=pl.ANY)] * pieces
            + [
                pl.BlockSpec((1, lat_total, degrees), lambda r, s: (first + r, 0, 0)),
                pl.BlockSpec((1, lat_total, degrees), lambda r, s: (first + r, 0, 0)),
                pl.BlockSpec((both, both), lambda r, s: (0, 0)),
                pl.BlockSpec((side * side, side * side), lambda r, s: (0, 0)),
            ],
            out_specs=pl.BlockSpec(out_shape, lambda r, s: (0, 0, 0, 0, 0)),
            scratch_shapes=[
                pltpu.VMEM((lat_total, side, width), BF16),
                pltpu.VMEM((side, lat_total, width), BF16),
                pltpu.VMEM((group, lat_total, both), BF16),
                pltpu.SemaphoreType.DMA((pieces * count,)),
            ],
        ),
        out_shape=jax.ShapeDtypeStruct(out_shape, BF16),
        compiler_params=pltpu.CompilerParams(vmem_limit_bytes=VMEM_BYTES),
        cost_estimate=work(
            group * 2 * both * degrees * (2 * lat_total + both), 8 * group * degrees * lat_total
        ),
    )(place, *spectra, fwd_table, inv_table, mix_t, swap)


def synthesis_kernel(*refs):
    *mode_refs, basis_ref, out_ref = refs
    sources, _, height, lanes = mode_refs[0].shape
    blocks = out_ref.shape[0]
    lats = mode_refs[0].shape[1]
    points = out_ref.shape[1] // lats
    right = jnp.concatenate(
        [
            jnp.concatenate(
                [ref[:, t].reshape(sources * height, lanes) for ref in mode_refs], axis=0
            )
            for t in range(lats)
        ],
        axis=1,
    )

    def one(k, carry):
        value = jnp.dot(basis_ref[k], right, preferred_element_type=F32)
        span = 4 * points
        for t in range(0, lats, 4):
            rows = [value[:points, (t + i) * lanes : (t + i + 1) * lanes] for i in range(4)]
            low = t * points
            out_ref[k, low : low + span, :] = jnp.concatenate(rows, axis=0).astype(BF16)
        return carry

    lax.fori_loop(0, blocks, one, 0)


def synthesis_steps(modes, basis, points, lats, first, count):
    sources, _, height, lanes = modes[0].shape
    blocks = basis.shape[0]
    offset = first // lats
    return pl.pallas_call(
        synthesis_kernel,
        grid=(-(-count // lats),),
        in_specs=[
            pl.BlockSpec((sources, lats, height, lanes), lambda i: (0, i + offset, 0, 0))
            for _ in modes
        ]
        + [pl.BlockSpec(basis.shape, lambda i: (0, 0, 0))],
        out_specs=pl.BlockSpec((blocks, lats * points, lanes), lambda i: (0, i, 0)),
        out_shape=jax.ShapeDtypeStruct((blocks, count * points, lanes), BF16),
        compiler_params=pltpu.CompilerParams(vmem_limit_bytes=VMEM_BYTES),
        cost_estimate=work(2 * count * lanes * basis.size, 4 * blocks * count * points * lanes),
    )(*modes, basis)


def finish_kernel(part_ref, enc_ref, out_ref, *, first, whole_groups, rest_rows):
    quarters, halves, rows, lanes = part_ref.shape
    group = pl.program_id(0) + first

    @pl.when(group < whole_groups)
    def _():
        for q in range(quarters):
            at = pl.ds(q * rows, rows)
            for h in range(halves):
                across = pl.ds(h * lanes, lanes)
                total = enc_ref[at, across].astype(F32) + part_ref[q, h].astype(F32)
                out_ref[at, across] = total.astype(BF16)

    @pl.when(group >= whole_groups)
    def _():
        count = quarters * rest_rows
        for h in range(halves):
            across = pl.ds(h * lanes, lanes)
            pieces = [part_ref[q, h].astype(F32)[:rest_rows] for q in range(quarters)]
            total = enc_ref[:count, across].astype(F32) + jnp.concatenate(pieces, axis=0)
            out_ref[:count, across] = total.astype(BF16)


def finish_steps(part, running, lats, points, first, whole_groups, rest):
    quarters, halves, count, lanes = part.shape
    rows = lats * points
    return pl.pallas_call(
        functools.partial(
            finish_kernel, first=first, whole_groups=whole_groups, rest_rows=rest * points
        ),
        grid=(-(-count // rows),),
        in_specs=[
            pl.BlockSpec((quarters, halves, rows, lanes), lambda i: (0, 0, i, 0)),
            pl.BlockSpec((quarters * rows, halves * lanes), lambda i: (i + first, 0)),
        ],
        out_specs=pl.BlockSpec((quarters * rows, halves * lanes), lambda i: (i + first, 0)),
        out_shape=jax.ShapeDtypeStruct(running.shape, BF16),
        input_output_aliases={1: 0},
        compiler_params=pltpu.CompilerParams(vmem_limit_bytes=VMEM_BYTES),
        cost_estimate=work(part.size * 4, 6 * part.size),
    )(part, running)


def listed_plan(
    source_cells,
    recv_src,
    recv_cell,
    recv_weight,
    enc_w1,
    enc_b1,
    enc_w2,
    enc_b2,
    mix_weight,
    fwd_table,
    inv_table,
):
    lon_count = lax.axis_size("lon")
    lat_count = lax.axis_size("lat")
    channels = source_cells.shape[0]
    slot_count = recv_src.shape[0] // lon_count
    lat_total = fwd_table.shape[2]
    lat_dev = lat_total // lat_count
    lon_dev = NLON // lon_count
    cells_dev = lat_dev * lon_dev
    width = enc_w1.shape[0]
    ord_dev = fwd_table.shape[0]
    halves = width // LANES
    quarters = lon_count // halves
    part_lats = lat_dev // quarters

    source_all = jnp.broadcast_to(source_cells[None], (lon_count,) + source_cells.shape)
    source_all = lax.all_to_all(source_all, "lon", split_axis=0, concat_axis=0, tiled=True)
    listed = regrid_listed(
        source_all, recv_src, recv_cell, recv_weight, lat_dev, lon_dev, slot_count
    )
    band = lax.all_gather(listed, "lon", axis=0, tiled=False)
    coded = band[:, channels + 2 : channels + 4, : lat_dev + 1].astype(jnp.int32)
    starts = coded[:, 0] * 128 + coded[:, 1]

    mine = lax.axis_index("lon")
    sets = ord_dev // ORDER_GROUP
    owned = (
        (jnp.arange(lat_count, dtype=jnp.int32)[:, None] * lon_count + mine) * ord_dev
        + jnp.arange(ord_dev, dtype=jnp.int32)[None, :]
    ).reshape(-1)
    point_rows = -(-lon_dev // LANES) * LANES
    at = jnp.arange(lon_count, dtype=jnp.int32)[:, None] * lon_dev + jnp.arange(
        point_rows, dtype=jnp.int32
    )
    inside = (jnp.arange(point_rows) < lon_dev)[None, :, None]
    basis_in = jnp.where(inside, basis_by_point(owned, at), 0)
    sums = jnp.sum(basis_in.astype(F32), axis=(0, 1))[:, None]
    w1 = jnp.zeros((band.shape[1], width), BF16).at[:channels].set(enc_w1.T)
    first, second = zonal_transform(
        band,
        starts,
        w1,
        enc_b1[None, :],
        enc_w2.T,
        enc_b2[None, :],
        basis_in,
        sums,
        lat_dev,
        lat_count,
        sets,
        channels,
    )

    run = quarters * LATS
    whole_groups = lat_dev // run
    rest = (lat_dev - whole_groups * run) // quarters
    lat = np.arange(lat_dev)
    tail = lat - whole_groups * run
    to_part = np.where(tail < 0, lat % run // LATS, tail // max(rest, 1))
    to_row = np.where(tail < 0, lat // run * LATS + lat % LATS, whole_groups * LATS + tail % max(rest, 1))
    place = (np.arange(lat_count)[:, None] * quarters + to_part) * 64 + to_row
    place = jnp.asarray(place.reshape(-1), jnp.int32)

    mix_t = mixing_matrix(mix_weight).T
    fwd_by_lat = fwd_table.transpose(0, 2, 1)
    def exchange(piece):
        return lax.all_to_all(piece, "lat", split_axis=0, concat_axis=0, tiled=True)

    early = exchange(first)
    modes, waiting = [], []
    for g in range(sets):
        piece = second[g]
        if waiting:
            piece, waiting[-1] = lax.optimization_barrier((piece, waiting[-1]))
        waiting.append(exchange(piece))
    for g in range(sets):
        made = order_steps(
            place,
            [early, waiting[g]],
            [g * 2 * ORDER_GROUP, 0],
            fwd_by_lat,
            inv_table,
            mix_t,
            g * ORDER_GROUP,
            lat_count * quarters,
            halves,
        )
        made = made.reshape(lat_count * lon_count, part_lats, 2 * ORDER_GROUP, LANES)
        if g + 1 < sets:
            made, waiting[g + 1] = lax.optimization_barrier((made, waiting[g + 1]))
        modes.append(
            lax.all_to_all(made, ("lat", "lon"), split_axis=0, concat_axis=0, tiled=True)
        )

    pad_points = -(-lon_dev // TILE) * TILE
    at = jnp.arange(lon_count, dtype=jnp.int32)[:, None] * lon_dev + jnp.arange(
        pad_points, dtype=jnp.int32
    )
    inside = (jnp.arange(pad_points) < lon_dev)[None, :, None]
    listing = jnp.arange(ORDERS, dtype=jnp.int32).reshape(-1, sets, ORDER_GROUP)
    basis_out = basis_by_point(listing.transpose(1, 0, 2).reshape(-1), at)
    basis_out = jnp.where(inside, basis_out, 0)

    piece = source_all.transpose(1, 0, 2).reshape(channels, -1)
    regridded = regrid_all(
        piece,
        recv_src.reshape(lon_count, slot_count),
        recv_cell.reshape(lon_count, slot_count),
        recv_weight.reshape(lon_count, slot_count),
        cells_dev,
    )
    encoded = encoder_by_cell(regridded, enc_w1, enc_b1, enc_w2, enc_b2)
    modes[-1], encoded = lax.optimization_barrier((modes[-1], encoded))
    running = encoded
    step = CHUNK_RUNS * LATS
    for first in range(0, part_lats, step):
        count = min(step, part_lats - first)
        part = synthesis_steps(modes, basis_out, lon_dev, LATS, first, count)
        part = lax.all_to_all(part, "lon", split_axis=0, concat_axis=0, tiled=True)
        part = part.reshape(quarters, halves, count * lon_dev, LANES)
        running = finish_steps(part, running, LATS, lon_dev, first // LATS, whole_groups, rest)
    return running.T


def dense_plan(
    source_cells,
    recv_src,
    recv_cell,
    recv_weight,
    enc_w1,
    enc_b1,
    enc_w2,
    enc_b2,
    mix_weight,
    fwd_table,
    inv_table,
):
    lon_count = lax.axis_size("lon")
    lat_count = lax.axis_size("lat")
    slot_count = recv_src.shape[0] // lon_count
    sources = recv_src.reshape(lon_count, slot_count)
    targets = recv_cell.reshape(lon_count, slot_count)
    weights = recv_weight.reshape(lon_count, slot_count)
    lat_total = fwd_table.shape[2]
    lat_dev = lat_total // lat_count
    lon_dev = NLON // lon_count
    cells_dev = lat_dev * lon_dev
    width = enc_w1.shape[0]
    ch_dev = width // lon_count
    orders_total = ORDERS
    ord_dev = fwd_table.shape[0]
    piece = lax.all_gather(source_cells, "lon", axis=1, tiled=True)
    regridded = regrid_all(piece, sources, targets, weights, cells_dev).T
    encoded = dense_encoder(regridded, enc_w1, enc_b1, enc_w2, enc_b2)
    blocked = encoded.reshape(width, lat_dev, 1, lon_dev)
    circles = lax.all_to_all(blocked, "lon", split_axis=0, concat_axis=2, tiled=True).reshape(
        ch_dev * lat_dev, NLON
    )
    natural_order = jnp.arange(orders_total, dtype=jnp.int32)
    dft_basis = build_basis(natural_order, NLON)
    spectra = lax.dot_general(
        dft_basis, circles, (((1,), (1,)), ((), ())), preferred_element_type=jnp.float32
    )
    spectra = spectra.astype(jnp.bfloat16).reshape(orders_total, 2, ch_dev, lat_dev)
    by_order = lax.all_to_all(
        lax.all_to_all(spectra, "lat", split_axis=0, concat_axis=3, tiled=True),
        "lon",
        split_axis=0,
        concat_axis=2,
        tiled=True,
    )
    by_order = by_order.reshape(ord_dev, 2 * width, lat_total)
    coeffs = jnp.einsum(
        "mrt,mlt->mrl", by_order, fwd_table, preferred_element_type=jnp.float32
    ).astype(jnp.bfloat16)
    mix_block = mixing_matrix(mix_weight)
    mixed = jnp.einsum("gr,mrl->mgl", mix_block, coeffs, preferred_element_type=jnp.float32).astype(
        jnp.bfloat16
    )
    synth_in = jnp.einsum(
        "mrl,mtl->mrt", mixed, inv_table, preferred_element_type=jnp.float32
    ).astype(jnp.bfloat16)
    synth_in = synth_in.reshape(ord_dev, 2, width, lat_total)
    returned_modes = lax.all_to_all(
        lax.all_to_all(synth_in, "lon", split_axis=2, concat_axis=0, tiled=True),
        "lat",
        split_axis=3,
        concat_axis=0,
        tiled=True,
    )
    returned_modes = returned_modes.reshape(2 * orders_total, ch_dev * lat_dev)
    synthesis = lax.dot_general(
        returned_modes, dft_basis, (((0,), (0,)), ((), ())), preferred_element_type=jnp.float32
    )
    synthesis = synthesis.astype(jnp.bfloat16).reshape(ch_dev, lat_dev, lon_count, lon_dev)
    regained = lax.all_to_all(synthesis, "lon", split_axis=2, concat_axis=0, tiled=True).reshape(
        width, cells_dev
    )
    return (encoded.astype(jnp.float32) + regained.astype(jnp.float32)).astype(jnp.bfloat16)


def solution(mesh):
    in_specs = (
        P(None, ("lat", "lon")),
        P(("lat", "lon")),
        P(("lat", "lon")),
        P(("lat", "lon")),
        P(),
        P(),
        P(),
        P(),
        P(),
        P(("lat", "lon"), None, None),
        P(("lat", "lon"), None, None),
    )
    out_specs = P(None, ("lat", "lon"))
    lon_count = mesh.shape["lon"]
    lat_count = mesh.shape["lat"]

    def on_device(*arrays):
        slots = arrays[1].shape[0]
        width = arrays[4].shape[0]
        ord_dev, _, lat_total = arrays[9].shape
        lat_dev = lat_total // lat_count
        cells_dev = lat_dev * (NLON // lon_count)
        halves = max(1, width // LANES)
        fits = (
            slots * 4 <= cells_dev
            and width % LANES == 0
            and lon_count % halves == 0
            and lat_dev % (lon_count // halves) == 0
            and lat_dev % 45 == 0
            and 4 * (NLON // lon_count) % TILE == 0
            and lat_dev // (lon_count // halves) < 64
            and ord_dev % ORDER_GROUP == 0
            and lat_total % TILE == 0
        )
        return listed_plan(*arrays) if fits else dense_plan(*arrays)

    return jax.shard_map(
        on_device, mesh=mesh, in_specs=in_specs, out_specs=out_specs, check_vma=False
    )
```

```python
import functools
import math

import jax
import jax.numpy as jnp
import numpy as np
from jax import lax
from jax.experimental import pallas as pl
from jax.experimental.pallas import tpu as pltpu
from jax.sharding import PartitionSpec as P

NLON = 1440
ORDERS = 512
LANES = 128
TILE = 16
WINDOW = 48
UNROLL = 3
LATS = 8
CHUNK_CUTS = (1, 4)
ORDER_GROUP = 8
VMEM_BYTES = 60 * 1024 * 1024

F32 = jnp.float32
BF16 = jnp.bfloat16


def work(flops, bytes_moved):
    return pl.CostEstimate(flops=flops, bytes_accessed=bytes_moved, transcendentals=0)


def build_basis(order_list, points_total):
    points = jnp.arange(points_total, dtype=jnp.int32)
    angles = (order_list[:, None] * points[None, :] % points_total).astype(jnp.float32) * (
        2.0 * math.pi / points_total
    )
    factor = math.sqrt(2.0 / points_total)
    stacked = jnp.stack([factor * jnp.cos(angles), -factor * jnp.sin(angles)], axis=1)
    return stacked.astype(jnp.bfloat16).reshape(2 * order_list.shape[0], points_total)


def basis_by_point(order_list, points):
    shape = points.shape + order_list.shape
    angles = (points[..., None] * order_list % NLON).astype(F32) * (2.0 * math.pi / NLON)
    factor = math.sqrt(2.0 / NLON)
    stacked = jnp.stack([factor * jnp.cos(angles), -factor * jnp.sin(angles)], axis=-1)
    return stacked.astype(BF16).reshape(shape[:-1] + (2 * shape[-1],))


def spread(running, values, weights, targets):
    channels = values.shape[-1]
    contrib = values.astype(jnp.float32) * weights[:, :, None]
    return running.at[targets.reshape(-1)].add(contrib.reshape(-1, channels))


def mixing_matrix(mix_weight):
    real_part = mix_weight[0]
    imag_part = mix_weight[1]
    return jnp.concatenate(
        [
            jnp.concatenate([real_part, -imag_part], axis=1),
            jnp.concatenate([imag_part, real_part], axis=1),
        ],
        axis=0,
    )


def regrid_all(piece, sources, targets, weights, cells_dev):
    shard_count, slot_count = sources.shape
    channels = piece.shape[0]
    src_rows = piece.shape[1] // shard_count
    piece_rows = piece.T
    offsets = jnp.arange(shard_count, dtype=jnp.int32)[:, None] * src_rows
    picked = jnp.take(piece_rows, (offsets + sources).reshape(-1), axis=0)
    picked = picked.reshape(shard_count, slot_count, channels)
    empty = jnp.zeros((cells_dev, channels), jnp.float32)
    return spread(empty, picked, weights, targets).astype(jnp.bfloat16)


def dense_encoder(regridded, enc_w1, enc_b1, enc_w2, enc_b2):
    hidden = jnp.dot(enc_w1, regridded, preferred_element_type=jnp.float32) + enc_b1[:, None]
    hidden = jax.nn.gelu(hidden, approximate=False).astype(jnp.bfloat16)
    return (
        jnp.dot(enc_w2, hidden, preferred_element_type=jnp.float32) + enc_b2[:, None]
    ).astype(jnp.bfloat16)


def encoder_by_cell(regridded, enc_w1, enc_b1, enc_w2, enc_b2):
    hidden = jnp.dot(regridded, enc_w1.T, preferred_element_type=F32) + enc_b1
    hidden = jax.nn.gelu(hidden, approximate=False).astype(BF16)
    return (jnp.dot(hidden, enc_w2.T, preferred_element_type=F32) + enc_b2).astype(BF16)


def regrid_kernel(live, src_ref, cols_ref, row_ref, out_ref, contrib, *, channels, shards, slots, src_rows):
    step = pl.program_id(0)
    height, rows = out_ref.shape

    @pl.when(step == 0)
    def _():
        contrib[...] = jnp.zeros_like(contrib)
        lane = lax.broadcasted_iota(jnp.int32, (slots, src_rows), 1).astype(F32)

        def one(j, carry):
            at = pl.ds(pl.multiple_of(j * slots, slots), slots)
            index = cols_ref[at, 0:1]
            weight = cols_ref[at, 1:2]
            hot = (index == lane).astype(BF16)
            picked = lax.dot_general(
                hot, src_ref[j], (((1,), (1,)), ((), ())), preferred_element_type=F32
            )
            value = picked * weight
            upper = value.astype(BF16)
            lower = (value - upper.astype(F32)).astype(BF16)
            contrib[at, 0:channels] = upper
            contrib[at, LANES : LANES + channels] = lower
            return carry

        lax.fori_loop(0, shards, one, 0)

    here = pl.ds(pl.multiple_of(step * rows, rows), rows)
    used = jnp.logical_or(step == 0, step * rows < live[0])

    @pl.when(used)
    def _():
        cell = cols_ref[here, 2:3]
        total = jnp.zeros((rows, 2 * LANES), F32)
        for s in range(shards):
            same = (cell == row_ref[:, s * slots : (s + 1) * slots]).astype(BF16)
            total += jnp.dot(
                same, contrib[s * slots : (s + 1) * slots, :], preferred_element_type=F32
            )
        merged = total[:, :LANES] + total[:, LANES:]
        lane = lax.broadcasted_iota(jnp.int32, (rows, LANES), 1)
        for place in range(4):
            merged = jnp.where(
                lane == channels + place, cols_ref[here, 3 + place : 4 + place], merged
            )
        out_ref[...] = merged.T[:height].astype(BF16)

    @pl.when(jnp.logical_not(used))
    def _():
        out_ref[...] = jnp.zeros_like(out_ref)


def regrid_listed(source_all, recv_src, recv_cell, recv_weight, lat_dev, lon_dev, slot_count):
    shards, channels, src_rows = source_all.shape
    total = recv_src.shape[0]
    keys = jnp.where(recv_weight != 0, recv_cell, lat_dev * lon_dev)
    ordered = jnp.sort(keys)
    lead = jnp.concatenate([jnp.ones((1,), jnp.bool_), ordered[1:] != ordered[:-1]])
    limits = jnp.arange(lat_dev + 1, dtype=jnp.int32) * lon_dev
    starts = jnp.sum((keys[None, :] < limits[:, None]).astype(jnp.int32), axis=1)
    live = starts[lat_dev:]
    starts = jnp.zeros((total,), jnp.int32).at[: lat_dev + 1].set(starts)
    cols = jnp.stack(
        [
            recv_src.astype(F32),
            recv_weight,
            ordered.astype(F32),
            (ordered % lon_dev).astype(F32),
            lead.astype(F32),
            (starts // 128).astype(F32),
            (starts % 128).astype(F32),
            jnp.zeros((total,), F32),
        ],
        axis=1,
    )
    rows = min(512, total)
    height = -(-(channels + 4) // TILE) * TILE
    return pl.pallas_call(
        functools.partial(
            regrid_kernel, channels=channels, shards=shards, slots=slot_count, src_rows=src_rows
        ),
        grid_spec=pltpu.PrefetchScalarGridSpec(
            num_scalar_prefetch=1,
            grid=(total // rows,),
            in_specs=[
                pl.BlockSpec((shards, channels, src_rows), lambda i, n: (0, 0, 0)),
                pl.BlockSpec((total, 8), lambda i, n: (0, 0)),
                pl.BlockSpec((1, total), lambda i, n: (0, 0)),
            ],
            out_specs=pl.BlockSpec((height, rows), lambda i, n: (0, i)),
            scratch_shapes=[pltpu.VMEM((total, 2 * LANES), BF16)],
        ),
        out_shape=jax.ShapeDtypeStruct((height, total), BF16),
        compiler_params=pltpu.CompilerParams(vmem_limit_bytes=VMEM_BYTES),
        cost_estimate=work(4 * total * total * LANES, 2 * total * LANES),
    )(live, source_all, cols, keys.astype(F32)[None, :])


def transform_latitudes(starts, hots, delta, base, out_refs, first_lat, blocks):
    step = pl.program_id(0)
    groups, lats, _, _ = out_refs[0].shape
    columns = hots.shape[1]
    block_rows = (hots.shape[0] - WINDOW) // blocks
    place = lax.broadcasted_iota(jnp.int32, (WINDOW, columns), 0)

    def bounds(t):
        lows = [starts[k, t] + k * block_rows for k in range(blocks)]
        highs = [starts[k, t + 1] + k * block_rows for k in range(blocks)]
        firsts = [(low // TILE) * TILE for low in lows]
        most = jnp.int32(1)
        for k in range(blocks):
            most = jnp.maximum(most, (highs[k] - firsts[k] + WINDOW - 1) // WINDOW)
        return lows, highs, firsts, most

    def window(lows, highs, firsts):
        left, right = [], []
        for k in range(blocks):
            first = pl.multiple_of(firsts[k], TILE)
            at = pl.ds(first, WINDOW)
            inside = (place >= lows[k] - first) & (place < highs[k] - first)
            left.append(jnp.where(inside, hots[at, :].astype(F32), 0.0).astype(BF16))
            right.append(delta[at, :])
        return lax.dot_general(
            jnp.concatenate(left, axis=0),
            jnp.concatenate(right, axis=0),
            (((0,), (0,)), ((), ())),
            preferred_element_type=F32,
        )

    def store(tt, result):
        result = result.astype(BF16)
        low = 0
        for g in range(groups):
            for out_ref in out_refs:
                height = out_ref.shape[2]
                out_ref[g, tt] = result[low : low + height, :]
                low += height

    def several(b, carry):
        chosen = [b * UNROLL + u for u in range(UNROLL)]
        limits = [bounds(first_lat + step * lats + tt) for tt in chosen]
        most = limits[0][3]
        for limit in limits[1:]:
            most = jnp.maximum(most, limit[3])

        @pl.when(most == 1)
        def _():
            for tt, (lows, highs, firsts, _) in zip(chosen, limits):
                store(tt, base[...] + window(lows, highs, firsts))

        @pl.when(most > 1)
        def _():
            for tt, (lows, highs, firsts, count) in zip(chosen, limits):

                def more(j, running):
                    moved = [
                        jnp.minimum(firsts[k] + j * WINDOW, (highs[k] + TILE - 1) // TILE * TILE)
                        for k in range(blocks)
                    ]
                    return running + window(lows, highs, moved)

                store(tt, lax.fori_loop(0, count, more, base[...]))

        return carry

    lax.fori_loop(0, lats // UNROLL, several, 0)


def zonal_first_kernel(
    starts,
    rows_ref,
    w1_ref,
    b1_ref,
    w2_ref,
    b2_ref,
    basis_ref,
    sums_ref,
    *rest,
    channels,
    blocks,
    block_rows,
    lat_dev,
):
    *out_refs, delta_out, hots_out, base, delta, hots, sems = rest
    step = pl.program_id(0)
    total = blocks * block_rows
    width = delta.shape[1]
    columns = hots.shape[1]
    chunk = min(512, block_rows)
    copies = [
        pltpu.make_async_copy(delta, delta_out, sems.at[0]),
        pltpu.make_async_copy(hots, hots_out, sems.at[1]),
    ]

    def encode(values):
        hidden = jnp.dot(values, w1_ref[...], preferred_element_type=F32) + b1_ref[...]
        hidden = 0.5 * hidden * (1.0 + lax.erf(hidden * math.sqrt(0.5)))
        encoded = jnp.dot(hidden.astype(BF16), w2_ref[...], preferred_element_type=F32)
        return (encoded + b2_ref[...]).astype(BF16).astype(F32)

    @pl.when(step == 0)
    def _():
        empty = encode(jnp.zeros((TILE, rows_ref.shape[1]), BF16))[0:1]
        base[...] = sums_ref[...] * empty
        delta[pl.ds(total, WINDOW), :] = jnp.zeros((WINDOW, width), BF16)
        hots[pl.ds(total, WINDOW), :] = jnp.zeros((WINDOW, columns), BF16)
        points = basis_ref.shape[1]
        lane = lax.broadcasted_iota(jnp.int32, (chunk, points), 1).astype(F32)
        per_block = block_rows // chunk

        def one_block(k, carry):
            used = starts[k, lat_dev] + TILE + WINDOW
            count = jnp.minimum((used + chunk - 1) // chunk, per_block)

            def one(j, inner):
                at = pl.ds(pl.multiple_of(k * block_rows + j * chunk, chunk), chunk)
                part = pl.ds(pl.multiple_of(j * chunk, chunk), chunk)
                values = rows_ref[k, :, part].astype(F32).T
                delta[at, :] = (encode(values.astype(BF16)) - empty).astype(BF16)
                point = values[:, channels : channels + 1]
                lead = values[:, channels + 1 : channels + 2]
                point = jnp.where(lead > 0.5, point, -1.0)
                hot = (point == lane).astype(BF16)
                hots[at, :] = jnp.dot(hot, basis_ref[k], preferred_element_type=F32).astype(BF16)
                return inner

            return lax.fori_loop(0, count, one, carry)

        lax.fori_loop(0, blocks, one_block, 0)
        for copy in copies:
            copy.start()

    transform_latitudes(starts, hots, delta, base, out_refs, 0, blocks)

    @pl.when(step == pl.num_programs(0) - 1)
    def _():
        for copy in copies:
            copy.wait()


def zonal_second_kernel(starts, delta, hots, base, *out_refs, first_lat, blocks):
    transform_latitudes(starts, hots, delta, base, out_refs, first_lat, blocks)


def whole_block(shape):
    return pl.BlockSpec(shape, lambda i, *_: (0,) * len(shape), pipeline_mode=pl.Buffered(1))


def zonal_outputs(groups, lat_count, heights, lats, width):
    shapes = [jax.ShapeDtypeStruct((groups, lat_count, h, width), BF16) for h in heights]
    specs = [pl.BlockSpec((groups, lats, h, width), lambda i, *_: (0, i, 0, 0)) for h in heights]
    return shapes, specs


def zonal_transform(rows, starts, w1, b1, w2, b2, basis, sums, lat_dev, groups, sets, channels):
    blocks, _, block_rows = rows.shape
    width = w2.shape[1]
    columns = basis.shape[2]
    height = columns // groups
    total = blocks * block_rows
    lats = 15
    early = lat_dev // 3 // lats * lats
    late = lat_dev - early
    flops = 25 * total * width * 2 * columns
    shapes, specs = zonal_outputs(groups, early, [height], lats, width)
    kept = [
        jax.ShapeDtypeStruct((total + WINDOW, width), BF16),
        jax.ShapeDtypeStruct((total + WINDOW, columns), BF16),
        jax.ShapeDtypeStruct((columns, width), F32),
    ]
    inputs = (rows, w1, b1, w2, b2, basis, sums)
    first, delta, hots, base = pl.pallas_call(
        functools.partial(
            zonal_first_kernel,
            channels=channels,
            blocks=blocks,
            block_rows=block_rows,
            lat_dev=lat_dev,
        ),
        grid_spec=pltpu.PrefetchScalarGridSpec(
            num_scalar_prefetch=1,
            grid=(early // lats,),
            in_specs=[whole_block(a.shape) for a in inputs],
            out_specs=specs
            + [pl.BlockSpec(memory_space=pl.ANY)] * 2
            + [whole_block((columns, width))],
            scratch_shapes=[
                pltpu.VMEM((total + WINDOW, width), BF16),
                pltpu.VMEM((total + WINDOW, columns), BF16),
                pltpu.SemaphoreType.DMA((2,)),
            ],
        ),
        out_shape=shapes + kept,
        compiler_params=pltpu.CompilerParams(vmem_limit_bytes=VMEM_BYTES),
        cost_estimate=work(flops, 4 * total * width),
    )(starts, *inputs)
    shapes, specs = zonal_outputs(groups, late, [height // sets] * sets, lats, width)
    second = pl.pallas_call(
        functools.partial(zonal_second_kernel, first_lat=early, blocks=blocks),
        grid_spec=pltpu.PrefetchScalarGridSpec(
            num_scalar_prefetch=1,
            grid=(late // lats,),
            in_specs=[whole_block(a.shape) for a in (delta, hots, base)],
            out_specs=specs,
        ),
        out_shape=shapes,
        compiler_params=pltpu.CompilerParams(vmem_limit_bytes=VMEM_BYTES),
        cost_estimate=work(flops, 4 * total * width),
    )(starts, delta, hots, base)
    return first, second


def orders_kernel(place, *refs, group, pieces, rows):
    spec_refs = refs[:pieces]
    fwd_ref, inv_ref, mix_ref, swap_ref, out_ref, arrived, taken, made, sems = refs[pieces:]
    order = pl.program_id(0)
    lat_total, _, width = arrived.shape
    halves, lanes = out_ref.shape[1], out_ref.shape[4]
    side = 2 * group
    count = spec_refs[0].shape[0]

    @pl.when(order == 0)
    def _():
        copies = []
        for i in range(count):
            low = i * lat_total // count
            for ref, row in zip(spec_refs, rows):
                lats = ref.shape[1]
                copies.append(
                    pltpu.make_async_copy(
                        ref.at[i, :, pl.ds(row, side)],
                        arrived.at[pl.ds(low, lats)],
                        sems.at[len(copies)],
                    )
                )
                low += lats
        for copy in copies:
            copy.start()
        for copy in copies:
            copy.wait()

        def one(j, carry):
            at = pl.ds(pl.multiple_of(j * side, side), side)
            block = arrived[at].reshape(side * side, width)
            turned = jnp.dot(swap_ref[...], block, preferred_element_type=F32).astype(BF16)
            taken[:, at, :] = turned.reshape(side, side, width)
            return carry

        lax.fori_loop(0, lat_total // side, one, 0)

    spectrum = jnp.concatenate([taken[2 * order], taken[2 * order + 1]], axis=1)
    coeffs = lax.dot_general(
        fwd_ref[0], spectrum, (((0,), (0,)), ((), ())), preferred_element_type=F32
    ).astype(BF16)
    mixed = jnp.dot(coeffs, mix_ref[...], preferred_element_type=F32).astype(BF16)
    made[order] = jnp.dot(inv_ref[0], mixed, preferred_element_type=F32).astype(BF16)

    @pl.when(order == group - 1)
    def _():
        def one(j, carry):
            first = pl.multiple_of(j * side, side)
            at = pl.ds(first, side)
            columns = []
            for h in range(halves):
                pieces = []
                for r in range(group):
                    for c in range(2):
                        low = (c * halves + h) * lanes
                        pieces.append(made[r, at, low : low + lanes])
                columns.append(jnp.concatenate(pieces, axis=0))
            block = jnp.concatenate(columns, axis=1)
            turned = jnp.dot(swap_ref[...], block, preferred_element_type=F32).astype(BF16)
            for i in range(side):
                spot = place[first + i]
                for h in range(halves):
                    out_ref[spot // 64, h, spot % 64] = turned[
                        i * side : (i + 1) * side, h * lanes : (h + 1) * lanes
                    ]
            return carry

        lax.fori_loop(0, lat_total // side, one, 0)


def order_steps(place, spectra, rows, fwd_table, inv_table, mix_t, first, parts, halves):
    pieces = len(spectra)
    count, width = spectra[0].shape[0], spectra[0].shape[3]
    side = 2 * ORDER_GROUP
    lat_total = fwd_table.shape[1]
    degrees = fwd_table.shape[2]
    group = side // 2
    index = jnp.arange(side * side, dtype=jnp.int32)
    swapped = (index % side) * side + index // side
    swap = (swapped[:, None] == index[None, :]).astype(BF16)
    both = 2 * width
    part_lats = lat_total // parts
    out_shape = (parts, halves, part_lats, side, width // halves)
    return pl.pallas_call(
        functools.partial(orders_kernel, group=group, pieces=pieces, rows=rows),
        grid_spec=pltpu.PrefetchScalarGridSpec(
            num_scalar_prefetch=1,
            grid=(group,),
            in_specs=[pl.BlockSpec(memory_space=pl.ANY)] * pieces
            + [
                pl.BlockSpec((1, lat_total, degrees), lambda r, s: (first + r, 0, 0)),
                pl.BlockSpec((1, lat_total, degrees), lambda r, s: (first + r, 0, 0)),
                pl.BlockSpec((both, both), lambda r, s: (0, 0)),
                pl.BlockSpec((side * side, side * side), lambda r, s: (0, 0)),
            ],
            out_specs=pl.BlockSpec(out_shape, lambda r, s: (0, 0, 0, 0, 0)),
            scratch_shapes=[
                pltpu.VMEM((lat_total, side, width), BF16),
                pltpu.VMEM((side, lat_total, width), BF16),
                pltpu.VMEM((group, lat_total, both), BF16),
                pltpu.SemaphoreType.DMA((pieces * count,)),
            ],
        ),
        out_shape=jax.ShapeDtypeStruct(out_shape, BF16),
        compiler_params=pltpu.CompilerParams(vmem_limit_bytes=VMEM_BYTES),
        cost_estimate=work(
            group * 2 * both * degrees * (2 * lat_total + both), 8 * group * degrees * lat_total
        ),
    )(place, *spectra, fwd_table, inv_table, mix_t, swap)


def synthesis_kernel(*refs):
    *mode_refs, basis_ref, out_ref = refs
    sources, _, height, lanes = mode_refs[0].shape
    blocks = out_ref.shape[0]
    lats = mode_refs[0].shape[1]
    points = out_ref.shape[1] // lats
    right = jnp.concatenate(
        [
            jnp.concatenate(
                [ref[:, t].reshape(sources * height, lanes) for ref in mode_refs], axis=0
            )
            for t in range(lats)
        ],
        axis=1,
    )

    def one(k, carry):
        value = jnp.dot(basis_ref[k], right, preferred_element_type=F32)
        span = 4 * points
        for t in range(0, lats, 4):
            rows = [value[:points, (t + i) * lanes : (t + i + 1) * lanes] for i in range(4)]
            low = t * points
            out_ref[k, low : low + span, :] = jnp.concatenate(rows, axis=0).astype(BF16)
        return carry

    lax.fori_loop(0, blocks, one, 0)


def synthesis_steps(modes, basis, points, lats, first, count):
    sources, _, height, lanes = modes[0].shape
    blocks = basis.shape[0]
    offset = first // lats
    return pl.pallas_call(
        synthesis_kernel,
        grid=(-(-count // lats),),
        in_specs=[
            pl.BlockSpec((sources, lats, height, lanes), lambda i: (0, i + offset, 0, 0))
            for _ in modes
        ]
        + [pl.BlockSpec(basis.shape, lambda i: (0, 0, 0))],
        out_specs=pl.BlockSpec((blocks, lats * points, lanes), lambda i: (0, i, 0)),
        out_shape=jax.ShapeDtypeStruct((blocks, count * points, lanes), BF16),
        compiler_params=pltpu.CompilerParams(vmem_limit_bytes=VMEM_BYTES),
        cost_estimate=work(2 * count * lanes * basis.size, 4 * blocks * count * points * lanes),
    )(*modes, basis)


def finish_kernel(part_ref, enc_ref, out_ref, *, first, whole_groups, rest_rows):
    quarters, halves, rows, lanes = part_ref.shape
    group = pl.program_id(0) + first

    @pl.when(group < whole_groups)
    def _():
        for q in range(quarters):
            at = pl.ds(q * rows, rows)
            for h in range(halves):
                across = pl.ds(h * lanes, lanes)
                total = enc_ref[at, across].astype(F32) + part_ref[q, h].astype(F32)
                out_ref[at, across] = total.astype(BF16)

    @pl.when(group >= whole_groups)
    def _():
        count = quarters * rest_rows
        for h in range(halves):
            across = pl.ds(h * lanes, lanes)
            pieces = [part_ref[q, h].astype(F32)[:rest_rows] for q in range(quarters)]
            total = enc_ref[:count, across].astype(F32) + jnp.concatenate(pieces, axis=0)
            out_ref[:count, across] = total.astype(BF16)


def finish_steps(part, running, lats, points, first, whole_groups, rest):
    quarters, halves, count, lanes = part.shape
    rows = lats * points
    return pl.pallas_call(
        functools.partial(
            finish_kernel, first=first, whole_groups=whole_groups, rest_rows=rest * points
        ),
        grid=(-(-count // rows),),
        in_specs=[
            pl.BlockSpec((quarters, halves, rows, lanes), lambda i: (0, 0, i, 0)),
            pl.BlockSpec((quarters * rows, halves * lanes), lambda i: (i + first, 0)),
        ],
        out_specs=pl.BlockSpec((quarters * rows, halves * lanes), lambda i: (i + first, 0)),
        out_shape=jax.ShapeDtypeStruct(running.shape, BF16),
        input_output_aliases={1: 0},
        compiler_params=pltpu.CompilerParams(vmem_limit_bytes=VMEM_BYTES),
        cost_estimate=work(part.size * 4, 6 * part.size),
    )(part, running)


def listed_plan(
    source_cells,
    recv_src,
    recv_cell,
    recv_weight,
    enc_w1,
    enc_b1,
    enc_w2,
    enc_b2,
    mix_weight,
    fwd_table,
    inv_table,
):
    lon_count = lax.axis_size("lon")
    lat_count = lax.axis_size("lat")
    channels = source_cells.shape[0]
    slot_count = recv_src.shape[0] // lon_count
    lat_total = fwd_table.shape[2]
    lat_dev = lat_total // lat_count
    lon_dev = NLON // lon_count
    cells_dev = lat_dev * lon_dev
    width = enc_w1.shape[0]
    ord_dev = fwd_table.shape[0]
    halves = width // LANES
    quarters = lon_count // halves
    part_lats = lat_dev // quarters

    source_all = jnp.broadcast_to(source_cells[None], (lon_count,) + source_cells.shape)
    source_all = lax.all_to_all(source_all, "lon", split_axis=0, concat_axis=0, tiled=True)
    listed = regrid_listed(
        source_all, recv_src, recv_cell, recv_weight, lat_dev, lon_dev, slot_count
    )
    band = lax.all_gather(listed, "lon", axis=0, tiled=False)
    pad_points = -(-lon_dev // TILE) * TILE
    at = jnp.arange(lon_count, dtype=jnp.int32)[:, None] * lon_dev + jnp.arange(
        pad_points, dtype=jnp.int32
    )
    inside = (jnp.arange(pad_points) < lon_dev)[None, :, None]
    listing = jnp.arange(ORDERS, dtype=jnp.int32).reshape(-1, ord_dev // ORDER_GROUP, ORDER_GROUP)
    basis_out = basis_by_point(listing.transpose(1, 0, 2).reshape(-1), at)
    basis_out = jnp.where(inside, basis_out, 0)
    band, basis_out = lax.optimization_barrier((band, basis_out))
    coded = band[:, channels + 2 : channels + 4, : lat_dev + 1].astype(jnp.int32)
    starts = coded[:, 0] * 128 + coded[:, 1]

    mine = lax.axis_index("lon")
    sets = ord_dev // ORDER_GROUP
    owned = (
        (jnp.arange(lat_count, dtype=jnp.int32)[:, None] * lon_count + mine) * ord_dev
        + jnp.arange(ord_dev, dtype=jnp.int32)[None, :]
    ).reshape(-1)
    point_rows = -(-lon_dev // LANES) * LANES
    at = jnp.arange(lon_count, dtype=jnp.int32)[:, None] * lon_dev + jnp.arange(
        point_rows, dtype=jnp.int32
    )
    inside = (jnp.arange(point_rows) < lon_dev)[None, :, None]
    basis_in = jnp.where(inside, basis_by_point(owned, at), 0)
    sums = jnp.sum(basis_in.astype(F32), axis=(0, 1))[:, None]
    w1 = jnp.zeros((band.shape[1], width), BF16).at[:channels].set(enc_w1.T)
    first, second = zonal_transform(
        band,
        starts,
        w1,
        enc_b1[None, :],
        enc_w2.T,
        enc_b2[None, :],
        basis_in,
        sums,
        lat_dev,
        lat_count,
        sets,
        channels,
    )

    run = quarters * LATS
    whole_groups = lat_dev // run
    rest = (lat_dev - whole_groups * run) // quarters
    lat = np.arange(lat_dev)
    tail = lat - whole_groups * run
    to_part = np.where(tail < 0, lat % run // LATS, tail // max(rest, 1))
    to_row = np.where(tail < 0, lat // run * LATS + lat % LATS, whole_groups * LATS + tail % max(rest, 1))
    place = (np.arange(lat_count)[:, None] * quarters + to_part) * 64 + to_row
    place = jnp.asarray(place.reshape(-1), jnp.int32)

    mix_t = mixing_matrix(mix_weight).T
    fwd_by_lat = fwd_table.transpose(0, 2, 1)
    def exchange(piece):
        return lax.all_to_all(piece, "lat", split_axis=0, concat_axis=0, tiled=True)

    early = exchange(first)
    modes, waiting = [], []
    for g in range(sets):
        piece = second[g]
        if waiting:
            piece, waiting[-1] = lax.optimization_barrier((piece, waiting[-1]))
        else:
            piece, early = lax.optimization_barrier((piece, early))
        waiting.append(exchange(piece))
    for g in range(sets):
        made = order_steps(
            place,
            [early, waiting[g]],
            [g * 2 * ORDER_GROUP, 0],
            fwd_by_lat,
            inv_table,
            mix_t,
            g * ORDER_GROUP,
            lat_count * quarters,
            halves,
        )
        made = made.reshape(lat_count * lon_count, part_lats, 2 * ORDER_GROUP, LANES)
        if g + 1 < sets:
            made, waiting[g + 1] = lax.optimization_barrier((made, waiting[g + 1]))
        modes.append(
            lax.all_to_all(made, ("lat", "lon"), split_axis=0, concat_axis=0, tiled=True)
        )

    piece = source_all.transpose(1, 0, 2).reshape(channels, -1)
    regridded = regrid_all(
        piece,
        recv_src.reshape(lon_count, slot_count),
        recv_cell.reshape(lon_count, slot_count),
        recv_weight.reshape(lon_count, slot_count),
        cells_dev,
    )
    modes[-1], regridded = lax.optimization_barrier((modes[-1], regridded))
    running = encoder_by_cell(regridded, enc_w1, enc_b1, enc_w2, enc_b2)
    cuts = [0] + [c * LATS for c in CHUNK_CUTS if c * LATS < part_lats] + [part_lats]
    parts = []
    for first, last in zip(cuts[:-1], cuts[1:]):
        parts.append(synthesis_steps(modes, basis_out, lon_dev, LATS, first, last - first))
    if len(parts) > 1:
        parts[1], running = lax.optimization_barrier((parts[1], running))
    for first, last, part in zip(cuts[:-1], cuts[1:], parts):
        count = last - first
        part = lax.all_to_all(part, "lon", split_axis=0, concat_axis=0, tiled=True)
        part = part.reshape(quarters, halves, count * lon_dev, LANES)
        running = finish_steps(part, running, LATS, lon_dev, first // LATS, whole_groups, rest)
    return running.T


def dense_plan(
    source_cells,
    recv_src,
    recv_cell,
    recv_weight,
    enc_w1,
    enc_b1,
    enc_w2,
    enc_b2,
    mix_weight,
    fwd_table,
    inv_table,
):
    lon_count = lax.axis_size("lon")
    lat_count = lax.axis_size("lat")
    slot_count = recv_src.shape[0] // lon_count
    sources = recv_src.reshape(lon_count, slot_count)
    targets = recv_cell.reshape(lon_count, slot_count)
    weights = recv_weight.reshape(lon_count, slot_count)
    lat_total = fwd_table.shape[2]
    lat_dev = lat_total // lat_count
    lon_dev = NLON // lon_count
    cells_dev = lat_dev * lon_dev
    width = enc_w1.shape[0]
    ch_dev = width // lon_count
    orders_total = ORDERS
    ord_dev = fwd_table.shape[0]
    piece = lax.all_gather(source_cells, "lon", axis=1, tiled=True)
    regridded = regrid_all(piece, sources, targets, weights, cells_dev).T
    encoded = dense_encoder(regridded, enc_w1, enc_b1, enc_w2, enc_b2)
    blocked = encoded.reshape(width, lat_dev, 1, lon_dev)
    circles = lax.all_to_all(blocked, "lon", split_axis=0, concat_axis=2, tiled=True).reshape(
        ch_dev * lat_dev, NLON
    )
    natural_order = jnp.arange(orders_total, dtype=jnp.int32)
    dft_basis = build_basis(natural_order, NLON)
    spectra = lax.dot_general(
        dft_basis, circles, (((1,), (1,)), ((), ())), preferred_element_type=jnp.float32
    )
    spectra = spectra.astype(jnp.bfloat16).reshape(orders_total, 2, ch_dev, lat_dev)
    by_order = lax.all_to_all(
        lax.all_to_all(spectra, "lat", split_axis=0, concat_axis=3, tiled=True),
        "lon",
        split_axis=0,
        concat_axis=2,
        tiled=True,
    )
    by_order = by_order.reshape(ord_dev, 2 * width, lat_total)
    coeffs = jnp.einsum(
        "mrt,mlt->mrl", by_order, fwd_table, preferred_element_type=jnp.float32
    ).astype(jnp.bfloat16)
    mix_block = mixing_matrix(mix_weight)
    mixed = jnp.einsum("gr,mrl->mgl", mix_block, coeffs, preferred_element_type=jnp.float32).astype(
        jnp.bfloat16
    )
    synth_in = jnp.einsum(
        "mrl,mtl->mrt", mixed, inv_table, preferred_element_type=jnp.float32
    ).astype(jnp.bfloat16)
    synth_in = synth_in.reshape(ord_dev, 2, width, lat_total)
    returned_modes = lax.all_to_all(
        lax.all_to_all(synth_in, "lon", split_axis=2, concat_axis=0, tiled=True),
        "lat",
        split_axis=3,
        concat_axis=0,
        tiled=True,
    )
    returned_modes = returned_modes.reshape(2 * orders_total, ch_dev * lat_dev)
    synthesis = lax.dot_general(
        returned_modes, dft_basis, (((0,), (0,)), ((), ())), preferred_element_type=jnp.float32
    )
    synthesis = synthesis.astype(jnp.bfloat16).reshape(ch_dev, lat_dev, lon_count, lon_dev)
    regained = lax.all_to_all(synthesis, "lon", split_axis=2, concat_axis=0, tiled=True).reshape(
        width, cells_dev
    )
    return (encoded.astype(jnp.float32) + regained.astype(jnp.float32)).astype(jnp.bfloat16)


def solution(mesh):
    in_specs = (
        P(None, ("lat", "lon")),
        P(("lat", "lon")),
        P(("lat", "lon")),
        P(("lat", "lon")),
        P(),
        P(),
        P(),
        P(),
        P(),
        P(("lat", "lon"), None, None),
        P(("lat", "lon"), None, None),
    )
    out_specs = P(None, ("lat", "lon"))
    lon_count = mesh.shape["lon"]
    lat_count = mesh.shape["lat"]

    def on_device(*arrays):
        slots = arrays[1].shape[0]
        width = arrays[4].shape[0]
        ord_dev, _, lat_total = arrays[9].shape
        lat_dev = lat_total // lat_count
        cells_dev = lat_dev * (NLON // lon_count)
        halves = max(1, width // LANES)
        fits = (
            slots * 4 <= cells_dev
            and width % LANES == 0
            and lon_count % halves == 0
            and lat_dev % (lon_count // halves) == 0
            and lat_dev % 45 == 0
            and 4 * (NLON // lon_count) % TILE == 0
            and lat_dev // (lon_count // halves) < 64
            and ord_dev % ORDER_GROUP == 0
            and lat_total % TILE == 0
        )
        return listed_plan(*arrays) if fits else dense_plan(*arrays)

    return jax.shard_map(
        on_device, mesh=mesh, in_specs=in_specs, out_specs=out_specs, check_vma=False
    )
```

```python
import functools
import math

import jax
import jax.numpy as jnp
import numpy as np
from jax import lax
from jax.experimental import pallas as pl
from jax.experimental.pallas import tpu as pltpu
from jax.sharding import PartitionSpec as P

NLON = 1440
ORDERS = 512
LANES = 128
TILE = 16
WINDOW = 48
UNROLL = 5
LATS = 8
CHUNK_CUTS = (1, 4)
ORDER_GROUP = 8
VMEM_BYTES = 60 * 1024 * 1024

F32 = jnp.float32
BF16 = jnp.bfloat16


def work(flops, bytes_moved):
    return pl.CostEstimate(flops=flops, bytes_accessed=bytes_moved, transcendentals=0)


def build_basis(order_list, points_total):
    points = jnp.arange(points_total, dtype=jnp.int32)
    angles = (order_list[:, None] * points[None, :] % points_total).astype(jnp.float32) * (
        2.0 * math.pi / points_total
    )
    factor = math.sqrt(2.0 / points_total)
    stacked = jnp.stack([factor * jnp.cos(angles), -factor * jnp.sin(angles)], axis=1)
    return stacked.astype(jnp.bfloat16).reshape(2 * order_list.shape[0], points_total)


def basis_by_point(order_list, points):
    shape = points.shape + order_list.shape
    angles = (points[..., None] * order_list % NLON).astype(F32) * (2.0 * math.pi / NLON)
    factor = math.sqrt(2.0 / NLON)
    stacked = jnp.stack([factor * jnp.cos(angles), -factor * jnp.sin(angles)], axis=-1)
    return stacked.astype(BF16).reshape(shape[:-1] + (2 * shape[-1],))


def spread(running, values, weights, targets):
    channels = values.shape[-1]
    contrib = values.astype(jnp.float32) * weights[:, :, None]
    return running.at[targets.reshape(-1)].add(contrib.reshape(-1, channels))


def mixing_matrix(mix_weight):
    real_part = mix_weight[0]
    imag_part = mix_weight[1]
    return jnp.concatenate(
        [
            jnp.concatenate([real_part, -imag_part], axis=1),
            jnp.concatenate([imag_part, real_part], axis=1),
        ],
        axis=0,
    )


def regrid_all(piece, sources, targets, weights, cells_dev):
    shard_count, slot_count = sources.shape
    channels = piece.shape[0]
    src_rows = piece.shape[1] // shard_count
    piece_rows = piece.T
    offsets = jnp.arange(shard_count, dtype=jnp.int32)[:, None] * src_rows
    picked = jnp.take(piece_rows, (offsets + sources).reshape(-1), axis=0)
    picked = picked.reshape(shard_count, slot_count, channels)
    empty = jnp.zeros((cells_dev, channels), jnp.float32)
    return spread(empty, picked, weights, targets).astype(jnp.bfloat16)


def dense_encoder(regridded, enc_w1, enc_b1, enc_w2, enc_b2):
    hidden = jnp.dot(enc_w1, regridded, preferred_element_type=jnp.float32) + enc_b1[:, None]
    hidden = jax.nn.gelu(hidden, approximate=False).astype(jnp.bfloat16)
    return (
        jnp.dot(enc_w2, hidden, preferred_element_type=jnp.float32) + enc_b2[:, None]
    ).astype(jnp.bfloat16)


def encoder_by_cell(regridded, enc_w1, enc_b1, enc_w2, enc_b2):
    hidden = jnp.dot(regridded, enc_w1.T, preferred_element_type=F32) + enc_b1
    hidden = jax.nn.gelu(hidden, approximate=False).astype(BF16)
    return (jnp.dot(hidden, enc_w2.T, preferred_element_type=F32) + enc_b2).astype(BF16)


def regrid_kernel(live, src_ref, cols_ref, row_ref, out_ref, contrib, *, channels, shards, slots, src_rows):
    step = pl.program_id(0)
    height, rows = out_ref.shape

    @pl.when(step == 0)
    def _():
        contrib[...] = jnp.zeros_like(contrib)
        lane = lax.broadcasted_iota(jnp.int32, (slots, src_rows), 1).astype(F32)

        def one(j, carry):
            at = pl.ds(pl.multiple_of(j * slots, slots), slots)
            index = cols_ref[at, 0:1]
            weight = cols_ref[at, 1:2]
            hot = (index == lane).astype(BF16)
            picked = lax.dot_general(
                hot, src_ref[j], (((1,), (1,)), ((), ())), preferred_element_type=F32
            )
            value = picked * weight
            upper = value.astype(BF16)
            lower = (value - upper.astype(F32)).astype(BF16)
            contrib[at, 0:channels] = upper
            contrib[at, LANES : LANES + channels] = lower
            return carry

        lax.fori_loop(0, shards, one, 0)

    here = pl.ds(pl.multiple_of(step * rows, rows), rows)
    used = jnp.logical_or(step == 0, step * rows < live[0])

    @pl.when(used)
    def _():
        cell = cols_ref[here, 2:3]
        total = jnp.zeros((rows, 2 * LANES), F32)
        for s in range(shards):
            same = (cell == row_ref[:, s * slots : (s + 1) * slots]).astype(BF16)
            total += jnp.dot(
                same, contrib[s * slots : (s + 1) * slots, :], preferred_element_type=F32
            )
        merged = total[:, :LANES] + total[:, LANES:]
        lane = lax.broadcasted_iota(jnp.int32, (rows, LANES), 1)
        for place in range(4):
            merged = jnp.where(
                lane == channels + place, cols_ref[here, 3 + place : 4 + place], merged
            )
        out_ref[...] = merged.T[:height].astype(BF16)

    @pl.when(jnp.logical_not(used))
    def _():
        out_ref[...] = jnp.zeros_like(out_ref)


def regrid_listed(source_all, recv_src, recv_cell, recv_weight, lat_dev, lon_dev, slot_count):
    shards, channels, src_rows = source_all.shape
    total = recv_src.shape[0]
    keys = jnp.where(recv_weight != 0, recv_cell, lat_dev * lon_dev)
    ordered = jnp.sort(keys)
    lead = jnp.concatenate([jnp.ones((1,), jnp.bool_), ordered[1:] != ordered[:-1]])
    limits = jnp.arange(lat_dev + 1, dtype=jnp.int32) * lon_dev
    starts = jnp.sum((keys[None, :] < limits[:, None]).astype(jnp.int32), axis=1)
    live = starts[lat_dev:]
    starts = jnp.zeros((total,), jnp.int32).at[: lat_dev + 1].set(starts)
    cols = jnp.stack(
        [
            recv_src.astype(F32),
            recv_weight,
            ordered.astype(F32),
            (ordered % lon_dev).astype(F32),
            lead.astype(F32),
            (starts // 128).astype(F32),
            (starts % 128).astype(F32),
            jnp.zeros((total,), F32),
        ],
        axis=1,
    )
    rows = min(512, total)
    height = -(-(channels + 4) // TILE) * TILE
    return pl.pallas_call(
        functools.partial(
            regrid_kernel, channels=channels, shards=shards, slots=slot_count, src_rows=src_rows
        ),
        grid_spec=pltpu.PrefetchScalarGridSpec(
            num_scalar_prefetch=1,
            grid=(total // rows,),
            in_specs=[
                pl.BlockSpec((shards, channels, src_rows), lambda i, n: (0, 0, 0)),
                pl.BlockSpec((total, 8), lambda i, n: (0, 0)),
                pl.BlockSpec((1, total), lambda i, n: (0, 0)),
            ],
            out_specs=pl.BlockSpec((height, rows), lambda i, n: (0, i)),
            scratch_shapes=[pltpu.VMEM((total, 2 * LANES), BF16)],
        ),
        out_shape=jax.ShapeDtypeStruct((height, total), BF16),
        compiler_params=pltpu.CompilerParams(vmem_limit_bytes=VMEM_BYTES),
        cost_estimate=work(4 * total * total * LANES, 2 * total * LANES),
    )(live, source_all, cols, keys.astype(F32)[None, :])


def transform_latitudes(starts, hots, delta, base, out_refs, first_lat, blocks):
    step = pl.program_id(0)
    groups, lats, _, _ = out_refs[0].shape
    columns = hots.shape[1]
    block_rows = (hots.shape[0] - WINDOW) // blocks
    place = lax.broadcasted_iota(jnp.int32, (WINDOW, columns), 0)

    def bounds(t):
        lows = [starts[k, t] + k * block_rows for k in range(blocks)]
        highs = [starts[k, t + 1] + k * block_rows for k in range(blocks)]
        firsts = [(low // TILE) * TILE for low in lows]
        most = jnp.int32(1)
        for k in range(blocks):
            most = jnp.maximum(most, (highs[k] - firsts[k] + WINDOW - 1) // WINDOW)
        return lows, highs, firsts, most

    def window(lows, highs, firsts):
        left, right = [], []
        for k in range(blocks):
            first = pl.multiple_of(firsts[k], TILE)
            at = pl.ds(first, WINDOW)
            inside = (place >= lows[k] - first) & (place < highs[k] - first)
            left.append(jnp.where(inside, hots[at, :].astype(F32), 0.0).astype(BF16))
            right.append(delta[at, :])
        return lax.dot_general(
            jnp.concatenate(left, axis=0),
            jnp.concatenate(right, axis=0),
            (((0,), (0,)), ((), ())),
            preferred_element_type=F32,
        )

    def store(tt, result):
        result = result.astype(BF16)
        low = 0
        for g in range(groups):
            for out_ref in out_refs:
                height = out_ref.shape[2]
                out_ref[g, tt] = result[low : low + height, :]
                low += height

    def several(b, carry):
        chosen = [b * UNROLL + u for u in range(UNROLL)]
        limits = [bounds(first_lat + step * lats + tt) for tt in chosen]
        most = limits[0][3]
        for limit in limits[1:]:
            most = jnp.maximum(most, limit[3])

        @pl.when(most == 1)
        def _():
            for tt, (lows, highs, firsts, _) in zip(chosen, limits):
                store(tt, base[...] + window(lows, highs, firsts))

        @pl.when(most > 1)
        def _():
            for tt, (lows, highs, firsts, count) in zip(chosen, limits):

                def more(j, running):
                    moved = [
                        jnp.minimum(firsts[k] + j * WINDOW, (highs[k] + TILE - 1) // TILE * TILE)
                        for k in range(blocks)
                    ]
                    return running + window(lows, highs, moved)

                store(tt, lax.fori_loop(0, count, more, base[...]))

        return carry

    lax.fori_loop(0, lats // UNROLL, several, 0)


def zonal_first_kernel(
    starts,
    rows_ref,
    w1_ref,
    b1_ref,
    w2_ref,
    b2_ref,
    basis_ref,
    sums_ref,
    *rest,
    channels,
    blocks,
    block_rows,
    lat_dev,
):
    *out_refs, delta_out, hots_out, base, delta, hots, sems = rest
    step = pl.program_id(0)
    total = blocks * block_rows
    width = delta.shape[1]
    columns = hots.shape[1]
    chunk = min(512, block_rows)
    copies = [
        pltpu.make_async_copy(delta, delta_out, sems.at[0]),
        pltpu.make_async_copy(hots, hots_out, sems.at[1]),
    ]

    def encode(values):
        hidden = jnp.dot(values, w1_ref[...], preferred_element_type=F32) + b1_ref[...]
        hidden = 0.5 * hidden * (1.0 + lax.erf(hidden * math.sqrt(0.5)))
        encoded = jnp.dot(hidden.astype(BF16), w2_ref[...], preferred_element_type=F32)
        return (encoded + b2_ref[...]).astype(BF16).astype(F32)

    @pl.when(step == 0)
    def _():
        empty = encode(jnp.zeros((TILE, rows_ref.shape[1]), BF16))[0:1]
        base[...] = sums_ref[...] * empty
        delta[pl.ds(total, WINDOW), :] = jnp.zeros((WINDOW, width), BF16)
        hots[pl.ds(total, WINDOW), :] = jnp.zeros((WINDOW, columns), BF16)
        points = basis_ref.shape[1]
        lane = lax.broadcasted_iota(jnp.int32, (chunk, points), 1).astype(F32)
        per_block = block_rows // chunk

        def one_block(k, carry):
            used = starts[k, lat_dev] + TILE + WINDOW
            count = jnp.minimum((used + chunk - 1) // chunk, per_block)

            def one(j, inner):
                at = pl.ds(pl.multiple_of(k * block_rows + j * chunk, chunk), chunk)
                part = pl.ds(pl.multiple_of(j * chunk, chunk), chunk)
                values = rows_ref[k, :, part].astype(F32).T
                delta[at, :] = (encode(values.astype(BF16)) - empty).astype(BF16)
                point = values[:, channels : channels + 1]
                lead = values[:, channels + 1 : channels + 2]
                point = jnp.where(lead > 0.5, point, -1.0)
                hot = (point == lane).astype(BF16)
                hots[at, :] = jnp.dot(hot, basis_ref[k], preferred_element_type=F32).astype(BF16)
                return inner

            return lax.fori_loop(0, count, one, carry)

        lax.fori_loop(0, blocks, one_block, 0)
        for copy in copies:
            copy.start()

    transform_latitudes(starts, hots, delta, base, out_refs, 0, blocks)

    @pl.when(step == pl.num_programs(0) - 1)
    def _():
        for copy in copies:
            copy.wait()


def zonal_second_kernel(starts, delta, hots, base, *out_refs, first_lat, blocks):
    transform_latitudes(starts, hots, delta, base, out_refs, first_lat, blocks)


def whole_block(shape):
    return pl.BlockSpec(shape, lambda i, *_: (0,) * len(shape), pipeline_mode=pl.Buffered(1))


def zonal_outputs(groups, lat_count, heights, lats, width):
    shapes = [jax.ShapeDtypeStruct((groups, lat_count, h, width), BF16) for h in heights]
    specs = [pl.BlockSpec((groups, lats, h, width), lambda i, *_: (0, i, 0, 0)) for h in heights]
    return shapes, specs


def zonal_transform(rows, starts, w1, b1, w2, b2, basis, sums, lat_dev, groups, sets, channels):
    blocks, _, block_rows = rows.shape
    width = w2.shape[1]
    columns = basis.shape[2]
    height = columns // groups
    total = blocks * block_rows
    lats = 15
    early = lat_dev // 3 // lats * lats
    late = lat_dev - early
    flops = 25 * total * width * 2 * columns
    shapes, specs = zonal_outputs(groups, early, [height], lats, width)
    kept = [
        jax.ShapeDtypeStruct((total + WINDOW, width), BF16),
        jax.ShapeDtypeStruct((total + WINDOW, columns), BF16),
        jax.ShapeDtypeStruct((columns, width), F32),
    ]
    inputs = (rows, w1, b1, w2, b2, basis, sums)
    first, delta, hots, base = pl.pallas_call(
        functools.partial(
            zonal_first_kernel,
            channels=channels,
            blocks=blocks,
            block_rows=block_rows,
            lat_dev=lat_dev,
        ),
        grid_spec=pltpu.PrefetchScalarGridSpec(
            num_scalar_prefetch=1,
            grid=(early // lats,),
            in_specs=[whole_block(a.shape) for a in inputs],
            out_specs=specs
            + [pl.BlockSpec(memory_space=pl.ANY)] * 2
            + [whole_block((columns, width))],
            scratch_shapes=[
                pltpu.VMEM((total + WINDOW, width), BF16),
                pltpu.VMEM((total + WINDOW, columns), BF16),
                pltpu.SemaphoreType.DMA((2,)),
            ],
        ),
        out_shape=shapes + kept,
        compiler_params=pltpu.CompilerParams(vmem_limit_bytes=VMEM_BYTES),
        cost_estimate=work(flops, 4 * total * width),
    )(starts, *inputs)
    shapes, specs = zonal_outputs(groups, late, [height // sets] * sets, lats, width)
    second = pl.pallas_call(
        functools.partial(zonal_second_kernel, first_lat=early, blocks=blocks),
        grid_spec=pltpu.PrefetchScalarGridSpec(
            num_scalar_prefetch=1,
            grid=(late // lats,),
            in_specs=[whole_block(a.shape) for a in (delta, hots, base)],
            out_specs=specs,
        ),
        out_shape=shapes,
        compiler_params=pltpu.CompilerParams(vmem_limit_bytes=VMEM_BYTES),
        cost_estimate=work(flops, 4 * total * width),
    )(starts, delta, hots, base)
    return first, second


def orders_kernel(place, *refs, group, pieces, rows):
    spec_refs = refs[:pieces]
    fwd_ref, inv_ref, mix_ref, swap_ref, out_ref, arrived, taken, made, sems = refs[pieces:]
    order = pl.program_id(0)
    lat_total, _, width = arrived.shape
    halves, lanes = out_ref.shape[1], out_ref.shape[4]
    side = 2 * group
    count = spec_refs[0].shape[0]

    @pl.when(order == 0)
    def _():
        copies = []
        for i in range(count):
            low = i * lat_total // count
            for ref, row in zip(spec_refs, rows):
                lats = ref.shape[1]
                copies.append(
                    pltpu.make_async_copy(
                        ref.at[i, :, pl.ds(row, side)],
                        arrived.at[pl.ds(low, lats)],
                        sems.at[len(copies)],
                    )
                )
                low += lats
        for copy in copies:
            copy.start()
        for copy in copies:
            copy.wait()

        def one(j, carry):
            at = pl.ds(pl.multiple_of(j * side, side), side)
            block = arrived[at].reshape(side * side, width)
            turned = jnp.dot(swap_ref[...], block, preferred_element_type=F32).astype(BF16)
            taken[:, at, :] = turned.reshape(side, side, width)
            return carry

        lax.fori_loop(0, lat_total // side, one, 0, unroll=5)

    spectrum = jnp.concatenate([taken[2 * order], taken[2 * order + 1]], axis=1)
    coeffs = lax.dot_general(
        fwd_ref[0], spectrum, (((0,), (0,)), ((), ())), preferred_element_type=F32
    ).astype(BF16)
    mixed = jnp.dot(coeffs, mix_ref[...], preferred_element_type=F32).astype(BF16)
    made[order] = jnp.dot(inv_ref[0], mixed, preferred_element_type=F32).astype(BF16)

    @pl.when(order == group - 1)
    def _():
        def one(j, carry):
            first = pl.multiple_of(j * side, side)
            at = pl.ds(first, side)
            columns = []
            for h in range(halves):
                pieces = []
                for r in range(group):
                    for c in range(2):
                        low = (c * halves + h) * lanes
                        pieces.append(made[r, at, low : low + lanes])
                columns.append(jnp.concatenate(pieces, axis=0))
            block = jnp.concatenate(columns, axis=1)
            turned = jnp.dot(swap_ref[...], block, preferred_element_type=F32).astype(BF16)
            for i in range(side):
                spot = place[first + i]
                for h in range(halves):
                    out_ref[spot // 64, h, spot % 64] = turned[
                        i * side : (i + 1) * side, h * lanes : (h + 1) * lanes
                    ]
            return carry

        lax.fori_loop(0, lat_total // side, one, 0, unroll=5)


def order_steps(place, spectra, rows, fwd_table, inv_table, mix_t, first, parts, halves):
    pieces = len(spectra)
    count, width = spectra[0].shape[0], spectra[0].shape[3]
    side = 2 * ORDER_GROUP
    lat_total = fwd_table.shape[1]
    degrees = fwd_table.shape[2]
    group = side // 2
    index = jnp.arange(side * side, dtype=jnp.int32)
    swapped = (index % side) * side + index // side
    swap = (swapped[:, None] == index[None, :]).astype(BF16)
    both = 2 * width
    part_lats = lat_total // parts
    out_shape = (parts, halves, part_lats, side, width // halves)
    return pl.pallas_call(
        functools.partial(orders_kernel, group=group, pieces=pieces, rows=rows),
        grid_spec=pltpu.PrefetchScalarGridSpec(
            num_scalar_prefetch=1,
            grid=(group,),
            in_specs=[pl.BlockSpec(memory_space=pl.ANY)] * pieces
            + [
                pl.BlockSpec((1, lat_total, degrees), lambda r, s: (first + r, 0, 0)),
                pl.BlockSpec((1, lat_total, degrees), lambda r, s: (first + r, 0, 0)),
                pl.BlockSpec((both, both), lambda r, s: (0, 0)),
                pl.BlockSpec((side * side, side * side), lambda r, s: (0, 0)),
            ],
            out_specs=pl.BlockSpec(out_shape, lambda r, s: (0, 0, 0, 0, 0)),
            scratch_shapes=[
                pltpu.VMEM((lat_total, side, width), BF16),
                pltpu.VMEM((side, lat_total, width), BF16),
                pltpu.VMEM((group, lat_total, both), BF16),
                pltpu.SemaphoreType.DMA((pieces * count,)),
            ],
        ),
        out_shape=jax.ShapeDtypeStruct(out_shape, BF16),
        compiler_params=pltpu.CompilerParams(vmem_limit_bytes=VMEM_BYTES),
        cost_estimate=work(
            group * 2 * both * degrees * (2 * lat_total + both), 8 * group * degrees * lat_total
        ),
    )(place, *spectra, fwd_table, inv_table, mix_t, swap)


def synthesis_kernel(*refs):
    *mode_refs, basis_ref, out_ref = refs
    sources, _, height, lanes = mode_refs[0].shape
    blocks = out_ref.shape[0]
    lats = mode_refs[0].shape[1]
    points = out_ref.shape[1] // lats
    right = jnp.concatenate(
        [
            jnp.concatenate(
                [ref[:, t].reshape(sources * height, lanes) for ref in mode_refs], axis=0
            )
            for t in range(lats)
        ],
        axis=1,
    )

    def one(k, carry):
        value = jnp.dot(basis_ref[k], right, preferred_element_type=F32)
        span = 4 * points
        for t in range(0, lats, 4):
            rows = [value[:points, (t + i) * lanes : (t + i + 1) * lanes] for i in range(4)]
            low = t * points
            out_ref[k, low : low + span, :] = jnp.concatenate(rows, axis=0).astype(BF16)
        return carry

    lax.fori_loop(0, blocks, one, 0)


def synthesis_steps(modes, basis, points, lats, first, count):
    sources, _, height, lanes = modes[0].shape
    blocks = basis.shape[0]
    offset = first // lats
    return pl.pallas_call(
        synthesis_kernel,
        grid=(-(-count // lats),),
        in_specs=[
            pl.BlockSpec((sources, lats, height, lanes), lambda i: (0, i + offset, 0, 0))
            for _ in modes
        ]
        + [pl.BlockSpec(basis.shape, lambda i: (0, 0, 0))],
        out_specs=pl.BlockSpec((blocks, lats * points, lanes), lambda i: (0, i, 0)),
        out_shape=jax.ShapeDtypeStruct((blocks, count * points, lanes), BF16),
        compiler_params=pltpu.CompilerParams(vmem_limit_bytes=VMEM_BYTES),
        cost_estimate=work(2 * count * lanes * basis.size, 4 * blocks * count * points * lanes),
    )(*modes, basis)


def finish_kernel(part_ref, enc_ref, out_ref, *, first, whole_groups, rest_rows):
    quarters, halves, rows, lanes = part_ref.shape
    group = pl.program_id(0) + first

    @pl.when(group < whole_groups)
    def _():
        for q in range(quarters):
            at = pl.ds(q * rows, rows)
            for h in range(halves):
                across = pl.ds(h * lanes, lanes)
                total = enc_ref[at, across].astype(F32) + part_ref[q, h].astype(F32)
                out_ref[at, across] = total.astype(BF16)

    @pl.when(group >= whole_groups)
    def _():
        count = quarters * rest_rows
        for h in range(halves):
            across = pl.ds(h * lanes, lanes)
            pieces = [part_ref[q, h].astype(F32)[:rest_rows] for q in range(quarters)]
            total = enc_ref[:count, across].astype(F32) + jnp.concatenate(pieces, axis=0)
            out_ref[:count, across] = total.astype(BF16)


def finish_steps(part, running, lats, points, first, whole_groups, rest):
    quarters, halves, count, lanes = part.shape
    rows = lats * points
    return pl.pallas_call(
        functools.partial(
            finish_kernel, first=first, whole_groups=whole_groups, rest_rows=rest * points
        ),
        grid=(-(-count // rows),),
        in_specs=[
            pl.BlockSpec((quarters, halves, rows, lanes), lambda i: (0, 0, i, 0)),
            pl.BlockSpec((quarters * rows, halves * lanes), lambda i: (i + first, 0)),
        ],
        out_specs=pl.BlockSpec((quarters * rows, halves * lanes), lambda i: (i + first, 0)),
        out_shape=jax.ShapeDtypeStruct(running.shape, BF16),
        input_output_aliases={1: 0},
        compiler_params=pltpu.CompilerParams(vmem_limit_bytes=VMEM_BYTES),
        cost_estimate=work(part.size * 4, 6 * part.size),
    )(part, running)


def listed_plan(
    source_cells,
    recv_src,
    recv_cell,
    recv_weight,
    enc_w1,
    enc_b1,
    enc_w2,
    enc_b2,
    mix_weight,
    fwd_table,
    inv_table,
):
    lon_count = lax.axis_size("lon")
    lat_count = lax.axis_size("lat")
    channels = source_cells.shape[0]
    slot_count = recv_src.shape[0] // lon_count
    lat_total = fwd_table.shape[2]
    lat_dev = lat_total // lat_count
    lon_dev = NLON // lon_count
    cells_dev = lat_dev * lon_dev
    width = enc_w1.shape[0]
    ord_dev = fwd_table.shape[0]
    halves = width // LANES
    quarters = lon_count // halves
    part_lats = lat_dev // quarters

    source_all = jnp.broadcast_to(source_cells[None], (lon_count,) + source_cells.shape)
    source_all = lax.all_to_all(source_all, "lon", split_axis=0, concat_axis=0, tiled=True)
    listed = regrid_listed(
        source_all, recv_src, recv_cell, recv_weight, lat_dev, lon_dev, slot_count
    )
    band = lax.all_gather(listed, "lon", axis=0, tiled=False)
    pad_points = -(-lon_dev // TILE) * TILE
    at = jnp.arange(lon_count, dtype=jnp.int32)[:, None] * lon_dev + jnp.arange(
        pad_points, dtype=jnp.int32
    )
    inside = (jnp.arange(pad_points) < lon_dev)[None, :, None]
    listing = jnp.arange(ORDERS, dtype=jnp.int32).reshape(-1, ord_dev // ORDER_GROUP, ORDER_GROUP)
    basis_out = basis_by_point(listing.transpose(1, 0, 2).reshape(-1), at)
    basis_out = jnp.where(inside, basis_out, 0)
    coded = band[:, channels + 2 : channels + 4, : lat_dev + 1].astype(jnp.int32)
    starts = coded[:, 0] * 128 + coded[:, 1]
    starts, basis_out = lax.optimization_barrier((starts, basis_out))

    mine = lax.axis_index("lon")
    sets = ord_dev // ORDER_GROUP
    owned = (
        (jnp.arange(lat_count, dtype=jnp.int32)[:, None] * lon_count + mine) * ord_dev
        + jnp.arange(ord_dev, dtype=jnp.int32)[None, :]
    ).reshape(-1)
    point_rows = -(-lon_dev // LANES) * LANES
    at = jnp.arange(lon_count, dtype=jnp.int32)[:, None] * lon_dev + jnp.arange(
        point_rows, dtype=jnp.int32
    )
    inside = (jnp.arange(point_rows) < lon_dev)[None, :, None]
    basis_in = jnp.where(inside, basis_by_point(owned, at), 0)
    sums = jnp.sum(basis_in.astype(F32), axis=(0, 1))[:, None]
    w1 = jnp.zeros((band.shape[1], width), BF16).at[:channels].set(enc_w1.T)
    first, second = zonal_transform(
        band,
        starts,
        w1,
        enc_b1[None, :],
        enc_w2.T,
        enc_b2[None, :],
        basis_in,
        sums,
        lat_dev,
        lat_count,
        sets,
        channels,
    )

    run = quarters * LATS
    whole_groups = lat_dev // run
    rest = (lat_dev - whole_groups * run) // quarters
    lat = np.arange(lat_dev)
    tail = lat - whole_groups * run
    to_part = np.where(tail < 0, lat % run // LATS, tail // max(rest, 1))
    to_row = np.where(tail < 0, lat // run * LATS + lat % LATS, whole_groups * LATS + tail % max(rest, 1))
    place = (np.arange(lat_count)[:, None] * quarters + to_part) * 64 + to_row
    place = jnp.asarray(place.reshape(-1), jnp.int32)

    mix_t = mixing_matrix(mix_weight).T
    fwd_by_lat = fwd_table.transpose(0, 2, 1)
    def exchange(piece):
        return lax.all_to_all(piece, "lat", split_axis=0, concat_axis=0, tiled=True)

    piece = source_all.transpose(1, 0, 2).reshape(channels, -1)
    regridded = regrid_all(
        piece,
        recv_src.reshape(lon_count, slot_count),
        recv_cell.reshape(lon_count, slot_count),
        recv_weight.reshape(lon_count, slot_count),
        cells_dev,
    )
    early = exchange(first)
    modes, waiting = [], []
    for g in range(sets):
        piece = second[g]
        if waiting:
            piece, waiting[-1] = lax.optimization_barrier((piece, waiting[-1]))
        else:
            piece, early = lax.optimization_barrier((piece, early))
        waiting.append(exchange(piece))
    waiting[0], regridded = lax.optimization_barrier((waiting[0], regridded))
    for g in range(sets):
        made = order_steps(
            place,
            [early, waiting[g]],
            [g * 2 * ORDER_GROUP, 0],
            fwd_by_lat,
            inv_table,
            mix_t,
            g * ORDER_GROUP,
            lat_count * quarters,
            halves,
        )
        made = made.reshape(lat_count * lon_count, part_lats, 2 * ORDER_GROUP, LANES)
        if g + 1 < sets:
            made, waiting[g + 1] = lax.optimization_barrier((made, waiting[g + 1]))
        if modes:
            made, modes[-1] = lax.optimization_barrier((made, modes[-1]))
        modes.append(
            lax.all_to_all(made, ("lat", "lon"), split_axis=0, concat_axis=0, tiled=True)
        )

    running = encoder_by_cell(regridded, enc_w1, enc_b1, enc_w2, enc_b2)
    modes[-1], running = lax.optimization_barrier((modes[-1], running))
    cuts = [0] + [c * LATS for c in CHUNK_CUTS if c * LATS < part_lats] + [part_lats]
    parts = []
    for first, last in zip(cuts[:-1], cuts[1:]):
        parts.append(synthesis_steps(modes, basis_out, lon_dev, LATS, first, last - first))
    for first, last, part in zip(cuts[:-1], cuts[1:], parts):
        count = last - first
        part = lax.all_to_all(part, "lon", split_axis=0, concat_axis=0, tiled=True)
        part = part.reshape(quarters, halves, count * lon_dev, LANES)
        running = finish_steps(part, running, LATS, lon_dev, first // LATS, whole_groups, rest)
    return running.T


def dense_plan(
    source_cells,
    recv_src,
    recv_cell,
    recv_weight,
    enc_w1,
    enc_b1,
    enc_w2,
    enc_b2,
    mix_weight,
    fwd_table,
    inv_table,
):
    lon_count = lax.axis_size("lon")
    lat_count = lax.axis_size("lat")
    slot_count = recv_src.shape[0] // lon_count
    sources = recv_src.reshape(lon_count, slot_count)
    targets = recv_cell.reshape(lon_count, slot_count)
    weights = recv_weight.reshape(lon_count, slot_count)
    lat_total = fwd_table.shape[2]
    lat_dev = lat_total // lat_count
    lon_dev = NLON // lon_count
    cells_dev = lat_dev * lon_dev
    width = enc_w1.shape[0]
    ch_dev = width // lon_count
    orders_total = ORDERS
    ord_dev = fwd_table.shape[0]
    piece = lax.all_gather(source_cells, "lon", axis=1, tiled=True)
    regridded = regrid_all(piece, sources, targets, weights, cells_dev).T
    encoded = dense_encoder(regridded, enc_w1, enc_b1, enc_w2, enc_b2)
    blocked = encoded.reshape(width, lat_dev, 1, lon_dev)
    circles = lax.all_to_all(blocked, "lon", split_axis=0, concat_axis=2, tiled=True).reshape(
        ch_dev * lat_dev, NLON
    )
    natural_order = jnp.arange(orders_total, dtype=jnp.int32)
    dft_basis = build_basis(natural_order, NLON)
    spectra = lax.dot_general(
        dft_basis, circles, (((1,), (1,)), ((), ())), preferred_element_type=jnp.float32
    )
    spectra = spectra.astype(jnp.bfloat16).reshape(orders_total, 2, ch_dev, lat_dev)
    by_order = lax.all_to_all(
        lax.all_to_all(spectra, "lat", split_axis=0, concat_axis=3, tiled=True),
        "lon",
        split_axis=0,
        concat_axis=2,
        tiled=True,
    )
    by_order = by_order.reshape(ord_dev, 2 * width, lat_total)
    coeffs = jnp.einsum(
        "mrt,mlt->mrl", by_order, fwd_table, preferred_element_type=jnp.float32
    ).astype(jnp.bfloat16)
    mix_block = mixing_matrix(mix_weight)
    mixed = jnp.einsum("gr,mrl->mgl", mix_block, coeffs, preferred_element_type=jnp.float32).astype(
        jnp.bfloat16
    )
    synth_in = jnp.einsum(
        "mrl,mtl->mrt", mixed, inv_table, preferred_element_type=jnp.float32
    ).astype(jnp.bfloat16)
    synth_in = synth_in.reshape(ord_dev, 2, width, lat_total)
    returned_modes = lax.all_to_all(
        lax.all_to_all(synth_in, "lon", split_axis=2, concat_axis=0, tiled=True),
        "lat",
        split_axis=3,
        concat_axis=0,
        tiled=True,
    )
    returned_modes = returned_modes.reshape(2 * orders_total, ch_dev * lat_dev)
    synthesis = lax.dot_general(
        returned_modes, dft_basis, (((0,), (0,)), ((), ())), preferred_element_type=jnp.float32
    )
    synthesis = synthesis.astype(jnp.bfloat16).reshape(ch_dev, lat_dev, lon_count, lon_dev)
    regained = lax.all_to_all(synthesis, "lon", split_axis=2, concat_axis=0, tiled=True).reshape(
        width, cells_dev
    )
    return (encoded.astype(jnp.float32) + regained.astype(jnp.float32)).astype(jnp.bfloat16)


def solution(mesh):
    in_specs = (
        P(None, ("lat", "lon")),
        P(("lat", "lon")),
        P(("lat", "lon")),
        P(("lat", "lon")),
        P(),
        P(),
        P(),
        P(),
        P(),
        P(("lat", "lon"), None, None),
        P(("lat", "lon"), None, None),
    )
    out_specs = P(None, ("lat", "lon"))
    lon_count = mesh.shape["lon"]
    lat_count = mesh.shape["lat"]

    def on_device(*arrays):
        slots = arrays[1].shape[0]
        width = arrays[4].shape[0]
        ord_dev, _, lat_total = arrays[9].shape
        lat_dev = lat_total // lat_count
        cells_dev = lat_dev * (NLON // lon_count)
        halves = max(1, width // LANES)
        fits = (
            slots * 4 <= cells_dev
            and width % LANES == 0
            and lon_count % halves == 0
            and lat_dev % (lon_count // halves) == 0
            and lat_dev % 45 == 0
            and 4 * (NLON // lon_count) % TILE == 0
            and lat_dev // (lon_count // halves) < 64
            and ord_dev % ORDER_GROUP == 0
            and lat_total % TILE == 0
        )
        return listed_plan(*arrays) if fits else dense_plan(*arrays)

    return jax.shard_map(
        on_device, mesh=mesh, in_specs=in_specs, out_specs=out_specs, check_vma=False
    )
```

```python
import functools
import math

import jax
import jax.numpy as jnp
import numpy as np
from jax import lax
from jax.experimental import pallas as pl
from jax.experimental.pallas import tpu as pltpu
from jax.sharding import PartitionSpec as P

NLON = 1440
ORDERS = 512
LANES = 128
TILE = 16
WINDOW = 48
UNROLL = 5
LATS = 8
CHUNK_CUTS = (1, 4)
ORDER_GROUP = 8
VMEM_BYTES = 60 * 1024 * 1024

F32 = jnp.float32
BF16 = jnp.bfloat16


def work(flops, bytes_moved):
    return pl.CostEstimate(flops=flops, bytes_accessed=bytes_moved, transcendentals=0)


def build_basis(order_list, points_total):
    points = jnp.arange(points_total, dtype=jnp.int32)
    angles = (order_list[:, None] * points[None, :] % points_total).astype(jnp.float32) * (
        2.0 * math.pi / points_total
    )
    factor = math.sqrt(2.0 / points_total)
    stacked = jnp.stack([factor * jnp.cos(angles), -factor * jnp.sin(angles)], axis=1)
    return stacked.astype(jnp.bfloat16).reshape(2 * order_list.shape[0], points_total)


def basis_by_point(order_list, points):
    shape = points.shape + order_list.shape
    angles = (points[..., None] * order_list % NLON).astype(F32) * (2.0 * math.pi / NLON)
    factor = math.sqrt(2.0 / NLON)
    stacked = jnp.stack([factor * jnp.cos(angles), -factor * jnp.sin(angles)], axis=-1)
    return stacked.astype(BF16).reshape(shape[:-1] + (2 * shape[-1],))


def spread(running, values, weights, targets):
    channels = values.shape[-1]
    contrib = values.astype(jnp.float32) * weights[:, :, None]
    return running.at[targets.reshape(-1)].add(contrib.reshape(-1, channels))


def mixing_matrix(mix_weight):
    real_part = mix_weight[0]
    imag_part = mix_weight[1]
    return jnp.concatenate(
        [
            jnp.concatenate([real_part, -imag_part], axis=1),
            jnp.concatenate([imag_part, real_part], axis=1),
        ],
        axis=0,
    )


def regrid_all(piece, sources, targets, weights, cells_dev):
    shard_count, slot_count = sources.shape
    channels = piece.shape[0]
    src_rows = piece.shape[1] // shard_count
    piece_rows = piece.T
    offsets = jnp.arange(shard_count, dtype=jnp.int32)[:, None] * src_rows
    picked = jnp.take(piece_rows, (offsets + sources).reshape(-1), axis=0)
    picked = picked.reshape(shard_count, slot_count, channels)
    empty = jnp.zeros((cells_dev, channels), jnp.float32)
    return spread(empty, picked, weights, targets).astype(jnp.bfloat16)


def dense_encoder(regridded, enc_w1, enc_b1, enc_w2, enc_b2):
    hidden = jnp.dot(enc_w1, regridded, preferred_element_type=jnp.float32) + enc_b1[:, None]
    hidden = jax.nn.gelu(hidden, approximate=False).astype(jnp.bfloat16)
    return (
        jnp.dot(enc_w2, hidden, preferred_element_type=jnp.float32) + enc_b2[:, None]
    ).astype(jnp.bfloat16)


def encoder_by_cell(regridded, enc_w1, enc_b1, enc_w2, enc_b2):
    hidden = jnp.dot(regridded, enc_w1.T, preferred_element_type=F32) + enc_b1
    hidden = jax.nn.gelu(hidden, approximate=False).astype(BF16)
    return (jnp.dot(hidden, enc_w2.T, preferred_element_type=F32) + enc_b2).astype(BF16)


def regrid_kernel(live, src_ref, cols_ref, row_ref, out_ref, contrib, *, channels, shards, slots, src_rows):
    step = pl.program_id(0)
    height, rows = out_ref.shape

    @pl.when(step == 0)
    def _():
        contrib[...] = jnp.zeros_like(contrib)
        lane = lax.broadcasted_iota(jnp.int32, (slots, src_rows), 1).astype(F32)

        def one(j, carry):
            at = pl.ds(pl.multiple_of(j * slots, slots), slots)
            index = cols_ref[at, 0:1]
            weight = cols_ref[at, 1:2]
            hot = (index == lane).astype(BF16)
            picked = lax.dot_general(
                hot, src_ref[j], (((1,), (1,)), ((), ())), preferred_element_type=F32
            )
            value = picked * weight
            upper = value.astype(BF16)
            lower = (value - upper.astype(F32)).astype(BF16)
            contrib[at, 0:channels] = upper
            contrib[at, LANES : LANES + channels] = lower
            return carry

        lax.fori_loop(0, shards, one, 0)

    here = pl.ds(pl.multiple_of(step * rows, rows), rows)
    used = jnp.logical_or(step == 0, step * rows < live[0])

    @pl.when(used)
    def _():
        cell = cols_ref[here, 2:3]
        total = jnp.zeros((rows, 2 * LANES), F32)
        for s in range(shards):
            same = (cell == row_ref[:, s * slots : (s + 1) * slots]).astype(BF16)
            total += jnp.dot(
                same, contrib[s * slots : (s + 1) * slots, :], preferred_element_type=F32
            )
        merged = total[:, :LANES] + total[:, LANES:]
        lane = lax.broadcasted_iota(jnp.int32, (rows, LANES), 1)
        for place in range(4):
            merged = jnp.where(
                lane == channels + place, cols_ref[here, 3 + place : 4 + place], merged
            )
        out_ref[...] = merged.T[:height].astype(BF16)

    @pl.when(jnp.logical_not(used))
    def _():
        out_ref[...] = jnp.zeros_like(out_ref)


def regrid_listed(source_all, recv_src, recv_cell, recv_weight, lat_dev, lon_dev, slot_count):
    shards, channels, src_rows = source_all.shape
    total = recv_src.shape[0]
    keys = jnp.where(recv_weight != 0, recv_cell, lat_dev * lon_dev)
    ordered = jnp.sort(keys)
    lead = jnp.concatenate([jnp.ones((1,), jnp.bool_), ordered[1:] != ordered[:-1]])
    limits = jnp.arange(lat_dev + 1, dtype=jnp.int32) * lon_dev
    starts = jnp.sum((keys[None, :] < limits[:, None]).astype(jnp.int32), axis=1)
    live = starts[lat_dev:]
    starts = jnp.zeros((total,), jnp.int32).at[: lat_dev + 1].set(starts)
    cols = jnp.stack(
        [
            recv_src.astype(F32),
            recv_weight,
            ordered.astype(F32),
            (ordered % lon_dev).astype(F32),
            lead.astype(F32),
            (starts // 128).astype(F32),
            (starts % 128).astype(F32),
            jnp.zeros((total,), F32),
        ],
        axis=1,
    )
    rows = min(512, total)
    height = -(-(channels + 4) // TILE) * TILE
    return pl.pallas_call(
        functools.partial(
            regrid_kernel, channels=channels, shards=shards, slots=slot_count, src_rows=src_rows
        ),
        grid_spec=pltpu.PrefetchScalarGridSpec(
            num_scalar_prefetch=1,
            grid=(total // rows,),
            in_specs=[
                pl.BlockSpec((shards, channels, src_rows), lambda i, n: (0, 0, 0)),
                pl.BlockSpec((total, 8), lambda i, n: (0, 0)),
                pl.BlockSpec((1, total), lambda i, n: (0, 0)),
            ],
            out_specs=pl.BlockSpec((height, rows), lambda i, n: (0, i)),
            scratch_shapes=[pltpu.VMEM((total, 2 * LANES), BF16)],
        ),
        out_shape=jax.ShapeDtypeStruct((height, total), BF16),
        compiler_params=pltpu.CompilerParams(vmem_limit_bytes=VMEM_BYTES),
        cost_estimate=work(4 * total * total * LANES, 2 * total * LANES),
    )(live, source_all, cols, keys.astype(F32)[None, :])


def transform_latitudes(starts, hots, delta, base, out_refs, first_lat, blocks):
    step = pl.program_id(0)
    groups, lats, _, _ = out_refs[0].shape
    columns = hots.shape[1]
    block_rows = (hots.shape[0] - WINDOW) // blocks
    place = lax.broadcasted_iota(jnp.int32, (WINDOW, columns), 0)

    def bounds(t):
        lows = [starts[k, t] + k * block_rows for k in range(blocks)]
        highs = [starts[k, t + 1] + k * block_rows for k in range(blocks)]
        firsts = [(low // TILE) * TILE for low in lows]
        most = jnp.int32(1)
        for k in range(blocks):
            most = jnp.maximum(most, (highs[k] - firsts[k] + WINDOW - 1) // WINDOW)
        return lows, highs, firsts, most

    def window(lows, highs, firsts):
        left, right = [], []
        for k in range(blocks):
            first = pl.multiple_of(firsts[k], TILE)
            at = pl.ds(first, WINDOW)
            inside = (place >= lows[k] - first) & (place < highs[k] - first)
            left.append(jnp.where(inside, hots[at, :].astype(F32), 0.0).astype(BF16))
            right.append(delta[at, :])
        return lax.dot_general(
            jnp.concatenate(left, axis=0),
            jnp.concatenate(right, axis=0),
            (((0,), (0,)), ((), ())),
            preferred_element_type=F32,
        )

    def store(tt, result):
        result = result.astype(BF16)
        low = 0
        for g in range(groups):
            for out_ref in out_refs:
                height = out_ref.shape[2]
                out_ref[g, tt] = result[low : low + height, :]
                low += height

    def several(b, carry):
        chosen = [b * UNROLL + u for u in range(UNROLL)]
        limits = [bounds(first_lat + step * lats + tt) for tt in chosen]
        most = limits[0][3]
        for limit in limits[1:]:
            most = jnp.maximum(most, limit[3])

        @pl.when(most == 1)
        def _():
            for tt, (lows, highs, firsts, _) in zip(chosen, limits):
                store(tt, base[...] + window(lows, highs, firsts))

        @pl.when(most > 1)
        def _():
            for tt, (lows, highs, firsts, count) in zip(chosen, limits):

                def more(j, running):
                    moved = [
                        jnp.minimum(firsts[k] + j * WINDOW, (highs[k] + TILE - 1) // TILE * TILE)
                        for k in range(blocks)
                    ]
                    return running + window(lows, highs, moved)

                store(tt, lax.fori_loop(0, count, more, base[...]))

        return carry

    lax.fori_loop(0, lats // UNROLL, several, 0)


def zonal_first_kernel(
    starts,
    rows_ref,
    w1_ref,
    b1_ref,
    w2_ref,
    b2_ref,
    basis_ref,
    sums_ref,
    *rest,
    channels,
    blocks,
    block_rows,
    lat_dev,
):
    *out_refs, delta_out, hots_out, base, delta, hots, sems = rest
    step = pl.program_id(0)
    total = blocks * block_rows
    width = delta.shape[1]
    columns = hots.shape[1]
    chunk = min(512, block_rows)
    copies = [
        pltpu.make_async_copy(delta, delta_out, sems.at[0]),
        pltpu.make_async_copy(hots, hots_out, sems.at[1]),
    ]

    def encode(values):
        hidden = jnp.dot(values, w1_ref[...], preferred_element_type=F32) + b1_ref[...]
        hidden = 0.5 * hidden * (1.0 + lax.erf(hidden * math.sqrt(0.5)))
        encoded = jnp.dot(hidden.astype(BF16), w2_ref[...], preferred_element_type=F32)
        return (encoded + b2_ref[...]).astype(BF16).astype(F32)

    @pl.when(step == 0)
    def _():
        empty = encode(jnp.zeros((TILE, rows_ref.shape[1]), BF16))[0:1]
        base[...] = sums_ref[...] * empty
        delta[pl.ds(total, WINDOW), :] = jnp.zeros((WINDOW, width), BF16)
        hots[pl.ds(total, WINDOW), :] = jnp.zeros((WINDOW, columns), BF16)
        points = basis_ref.shape[1]
        lane = lax.broadcasted_iota(jnp.int32, (chunk, points), 1).astype(F32)
        per_block = block_rows // chunk

        def one_block(k, carry):
            used = starts[k, lat_dev] + TILE + WINDOW
            count = jnp.minimum((used + chunk - 1) // chunk, per_block)

            def one(j, inner):
                at = pl.ds(pl.multiple_of(k * block_rows + j * chunk, chunk), chunk)
                part = pl.ds(pl.multiple_of(j * chunk, chunk), chunk)
                values = rows_ref[k, :, part].astype(F32).T
                delta[at, :] = (encode(values.astype(BF16)) - empty).astype(BF16)
                point = values[:, channels : channels + 1]
                lead = values[:, channels + 1 : channels + 2]
                point = jnp.where(lead > 0.5, point, -1.0)
                hot = (point == lane).astype(BF16)
                hots[at, :] = jnp.dot(hot, basis_ref[k], preferred_element_type=F32).astype(BF16)
                return inner

            return lax.fori_loop(0, count, one, carry)

        lax.fori_loop(0, blocks, one_block, 0)
        for copy in copies:
            copy.start()

    transform_latitudes(starts, hots, delta, base, out_refs, 0, blocks)

    @pl.when(step == pl.num_programs(0) - 1)
    def _():
        for copy in copies:
            copy.wait()


def zonal_second_kernel(starts, delta, hots, base, *out_refs, first_lat, blocks):
    transform_latitudes(starts, hots, delta, base, out_refs, first_lat, blocks)


def whole_block(shape):
    return pl.BlockSpec(shape, lambda i, *_: (0,) * len(shape), pipeline_mode=pl.Buffered(1))


def zonal_outputs(groups, lat_count, heights, lats, width):
    shapes = [jax.ShapeDtypeStruct((groups, lat_count, h, width), BF16) for h in heights]
    specs = [pl.BlockSpec((groups, lats, h, width), lambda i, *_: (0, i, 0, 0)) for h in heights]
    return shapes, specs


def zonal_transform(rows, starts, w1, b1, w2, b2, basis, sums, lat_dev, groups, sets, channels):
    blocks, _, block_rows = rows.shape
    width = w2.shape[1]
    columns = basis.shape[2]
    height = columns // groups
    total = blocks * block_rows
    lats = 15
    early = lat_dev // 3 // lats * lats
    late = lat_dev - early
    flops = 25 * total * width * 2 * columns
    shapes, specs = zonal_outputs(groups, early, [height], lats, width)
    kept = [
        jax.ShapeDtypeStruct((total + WINDOW, width), BF16),
        jax.ShapeDtypeStruct((total + WINDOW, columns), BF16),
        jax.ShapeDtypeStruct((columns, width), F32),
    ]
    inputs = (rows, w1, b1, w2, b2, basis, sums)
    first, delta, hots, base = pl.pallas_call(
        functools.partial(
            zonal_first_kernel,
            channels=channels,
            blocks=blocks,
            block_rows=block_rows,
            lat_dev=lat_dev,
        ),
        grid_spec=pltpu.PrefetchScalarGridSpec(
            num_scalar_prefetch=1,
            grid=(early // lats,),
            in_specs=[whole_block(a.shape) for a in inputs],
            out_specs=specs
            + [pl.BlockSpec(memory_space=pl.ANY)] * 2
            + [whole_block((columns, width))],
            scratch_shapes=[
                pltpu.VMEM((total + WINDOW, width), BF16),
                pltpu.VMEM((total + WINDOW, columns), BF16),
                pltpu.SemaphoreType.DMA((2,)),
            ],
        ),
        out_shape=shapes + kept,
        compiler_params=pltpu.CompilerParams(vmem_limit_bytes=VMEM_BYTES),
        cost_estimate=work(flops, 4 * total * width),
    )(starts, *inputs)
    shapes, specs = zonal_outputs(groups, late, [height // sets] * sets, lats, width)
    second = pl.pallas_call(
        functools.partial(zonal_second_kernel, first_lat=early, blocks=blocks),
        grid_spec=pltpu.PrefetchScalarGridSpec(
            num_scalar_prefetch=1,
            grid=(late // lats,),
            in_specs=[whole_block(a.shape) for a in (delta, hots, base)],
            out_specs=specs,
        ),
        out_shape=shapes,
        compiler_params=pltpu.CompilerParams(vmem_limit_bytes=VMEM_BYTES),
        cost_estimate=work(flops, 4 * total * width),
    )(starts, delta, hots, base)
    return first, second


def orders_kernel(place, *refs, group, pieces, rows):
    spec_refs = refs[:pieces]
    fwd_ref, inv_ref, mix_ref, swap_ref, out_ref, arrived, taken, made, sems = refs[pieces:]
    order = pl.program_id(0)
    lat_total, _, width = arrived.shape
    halves, lanes = out_ref.shape[1], out_ref.shape[4]
    side = 2 * group
    count = spec_refs[0].shape[0]

    @pl.when(order == 0)
    def _():
        copies = []
        for i in range(count):
            low = i * lat_total // count
            for ref, row in zip(spec_refs, rows):
                lats = ref.shape[1]
                copies.append(
                    pltpu.make_async_copy(
                        ref.at[i, :, pl.ds(row, side)],
                        arrived.at[pl.ds(low, lats)],
                        sems.at[len(copies)],
                    )
                )
                low += lats
        for copy in copies:
            copy.start()
        for copy in copies:
            copy.wait()

        def one(j, carry):
            at = pl.ds(pl.multiple_of(j * side, side), side)
            block = arrived[at].reshape(side * side, width)
            turned = jnp.dot(swap_ref[...], block, preferred_element_type=F32).astype(BF16)
            taken[:, at, :] = turned.reshape(side, side, width)
            return carry

        lax.fori_loop(0, lat_total // side, one, 0, unroll=5)

    spectrum = jnp.concatenate([taken[2 * order], taken[2 * order + 1]], axis=1)
    coeffs = lax.dot_general(
        fwd_ref[0], spectrum, (((0,), (0,)), ((), ())), preferred_element_type=F32
    ).astype(BF16)
    mixed = jnp.dot(coeffs, mix_ref[...], preferred_element_type=F32).astype(BF16)
    made[order] = jnp.dot(inv_ref[0], mixed, preferred_element_type=F32).astype(BF16)

    @pl.when(order == group - 1)
    def _():
        def one(j, carry):
            first = pl.multiple_of(j * side, side)
            at = pl.ds(first, side)
            columns = []
            for h in range(halves):
                pieces = []
                for r in range(group):
                    for c in range(2):
                        low = (c * halves + h) * lanes
                        pieces.append(made[r, at, low : low + lanes])
                columns.append(jnp.concatenate(pieces, axis=0))
            block = jnp.concatenate(columns, axis=1)
            turned = jnp.dot(swap_ref[...], block, preferred_element_type=F32).astype(BF16)
            for i in range(side):
                spot = place[first + i]
                for h in range(halves):
                    out_ref[spot // 64, h, spot % 64] = turned[
                        i * side : (i + 1) * side, h * lanes : (h + 1) * lanes
                    ]
            return carry

        lax.fori_loop(0, lat_total // side, one, 0, unroll=5)


def order_steps(place, spectra, rows, fwd_table, inv_table, mix_t, first, parts, halves):
    pieces = len(spectra)
    count, width = spectra[0].shape[0], spectra[0].shape[3]
    side = 2 * ORDER_GROUP
    lat_total = fwd_table.shape[1]
    degrees = fwd_table.shape[2]
    group = side // 2
    index = jnp.arange(side * side, dtype=jnp.int32)
    swapped = (index % side) * side + index // side
    swap = (swapped[:, None] == index[None, :]).astype(BF16)
    both = 2 * width
    part_lats = lat_total // parts
    out_shape = (parts, halves, part_lats, side, width // halves)
    return pl.pallas_call(
        functools.partial(orders_kernel, group=group, pieces=pieces, rows=rows),
        grid_spec=pltpu.PrefetchScalarGridSpec(
            num_scalar_prefetch=1,
            grid=(group,),
            in_specs=[pl.BlockSpec(memory_space=pl.ANY)] * pieces
            + [
                pl.BlockSpec((1, lat_total, degrees), lambda r, s: (first + r, 0, 0)),
                pl.BlockSpec((1, lat_total, degrees), lambda r, s: (first + r, 0, 0)),
                pl.BlockSpec((both, both), lambda r, s: (0, 0)),
                pl.BlockSpec((side * side, side * side), lambda r, s: (0, 0)),
            ],
            out_specs=pl.BlockSpec(out_shape, lambda r, s: (0, 0, 0, 0, 0)),
            scratch_shapes=[
                pltpu.VMEM((lat_total, side, width), BF16),
                pltpu.VMEM((side, lat_total, width), BF16),
                pltpu.VMEM((group, lat_total, both), BF16),
                pltpu.SemaphoreType.DMA((pieces * count,)),
            ],
        ),
        out_shape=jax.ShapeDtypeStruct(out_shape, BF16),
        compiler_params=pltpu.CompilerParams(vmem_limit_bytes=VMEM_BYTES),
        cost_estimate=work(
            group * 2 * both * degrees * (2 * lat_total + both), 8 * group * degrees * lat_total
        ),
    )(place, *spectra, fwd_table, inv_table, mix_t, swap)


def synthesis_kernel(*refs):
    *mode_refs, basis_ref, out_ref = refs
    sources, _, height, lanes = mode_refs[0].shape
    blocks = out_ref.shape[0]
    lats = mode_refs[0].shape[1]
    points = out_ref.shape[1] // lats
    right = jnp.concatenate(
        [
            jnp.concatenate(
                [ref[:, t].reshape(sources * height, lanes) for ref in mode_refs], axis=0
            )
            for t in range(lats)
        ],
        axis=1,
    )

    def one(k, carry):
        value = jnp.dot(basis_ref[k], right, preferred_element_type=F32)
        span = 4 * points
        for t in range(0, lats, 4):
            rows = [value[:points, (t + i) * lanes : (t + i + 1) * lanes] for i in range(4)]
            low = t * points
            out_ref[k, low : low + span, :] = jnp.concatenate(rows, axis=0).astype(BF16)
        return carry

    lax.fori_loop(0, blocks, one, 0)


def synthesis_steps(modes, basis, points, lats, first, count):
    sources, _, height, lanes = modes[0].shape
    blocks = basis.shape[0]
    offset = first // lats
    return pl.pallas_call(
        synthesis_kernel,
        grid=(-(-count // lats),),
        in_specs=[
            pl.BlockSpec((sources, lats, height, lanes), lambda i: (0, i + offset, 0, 0))
            for _ in modes
        ]
        + [pl.BlockSpec(basis.shape, lambda i: (0, 0, 0))],
        out_specs=pl.BlockSpec((blocks, lats * points, lanes), lambda i: (0, i, 0)),
        out_shape=jax.ShapeDtypeStruct((blocks, count * points, lanes), BF16),
        compiler_params=pltpu.CompilerParams(vmem_limit_bytes=VMEM_BYTES),
        cost_estimate=work(2 * count * lanes * basis.size, 4 * blocks * count * points * lanes),
    )(*modes, basis)


def finish_kernel(part_ref, enc_ref, out_ref, *, first, whole_groups, rest_rows):
    quarters, halves, rows, lanes = part_ref.shape
    group = pl.program_id(0) + first

    @pl.when(group < whole_groups)
    def _():
        for q in range(quarters):
            at = pl.ds(q * rows, rows)
            for h in range(halves):
                across = pl.ds(h * lanes, lanes)
                total = enc_ref[at, across].astype(F32) + part_ref[q, h].astype(F32)
                out_ref[at, across] = total.astype(BF16)

    @pl.when(group >= whole_groups)
    def _():
        count = quarters * rest_rows
        for h in range(halves):
            across = pl.ds(h * lanes, lanes)
            pieces = [part_ref[q, h].astype(F32)[:rest_rows] for q in range(quarters)]
            total = enc_ref[:count, across].astype(F32) + jnp.concatenate(pieces, axis=0)
            out_ref[:count, across] = total.astype(BF16)


def finish_steps(part, running, lats, points, first, whole_groups, rest):
    quarters, halves, count, lanes = part.shape
    rows = lats * points
    return pl.pallas_call(
        functools.partial(
            finish_kernel, first=first, whole_groups=whole_groups, rest_rows=rest * points
        ),
        grid=(-(-count // rows),),
        in_specs=[
            pl.BlockSpec((quarters, halves, rows, lanes), lambda i: (0, 0, i, 0)),
            pl.BlockSpec((quarters * rows, halves * lanes), lambda i: (i + first, 0)),
        ],
        out_specs=pl.BlockSpec((quarters * rows, halves * lanes), lambda i: (i + first, 0)),
        out_shape=jax.ShapeDtypeStruct(running.shape, BF16),
        input_output_aliases={1: 0},
        compiler_params=pltpu.CompilerParams(vmem_limit_bytes=VMEM_BYTES),
        cost_estimate=work(part.size * 4, 6 * part.size),
    )(part, running)


def listed_plan(
    source_cells,
    recv_src,
    recv_cell,
    recv_weight,
    enc_w1,
    enc_b1,
    enc_w2,
    enc_b2,
    mix_weight,
    fwd_table,
    inv_table,
):
    lon_count = lax.axis_size("lon")
    lat_count = lax.axis_size("lat")
    channels = source_cells.shape[0]
    slot_count = recv_src.shape[0] // lon_count
    lat_total = fwd_table.shape[2]
    lat_dev = lat_total // lat_count
    lon_dev = NLON // lon_count
    cells_dev = lat_dev * lon_dev
    width = enc_w1.shape[0]
    ord_dev = fwd_table.shape[0]
    halves = width // LANES
    quarters = lon_count // halves
    part_lats = lat_dev // quarters

    source_all = jnp.broadcast_to(source_cells[None], (lon_count,) + source_cells.shape)
    source_all = lax.all_to_all(source_all, "lon", split_axis=0, concat_axis=0, tiled=True)
    listed = regrid_listed(
        source_all, recv_src, recv_cell, recv_weight, lat_dev, lon_dev, slot_count
    )
    band = lax.all_gather(listed, "lon", axis=0, tiled=False)
    pad_points = -(-lon_dev // TILE) * TILE
    at = jnp.arange(lon_count, dtype=jnp.int32)[:, None] * lon_dev + jnp.arange(
        pad_points, dtype=jnp.int32
    )
    inside = (jnp.arange(pad_points) < lon_dev)[None, :, None]
    listing = jnp.arange(ORDERS, dtype=jnp.int32).reshape(-1, ord_dev // ORDER_GROUP, ORDER_GROUP)
    basis_out = basis_by_point(listing.transpose(1, 0, 2).reshape(-1), at)
    basis_out = jnp.where(inside, basis_out, 0)
    coded = band[:, channels + 2 : channels + 4, : lat_dev + 1].astype(jnp.int32)
    starts = coded[:, 0] * 128 + coded[:, 1]
    starts, basis_out = lax.optimization_barrier((starts, basis_out))

    mine = lax.axis_index("lon")
    sets = ord_dev // ORDER_GROUP
    owned = (
        (jnp.arange(lat_count, dtype=jnp.int32)[:, None] * lon_count + mine) * ord_dev
        + jnp.arange(ord_dev, dtype=jnp.int32)[None, :]
    ).reshape(-1)
    point_rows = -(-lon_dev // LANES) * LANES
    at = jnp.arange(lon_count, dtype=jnp.int32)[:, None] * lon_dev + jnp.arange(
        point_rows, dtype=jnp.int32
    )
    inside = (jnp.arange(point_rows) < lon_dev)[None, :, None]
    basis_in = jnp.where(inside, basis_by_point(owned, at), 0)
    sums = jnp.sum(basis_in.astype(F32), axis=(0, 1))[:, None]
    w1 = jnp.zeros((band.shape[1], width), BF16).at[:channels].set(enc_w1.T)
    first, second = zonal_transform(
        band,
        starts,
        w1,
        enc_b1[None, :],
        enc_w2.T,
        enc_b2[None, :],
        basis_in,
        sums,
        lat_dev,
        lat_count,
        sets,
        channels,
    )

    run = quarters * LATS
    whole_groups = lat_dev // run
    rest = (lat_dev - whole_groups * run) // quarters
    lat = np.arange(lat_dev)
    tail = lat - whole_groups * run
    to_part = np.where(tail < 0, lat % run // LATS, tail // max(rest, 1))
    to_row = np.where(tail < 0, lat // run * LATS + lat % LATS, whole_groups * LATS + tail % max(rest, 1))
    place = (np.arange(lat_count)[:, None] * quarters + to_part) * 64 + to_row
    place = jnp.asarray(place.reshape(-1), jnp.int32)

    mix_t = mixing_matrix(mix_weight).T
    fwd_by_lat = fwd_table.transpose(0, 2, 1)
    def exchange(piece):
        return lax.all_to_all(piece, "lat", split_axis=0, concat_axis=0, tiled=True)

    piece = source_all.transpose(1, 0, 2).reshape(channels, -1)
    regridded = regrid_all(
        piece,
        recv_src.reshape(lon_count, slot_count),
        recv_cell.reshape(lon_count, slot_count),
        recv_weight.reshape(lon_count, slot_count),
        cells_dev,
    )
    early = exchange(first)
    modes, waiting = [], []
    for g in range(sets):
        piece = second[g]
        if waiting:
            piece, waiting[-1] = lax.optimization_barrier((piece, waiting[-1]))
        else:
            piece, early = lax.optimization_barrier((piece, early))
        waiting.append(exchange(piece))
    for g in range(sets):
        made = order_steps(
            place,
            [early, waiting[g]],
            [g * 2 * ORDER_GROUP, 0],
            fwd_by_lat,
            inv_table,
            mix_t,
            g * ORDER_GROUP,
            lat_count * quarters,
            halves,
        )
        made = made.reshape(lat_count * lon_count, part_lats, 2 * ORDER_GROUP, LANES)
        if g + 1 < sets:
            made, waiting[g + 1] = lax.optimization_barrier((made, waiting[g + 1]))
        if modes:
            made, modes[-1], regridded = lax.optimization_barrier((made, modes[-1], regridded))
        modes.append(
            lax.all_to_all(made, ("lat", "lon"), split_axis=0, concat_axis=0, tiled=True)
        )

    running = encoder_by_cell(regridded, enc_w1, enc_b1, enc_w2, enc_b2)
    modes[-1], running = lax.optimization_barrier((modes[-1], running))
    cuts = [0] + [c * LATS for c in CHUNK_CUTS if c * LATS < part_lats] + [part_lats]
    parts = []
    for first, last in zip(cuts[:-1], cuts[1:]):
        parts.append(synthesis_steps(modes, basis_out, lon_dev, LATS, first, last - first))
    for first, last, part in zip(cuts[:-1], cuts[1:], parts):
        count = last - first
        part = lax.all_to_all(part, "lon", split_axis=0, concat_axis=0, tiled=True)
        part = part.reshape(quarters, halves, count * lon_dev, LANES)
        running = finish_steps(part, running, LATS, lon_dev, first // LATS, whole_groups, rest)
    return running.T


def dense_plan(
    source_cells,
    recv_src,
    recv_cell,
    recv_weight,
    enc_w1,
    enc_b1,
    enc_w2,
    enc_b2,
    mix_weight,
    fwd_table,
    inv_table,
):
    lon_count = lax.axis_size("lon")
    lat_count = lax.axis_size("lat")
    slot_count = recv_src.shape[0] // lon_count
    sources = recv_src.reshape(lon_count, slot_count)
    targets = recv_cell.reshape(lon_count, slot_count)
    weights = recv_weight.reshape(lon_count, slot_count)
    lat_total = fwd_table.shape[2]
    lat_dev = lat_total // lat_count
    lon_dev = NLON // lon_count
    cells_dev = lat_dev * lon_dev
    width = enc_w1.shape[0]
    ch_dev = width // lon_count
    orders_total = ORDERS
    ord_dev = fwd_table.shape[0]
    piece = lax.all_gather(source_cells, "lon", axis=1, tiled=True)
    regridded = regrid_all(piece, sources, targets, weights, cells_dev).T
    encoded = dense_encoder(regridded, enc_w1, enc_b1, enc_w2, enc_b2)
    blocked = encoded.reshape(width, lat_dev, 1, lon_dev)
    circles = lax.all_to_all(blocked, "lon", split_axis=0, concat_axis=2, tiled=True).reshape(
        ch_dev * lat_dev, NLON
    )
    natural_order = jnp.arange(orders_total, dtype=jnp.int32)
    dft_basis = build_basis(natural_order, NLON)
    spectra = lax.dot_general(
        dft_basis, circles, (((1,), (1,)), ((), ())), preferred_element_type=jnp.float32
    )
    spectra = spectra.astype(jnp.bfloat16).reshape(orders_total, 2, ch_dev, lat_dev)
    by_order = lax.all_to_all(
        lax.all_to_all(spectra, "lat", split_axis=0, concat_axis=3, tiled=True),
        "lon",
        split_axis=0,
        concat_axis=2,
        tiled=True,
    )
    by_order = by_order.reshape(ord_dev, 2 * width, lat_total)
    coeffs = jnp.einsum(
        "mrt,mlt->mrl", by_order, fwd_table, preferred_element_type=jnp.float32
    ).astype(jnp.bfloat16)
    mix_block = mixing_matrix(mix_weight)
    mixed = jnp.einsum("gr,mrl->mgl", mix_block, coeffs, preferred_element_type=jnp.float32).astype(
        jnp.bfloat16
    )
    synth_in = jnp.einsum(
        "mrl,mtl->mrt", mixed, inv_table, preferred_element_type=jnp.float32
    ).astype(jnp.bfloat16)
    synth_in = synth_in.reshape(ord_dev, 2, width, lat_total)
    returned_modes = lax.all_to_all(
        lax.all_to_all(synth_in, "lon", split_axis=2, concat_axis=0, tiled=True),
        "lat",
        split_axis=3,
        concat_axis=0,
        tiled=True,
    )
    returned_modes = returned_modes.reshape(2 * orders_total, ch_dev * lat_dev)
    synthesis = lax.dot_general(
        returned_modes, dft_basis, (((0,), (0,)), ((), ())), preferred_element_type=jnp.float32
    )
    synthesis = synthesis.astype(jnp.bfloat16).reshape(ch_dev, lat_dev, lon_count, lon_dev)
    regained = lax.all_to_all(synthesis, "lon", split_axis=2, concat_axis=0, tiled=True).reshape(
        width, cells_dev
    )
    return (encoded.astype(jnp.float32) + regained.astype(jnp.float32)).astype(jnp.bfloat16)


def solution(mesh):
    in_specs = (
        P(None, ("lat", "lon")),
        P(("lat", "lon")),
        P(("lat", "lon")),
        P(("lat", "lon")),
        P(),
        P(),
        P(),
        P(),
        P(),
        P(("lat", "lon"), None, None),
        P(("lat", "lon"), None, None),
    )
    out_specs = P(None, ("lat", "lon"))
    lon_count = mesh.shape["lon"]
    lat_count = mesh.shape["lat"]

    def on_device(*arrays):
        slots = arrays[1].shape[0]
        width = arrays[4].shape[0]
        ord_dev, _, lat_total = arrays[9].shape
        lat_dev = lat_total // lat_count
        cells_dev = lat_dev * (NLON // lon_count)
        halves = max(1, width // LANES)
        fits = (
            slots * 4 <= cells_dev
            and width % LANES == 0
            and lon_count % halves == 0
            and lat_dev % (lon_count // halves) == 0
            and lat_dev % 45 == 0
            and 4 * (NLON // lon_count) % TILE == 0
            and lat_dev // (lon_count // halves) < 64
            and ord_dev % ORDER_GROUP == 0
            and lat_total % TILE == 0
        )
        return listed_plan(*arrays) if fits else dense_plan(*arrays)

    return jax.shard_map(
        on_device, mesh=mesh, in_specs=in_specs, out_specs=out_specs, check_vma=False
    )
```

```python
import functools
import math

import jax
import jax.numpy as jnp
import numpy as np
from jax import lax
from jax.experimental import pallas as pl
from jax.experimental.pallas import tpu as pltpu
from jax.sharding import PartitionSpec as P

NLON = 1440
ORDERS = 512
LANES = 128
TILE = 16
WINDOW = 48
UNROLL = 5
LATS = 8
CHUNK_CUTS = (1, 5)
ORDER_GROUP = 8
VMEM_BYTES = 60 * 1024 * 1024

F32 = jnp.float32
BF16 = jnp.bfloat16


def work(flops, bytes_moved):
    return pl.CostEstimate(flops=flops, bytes_accessed=bytes_moved, transcendentals=0)


def build_basis(order_list, points_total):
    points = jnp.arange(points_total, dtype=jnp.int32)
    angles = (order_list[:, None] * points[None, :] % points_total).astype(jnp.float32) * (
        2.0 * math.pi / points_total
    )
    factor = math.sqrt(2.0 / points_total)
    stacked = jnp.stack([factor * jnp.cos(angles), -factor * jnp.sin(angles)], axis=1)
    return stacked.astype(jnp.bfloat16).reshape(2 * order_list.shape[0], points_total)


def basis_by_point(order_list, points):
    shape = points.shape + order_list.shape
    angles = (points[..., None] * order_list % NLON).astype(F32) * (2.0 * math.pi / NLON)
    factor = math.sqrt(2.0 / NLON)
    stacked = jnp.stack([factor * jnp.cos(angles), -factor * jnp.sin(angles)], axis=-1)
    return stacked.astype(BF16).reshape(shape[:-1] + (2 * shape[-1],))


def spread(running, values, weights, targets):
    channels = values.shape[-1]
    contrib = values.astype(jnp.float32) * weights[:, :, None]
    return running.at[targets.reshape(-1)].add(contrib.reshape(-1, channels))


def mixing_matrix(mix_weight):
    real_part = mix_weight[0]
    imag_part = mix_weight[1]
    return jnp.concatenate(
        [
            jnp.concatenate([real_part, -imag_part], axis=1),
            jnp.concatenate([imag_part, real_part], axis=1),
        ],
        axis=0,
    )


def regrid_all(piece, sources, targets, weights, cells_dev):
    shard_count, slot_count = sources.shape
    channels = piece.shape[0]
    src_rows = piece.shape[1] // shard_count
    piece_rows = piece.T
    offsets = jnp.arange(shard_count, dtype=jnp.int32)[:, None] * src_rows
    picked = jnp.take(piece_rows, (offsets + sources).reshape(-1), axis=0)
    picked = picked.reshape(shard_count, slot_count, channels)
    empty = jnp.zeros((cells_dev, channels), jnp.float32)
    return spread(empty, picked, weights, targets).astype(jnp.bfloat16)


def dense_encoder(regridded, enc_w1, enc_b1, enc_w2, enc_b2):
    hidden = jnp.dot(enc_w1, regridded, preferred_element_type=jnp.float32) + enc_b1[:, None]
    hidden = jax.nn.gelu(hidden, approximate=False).astype(jnp.bfloat16)
    return (
        jnp.dot(enc_w2, hidden, preferred_element_type=jnp.float32) + enc_b2[:, None]
    ).astype(jnp.bfloat16)


def encoder_by_cell(regridded, enc_w1, enc_b1, enc_w2, enc_b2):
    hidden = jnp.dot(regridded, enc_w1.T, preferred_element_type=F32) + enc_b1
    hidden = jax.nn.gelu(hidden, approximate=False).astype(BF16)
    return (jnp.dot(hidden, enc_w2.T, preferred_element_type=F32) + enc_b2).astype(BF16)


def regrid_kernel(live, src_ref, cols_ref, row_ref, out_ref, contrib, *, channels, shards, slots, src_rows):
    step = pl.program_id(0)
    height, rows = out_ref.shape

    @pl.when(step == 0)
    def _():
        contrib[...] = jnp.zeros_like(contrib)
        lane = lax.broadcasted_iota(jnp.int32, (slots, src_rows), 1).astype(F32)

        def one(j, carry):
            at = pl.ds(pl.multiple_of(j * slots, slots), slots)
            index = cols_ref[at, 0:1]
            weight = cols_ref[at, 1:2]
            hot = (index == lane).astype(BF16)
            picked = lax.dot_general(
                hot, src_ref[j], (((1,), (1,)), ((), ())), preferred_element_type=F32
            )
            value = picked * weight
            upper = value.astype(BF16)
            lower = (value - upper.astype(F32)).astype(BF16)
            contrib[at, 0:channels] = upper
            contrib[at, LANES : LANES + channels] = lower
            return carry

        lax.fori_loop(0, shards, one, 0, unroll=4)

    here = pl.ds(pl.multiple_of(step * rows, rows), rows)
    used = jnp.logical_or(step == 0, step * rows < live[0])

    @pl.when(used)
    def _():
        cell = cols_ref[here, 2:3]
        total = jnp.zeros((rows, 2 * LANES), F32)
        for s in range(shards):
            same = (cell == row_ref[:, s * slots : (s + 1) * slots]).astype(BF16)
            total += jnp.dot(
                same, contrib[s * slots : (s + 1) * slots, :], preferred_element_type=F32
            )
        merged = total[:, :LANES] + total[:, LANES:]
        lane = lax.broadcasted_iota(jnp.int32, (rows, LANES), 1)
        for place in range(4):
            merged = jnp.where(
                lane == channels + place, cols_ref[here, 3 + place : 4 + place], merged
            )
        out_ref[...] = merged.T[:height].astype(BF16)

    @pl.when(jnp.logical_not(used))
    def _():
        out_ref[...] = jnp.zeros_like(out_ref)


def regrid_listed(source_all, recv_src, recv_cell, recv_weight, lat_dev, lon_dev, slot_count):
    shards, channels, src_rows = source_all.shape
    total = recv_src.shape[0]
    keys = jnp.where(recv_weight != 0, recv_cell, lat_dev * lon_dev)
    ordered = jnp.sort(keys)
    lead = jnp.concatenate([jnp.ones((1,), jnp.bool_), ordered[1:] != ordered[:-1]])
    limits = jnp.arange(lat_dev + 1, dtype=jnp.int32) * lon_dev
    starts = jnp.sum((keys[None, :] < limits[:, None]).astype(jnp.int32), axis=1)
    live = starts[lat_dev:]
    starts = jnp.zeros((total,), jnp.int32).at[: lat_dev + 1].set(starts)
    cols = jnp.stack(
        [
            recv_src.astype(F32),
            recv_weight,
            ordered.astype(F32),
            (ordered % lon_dev).astype(F32),
            lead.astype(F32),
            (starts // 128).astype(F32),
            (starts % 128).astype(F32),
            jnp.zeros((total,), F32),
        ],
        axis=1,
    )
    rows = min(512, total)
    height = -(-(channels + 4) // TILE) * TILE
    return pl.pallas_call(
        functools.partial(
            regrid_kernel, channels=channels, shards=shards, slots=slot_count, src_rows=src_rows
        ),
        grid_spec=pltpu.PrefetchScalarGridSpec(
            num_scalar_prefetch=1,
            grid=(total // rows,),
            in_specs=[
                pl.BlockSpec((shards, channels, src_rows), lambda i, n: (0, 0, 0)),
                pl.BlockSpec((total, 8), lambda i, n: (0, 0)),
                pl.BlockSpec((1, total), lambda i, n: (0, 0)),
            ],
            out_specs=pl.BlockSpec((height, rows), lambda i, n: (0, i)),
            scratch_shapes=[pltpu.VMEM((total, 2 * LANES), BF16)],
        ),
        out_shape=jax.ShapeDtypeStruct((height, total), BF16),
        compiler_params=pltpu.CompilerParams(vmem_limit_bytes=VMEM_BYTES),
        cost_estimate=work(4 * total * total * LANES, 2 * total * LANES),
    )(live, source_all, cols, keys.astype(F32)[None, :])


def transform_latitudes(starts, hots, delta, base, out_refs, first_lat, blocks):
    step = pl.program_id(0)
    groups, lats, _, _ = out_refs[0].shape
    columns = hots.shape[1]
    block_rows = (hots.shape[0] - WINDOW) // blocks
    place = lax.broadcasted_iota(jnp.int32, (WINDOW, columns), 0)

    def bounds(t):
        lows = [starts[k, t] + k * block_rows for k in range(blocks)]
        highs = [starts[k, t + 1] + k * block_rows for k in range(blocks)]
        firsts = [(low // TILE) * TILE for low in lows]
        most = jnp.int32(1)
        for k in range(blocks):
            most = jnp.maximum(most, (highs[k] - firsts[k] + WINDOW - 1) // WINDOW)
        return lows, highs, firsts, most

    def window(lows, highs, firsts):
        left, right = [], []
        for k in range(blocks):
            first = pl.multiple_of(firsts[k], TILE)
            at = pl.ds(first, WINDOW)
            inside = (place >= lows[k] - first) & (place < highs[k] - first)
            left.append(jnp.where(inside, hots[at, :].astype(F32), 0.0).astype(BF16))
            right.append(delta[at, :])
        return lax.dot_general(
            jnp.concatenate(left, axis=0),
            jnp.concatenate(right, axis=0),
            (((0,), (0,)), ((), ())),
            preferred_element_type=F32,
        )

    def store(tt, result):
        result = result.astype(BF16)
        low = 0
        for g in range(groups):
            for out_ref in out_refs:
                height = out_ref.shape[2]
                out_ref[g, tt] = result[low : low + height, :]
                low += height

    def several(b, carry):
        chosen = [b * UNROLL + u for u in range(UNROLL)]
        limits = [bounds(first_lat + step * lats + tt) for tt in chosen]
        most = limits[0][3]
        for limit in limits[1:]:
            most = jnp.maximum(most, limit[3])

        @pl.when(most == 1)
        def _():
            for tt, (lows, highs, firsts, _) in zip(chosen, limits):
                store(tt, base[...] + window(lows, highs, firsts))

        @pl.when(most > 1)
        def _():
            for tt, (lows, highs, firsts, count) in zip(chosen, limits):

                def more(j, running):
                    moved = [
                        jnp.minimum(firsts[k] + j * WINDOW, (highs[k] + TILE - 1) // TILE * TILE)
                        for k in range(blocks)
                    ]
                    return running + window(lows, highs, moved)

                store(tt, lax.fori_loop(0, count, more, base[...]))

        return carry

    lax.fori_loop(0, lats // UNROLL, several, 0)


def zonal_first_kernel(
    starts,
    rows_ref,
    w1_ref,
    b1_ref,
    w2_ref,
    b2_ref,
    basis_ref,
    sums_ref,
    *rest,
    channels,
    blocks,
    block_rows,
    lat_dev,
):
    *out_refs, delta_out, hots_out, base, delta, hots, sems = rest
    step = pl.program_id(0)
    total = blocks * block_rows
    width = delta.shape[1]
    columns = hots.shape[1]
    chunk = min(512, block_rows)
    copies = [
        pltpu.make_async_copy(delta, delta_out, sems.at[0]),
        pltpu.make_async_copy(hots, hots_out, sems.at[1]),
    ]

    def encode(values):
        hidden = jnp.dot(values, w1_ref[...], preferred_element_type=F32) + b1_ref[...]
        hidden = 0.5 * hidden * (1.0 + lax.erf(hidden * math.sqrt(0.5)))
        encoded = jnp.dot(hidden.astype(BF16), w2_ref[...], preferred_element_type=F32)
        return (encoded + b2_ref[...]).astype(BF16).astype(F32)

    @pl.when(step == 0)
    def _():
        empty = encode(jnp.zeros((TILE, rows_ref.shape[1]), BF16))[0:1]
        base[...] = sums_ref[...] * empty
        delta[pl.ds(total, WINDOW), :] = jnp.zeros((WINDOW, width), BF16)
        hots[pl.ds(total, WINDOW), :] = jnp.zeros((WINDOW, columns), BF16)
        points = basis_ref.shape[1]
        lane = lax.broadcasted_iota(jnp.int32, (chunk, points), 1).astype(F32)
        per_block = block_rows // chunk

        def one_block(k, carry):
            used = starts[k, lat_dev] + TILE + WINDOW
            count = jnp.minimum((used + chunk - 1) // chunk, per_block)

            def one(j, inner):
                at = pl.ds(pl.multiple_of(k * block_rows + j * chunk, chunk), chunk)
                part = pl.ds(pl.multiple_of(j * chunk, chunk), chunk)
                values = rows_ref[k, :, part].astype(F32).T
                delta[at, :] = (encode(values.astype(BF16)) - empty).astype(BF16)
                point = values[:, channels : channels + 1]
                lead = values[:, channels + 1 : channels + 2]
                point = jnp.where(lead > 0.5, point, -1.0)
                hot = (point == lane).astype(BF16)
                hots[at, :] = jnp.dot(hot, basis_ref[k], preferred_element_type=F32).astype(BF16)
                return inner

            return lax.fori_loop(0, count, one, carry)

        lax.fori_loop(0, blocks, one_block, 0)
        for copy in copies:
            copy.start()

    transform_latitudes(starts, hots, delta, base, out_refs, 0, blocks)

    @pl.when(step == pl.num_programs(0) - 1)
    def _():
        for copy in copies:
            copy.wait()


def zonal_second_kernel(starts, delta, hots, base, *out_refs, first_lat, blocks):
    transform_latitudes(starts, hots, delta, base, out_refs, first_lat, blocks)


def whole_block(shape):
    return pl.BlockSpec(shape, lambda i, *_: (0,) * len(shape), pipeline_mode=pl.Buffered(1))


def zonal_outputs(groups, lat_count, heights, lats, width):
    shapes = [jax.ShapeDtypeStruct((groups, lat_count, h, width), BF16) for h in heights]
    specs = [pl.BlockSpec((groups, lats, h, width), lambda i, *_: (0, i, 0, 0)) for h in heights]
    return shapes, specs


def zonal_transform(rows, starts, w1, b1, w2, b2, basis, sums, lat_dev, groups, sets, channels):
    blocks, _, block_rows = rows.shape
    width = w2.shape[1]
    columns = basis.shape[2]
    height = columns // groups
    total = blocks * block_rows
    lats = 15
    early = lat_dev // 3 // lats * lats
    late = lat_dev - early
    flops = 25 * total * width * 2 * columns
    shapes, specs = zonal_outputs(groups, early, [height], lats, width)
    kept = [
        jax.ShapeDtypeStruct((total + WINDOW, width), BF16),
        jax.ShapeDtypeStruct((total + WINDOW, columns), BF16),
        jax.ShapeDtypeStruct((columns, width), F32),
    ]
    inputs = (rows, w1, b1, w2, b2, basis, sums)
    first, delta, hots, base = pl.pallas_call(
        functools.partial(
            zonal_first_kernel,
            channels=channels,
            blocks=blocks,
            block_rows=block_rows,
            lat_dev=lat_dev,
        ),
        grid_spec=pltpu.PrefetchScalarGridSpec(
            num_scalar_prefetch=1,
            grid=(early // lats,),
            in_specs=[whole_block(a.shape) for a in inputs],
            out_specs=specs
            + [pl.BlockSpec(memory_space=pl.ANY)] * 2
            + [whole_block((columns, width))],
            scratch_shapes=[
                pltpu.VMEM((total + WINDOW, width), BF16),
                pltpu.VMEM((total + WINDOW, columns), BF16),
                pltpu.SemaphoreType.DMA((2,)),
            ],
        ),
        out_shape=shapes + kept,
        compiler_params=pltpu.CompilerParams(vmem_limit_bytes=VMEM_BYTES),
        cost_estimate=work(flops, 4 * total * width),
    )(starts, *inputs)
    shapes, specs = zonal_outputs(groups, late, [height // sets] * sets, lats, width)
    second = pl.pallas_call(
        functools.partial(zonal_second_kernel, first_lat=early, blocks=blocks),
        grid_spec=pltpu.PrefetchScalarGridSpec(
            num_scalar_prefetch=1,
            grid=(late // lats,),
            in_specs=[whole_block(a.shape) for a in (delta, hots, base)],
            out_specs=specs,
        ),
        out_shape=shapes,
        compiler_params=pltpu.CompilerParams(vmem_limit_bytes=VMEM_BYTES),
        cost_estimate=work(flops, 4 * total * width),
    )(starts, delta, hots, base)
    return first, second


def orders_kernel(place, *refs, group, pieces, rows):
    spec_refs = refs[:pieces]
    fwd_ref, inv_ref, mix_ref, swap_ref, out_ref, arrived, taken, made, sems = refs[pieces:]
    order = pl.program_id(0)
    lat_total, _, width = arrived.shape
    halves, lanes = out_ref.shape[1], out_ref.shape[4]
    side = 2 * group
    count = spec_refs[0].shape[0]

    @pl.when(order == 0)
    def _():
        copies = []
        for i in range(count):
            low = i * lat_total // count
            for ref, row in zip(spec_refs, rows):
                lats = ref.shape[1]
                copies.append(
                    pltpu.make_async_copy(
                        ref.at[i, :, pl.ds(row, side)],
                        arrived.at[pl.ds(low, lats)],
                        sems.at[len(copies)],
                    )
                )
                low += lats
        for copy in copies:
            copy.start()
        for copy in copies:
            copy.wait()

        def one(j, carry):
            at = pl.ds(pl.multiple_of(j * side, side), side)
            block = arrived[at].reshape(side * side, width)
            turned = jnp.dot(swap_ref[...], block, preferred_element_type=F32).astype(BF16)
            taken[:, at, :] = turned.reshape(side, side, width)
            return carry

        lax.fori_loop(0, lat_total // side, one, 0, unroll=5)

    spectrum = jnp.concatenate([taken[2 * order], taken[2 * order + 1]], axis=1)
    coeffs = lax.dot_general(
        fwd_ref[0], spectrum, (((0,), (0,)), ((), ())), preferred_element_type=F32
    ).astype(BF16)
    mixed = jnp.dot(coeffs, mix_ref[...], preferred_element_type=F32).astype(BF16)
    made[order] = jnp.dot(inv_ref[0], mixed, preferred_element_type=F32).astype(BF16)

    @pl.when(order == group - 1)
    def _():
        def one(j, carry):
            first = pl.multiple_of(j * side, side)
            at = pl.ds(first, side)
            columns = []
            for h in range(halves):
                pieces = []
                for r in range(group):
                    for c in range(2):
                        low = (c * halves + h) * lanes
                        pieces.append(made[r, at, low : low + lanes])
                columns.append(jnp.concatenate(pieces, axis=0))
            block = jnp.concatenate(columns, axis=1)
            turned = jnp.dot(swap_ref[...], block, preferred_element_type=F32).astype(BF16)
            for i in range(side):
                spot = place[first + i]
                for h in range(halves):
                    out_ref[spot // 64, h, spot % 64] = turned[
                        i * side : (i + 1) * side, h * lanes : (h + 1) * lanes
                    ]
            return carry

        lax.fori_loop(0, lat_total // side, one, 0, unroll=5)


def order_steps(place, spectra, rows, fwd_table, inv_table, mix_t, first, parts, halves):
    pieces = len(spectra)
    count, width = spectra[0].shape[0], spectra[0].shape[3]
    side = 2 * ORDER_GROUP
    lat_total = fwd_table.shape[1]
    degrees = fwd_table.shape[2]
    group = side // 2
    index = jnp.arange(side * side, dtype=jnp.int32)
    swapped = (index % side) * side + index // side
    swap = (swapped[:, None] == index[None, :]).astype(BF16)
    both = 2 * width
    part_lats = lat_total // parts
    out_shape = (parts, halves, part_lats, side, width // halves)
    return pl.pallas_call(
        functools.partial(orders_kernel, group=group, pieces=pieces, rows=rows),
        grid_spec=pltpu.PrefetchScalarGridSpec(
            num_scalar_prefetch=1,
            grid=(group,),
            in_specs=[pl.BlockSpec(memory_space=pl.ANY)] * pieces
            + [
                pl.BlockSpec((1, lat_total, degrees), lambda r, s: (first + r, 0, 0)),
                pl.BlockSpec((1, lat_total, degrees), lambda r, s: (first + r, 0, 0)),
                pl.BlockSpec((both, both), lambda r, s: (0, 0)),
                pl.BlockSpec((side * side, side * side), lambda r, s: (0, 0)),
            ],
            out_specs=pl.BlockSpec(out_shape, lambda r, s: (0, 0, 0, 0, 0)),
            scratch_shapes=[
                pltpu.VMEM((lat_total, side, width), BF16),
                pltpu.VMEM((side, lat_total, width), BF16),
                pltpu.VMEM((group, lat_total, both), BF16),
                pltpu.SemaphoreType.DMA((pieces * count,)),
            ],
        ),
        out_shape=jax.ShapeDtypeStruct(out_shape, BF16),
        compiler_params=pltpu.CompilerParams(vmem_limit_bytes=VMEM_BYTES),
        cost_estimate=work(
            group * 2 * both * degrees * (2 * lat_total + both), 8 * group * degrees * lat_total
        ),
    )(place, *spectra, fwd_table, inv_table, mix_t, swap)


def synthesis_kernel(*refs):
    *mode_refs, basis_ref, out_ref = refs
    sources, _, height, lanes = mode_refs[0].shape
    blocks = out_ref.shape[0]
    lats = mode_refs[0].shape[1]
    points = out_ref.shape[1] // lats
    right = jnp.concatenate(
        [
            jnp.concatenate(
                [ref[:, t].reshape(sources * height, lanes) for ref in mode_refs], axis=0
            )
            for t in range(lats)
        ],
        axis=1,
    )

    def one(k, carry):
        value = jnp.dot(basis_ref[k], right, preferred_element_type=F32)
        span = 4 * points
        for t in range(0, lats, 4):
            rows = [value[:points, (t + i) * lanes : (t + i + 1) * lanes] for i in range(4)]
            low = t * points
            out_ref[k, low : low + span, :] = jnp.concatenate(rows, axis=0).astype(BF16)
        return carry

    lax.fori_loop(0, blocks, one, 0)


def synthesis_steps(modes, basis, points, lats, first, count):
    sources, _, height, lanes = modes[0].shape
    blocks = basis.shape[0]
    offset = first // lats
    return pl.pallas_call(
        synthesis_kernel,
        grid=(-(-count // lats),),
        in_specs=[
            pl.BlockSpec((sources, lats, height, lanes), lambda i: (0, i + offset, 0, 0))
            for _ in modes
        ]
        + [pl.BlockSpec(basis.shape, lambda i: (0, 0, 0))],
        out_specs=pl.BlockSpec((blocks, lats * points, lanes), lambda i: (0, i, 0)),
        out_shape=jax.ShapeDtypeStruct((blocks, count * points, lanes), BF16),
        compiler_params=pltpu.CompilerParams(vmem_limit_bytes=VMEM_BYTES),
        cost_estimate=work(2 * count * lanes * basis.size, 4 * blocks * count * points * lanes),
    )(*modes, basis)


def finish_kernel(part_ref, enc_ref, out_ref, *, first, whole_groups, rest_rows):
    quarters, halves, rows, lanes = part_ref.shape
    group = pl.program_id(0) + first

    @pl.when(group < whole_groups)
    def _():
        for q in range(quarters):
            at = pl.ds(q * rows, rows)
            for h in range(halves):
                across = pl.ds(h * lanes, lanes)
                total = enc_ref[at, across].astype(F32) + part_ref[q, h].astype(F32)
                out_ref[at, across] = total.astype(BF16)

    @pl.when(group >= whole_groups)
    def _():
        count = quarters * rest_rows
        for h in range(halves):
            across = pl.ds(h * lanes, lanes)
            pieces = [part_ref[q, h].astype(F32)[:rest_rows] for q in range(quarters)]
            total = enc_ref[:count, across].astype(F32) + jnp.concatenate(pieces, axis=0)
            out_ref[:count, across] = total.astype(BF16)


def finish_steps(part, running, lats, points, first, whole_groups, rest):
    quarters, halves, count, lanes = part.shape
    rows = lats * points
    return pl.pallas_call(
        functools.partial(
            finish_kernel, first=first, whole_groups=whole_groups, rest_rows=rest * points
        ),
        grid=(-(-count // rows),),
        in_specs=[
            pl.BlockSpec((quarters, halves, rows, lanes), lambda i: (0, 0, i, 0)),
            pl.BlockSpec((quarters * rows, halves * lanes), lambda i: (i + first, 0)),
        ],
        out_specs=pl.BlockSpec((quarters * rows, halves * lanes), lambda i: (i + first, 0)),
        out_shape=jax.ShapeDtypeStruct(running.shape, BF16),
        input_output_aliases={1: 0},
        compiler_params=pltpu.CompilerParams(vmem_limit_bytes=VMEM_BYTES),
        cost_estimate=work(part.size * 4, 6 * part.size),
    )(part, running)


def listed_plan(
    source_cells,
    recv_src,
    recv_cell,
    recv_weight,
    enc_w1,
    enc_b1,
    enc_w2,
    enc_b2,
    mix_weight,
    fwd_table,
    inv_table,
):
    lon_count = lax.axis_size("lon")
    lat_count = lax.axis_size("lat")
    channels = source_cells.shape[0]
    slot_count = recv_src.shape[0] // lon_count
    lat_total = fwd_table.shape[2]
    lat_dev = lat_total // lat_count
    lon_dev = NLON // lon_count
    cells_dev = lat_dev * lon_dev
    width = enc_w1.shape[0]
    ord_dev = fwd_table.shape[0]
    halves = width // LANES
    quarters = lon_count // halves
    part_lats = lat_dev // quarters

    source_all = jnp.broadcast_to(source_cells[None], (lon_count,) + source_cells.shape)
    source_all = lax.all_to_all(source_all, "lon", split_axis=0, concat_axis=0, tiled=True)
    listed = regrid_listed(
        source_all, recv_src, recv_cell, recv_weight, lat_dev, lon_dev, slot_count
    )
    band = lax.all_gather(listed, "lon", axis=0, tiled=False)
    pad_points = -(-lon_dev // TILE) * TILE
    at = jnp.arange(lon_count, dtype=jnp.int32)[:, None] * lon_dev + jnp.arange(
        pad_points, dtype=jnp.int32
    )
    inside = (jnp.arange(pad_points) < lon_dev)[None, :, None]
    listing = jnp.arange(ORDERS, dtype=jnp.int32).reshape(-1, ord_dev // ORDER_GROUP, ORDER_GROUP)
    basis_out = basis_by_point(listing.transpose(1, 0, 2).reshape(-1), at)
    basis_out = jnp.where(inside, basis_out, 0)
    coded = band[:, channels + 2 : channels + 4, : lat_dev + 1].astype(jnp.int32)
    starts = coded[:, 0] * 128 + coded[:, 1]
    starts, basis_out = lax.optimization_barrier((starts, basis_out))

    mine = lax.axis_index("lon")
    sets = ord_dev // ORDER_GROUP
    owned = (
        (jnp.arange(lat_count, dtype=jnp.int32)[:, None] * lon_count + mine) * ord_dev
        + jnp.arange(ord_dev, dtype=jnp.int32)[None, :]
    ).reshape(-1)
    point_rows = -(-lon_dev // LANES) * LANES
    at = jnp.arange(lon_count, dtype=jnp.int32)[:, None] * lon_dev + jnp.arange(
        point_rows, dtype=jnp.int32
    )
    inside = (jnp.arange(point_rows) < lon_dev)[None, :, None]
    basis_in = jnp.where(inside, basis_by_point(owned, at), 0)
    sums = jnp.sum(basis_in.astype(F32), axis=(0, 1))[:, None]
    w1 = jnp.zeros((band.shape[1], width), BF16).at[:channels].set(enc_w1.T)
    first, second = zonal_transform(
        band,
        starts,
        w1,
        enc_b1[None, :],
        enc_w2.T,
        enc_b2[None, :],
        basis_in,
        sums,
        lat_dev,
        lat_count,
        sets,
        channels,
    )

    run = quarters * LATS
    whole_groups = lat_dev // run
    rest = (lat_dev - whole_groups * run) // quarters
    lat = np.arange(lat_dev)
    tail = lat - whole_groups * run
    to_part = np.where(tail < 0, lat % run // LATS, tail // max(rest, 1))
    to_row = np.where(tail < 0, lat // run * LATS + lat % LATS, whole_groups * LATS + tail % max(rest, 1))
    place = (np.arange(lat_count)[:, None] * quarters + to_part) * 64 + to_row
    place = jnp.asarray(place.reshape(-1), jnp.int32)

    mix_t = mixing_matrix(mix_weight).T
    fwd_by_lat = fwd_table.transpose(0, 2, 1)
    def exchange(piece):
        return lax.all_to_all(piece, "lat", split_axis=0, concat_axis=0, tiled=True)

    piece = source_all.transpose(1, 0, 2).reshape(channels, -1)
    regridded = regrid_all(
        piece,
        recv_src.reshape(lon_count, slot_count),
        recv_cell.reshape(lon_count, slot_count),
        recv_weight.reshape(lon_count, slot_count),
        cells_dev,
    )
    early = exchange(first)
    modes, waiting = [], []
    for g in range(sets):
        piece = second[g]
        if waiting:
            piece, waiting[-1] = lax.optimization_barrier((piece, waiting[-1]))
        else:
            piece, early = lax.optimization_barrier((piece, early))
        waiting.append(exchange(piece))
    for g in range(sets):
        made = order_steps(
            place,
            [early, waiting[g]],
            [g * 2 * ORDER_GROUP, 0],
            fwd_by_lat,
            inv_table,
            mix_t,
            g * ORDER_GROUP,
            lat_count * quarters,
            halves,
        )
        made = made.reshape(lat_count * lon_count, part_lats, 2 * ORDER_GROUP, LANES)
        if g + 1 < sets:
            made, waiting[g + 1] = lax.optimization_barrier((made, waiting[g + 1]))
        if modes:
            made, modes[-1], regridded = lax.optimization_barrier((made, modes[-1], regridded))
        modes.append(
            lax.all_to_all(made, ("lat", "lon"), split_axis=0, concat_axis=0, tiled=True)
        )

    running = encoder_by_cell(regridded, enc_w1, enc_b1, enc_w2, enc_b2)
    modes[-1], running = lax.optimization_barrier((modes[-1], running))
    cuts = [0] + [c * LATS for c in CHUNK_CUTS if c * LATS < part_lats] + [part_lats]
    parts = []
    for first, last in zip(cuts[:-1], cuts[1:]):
        parts.append(synthesis_steps(modes, basis_out, lon_dev, LATS, first, last - first))
    for first, last, part in zip(cuts[:-1], cuts[1:], parts):
        count = last - first
        part = lax.all_to_all(part, "lon", split_axis=0, concat_axis=0, tiled=True)
        part = part.reshape(quarters, halves, count * lon_dev, LANES)
        running = finish_steps(part, running, LATS, lon_dev, first // LATS, whole_groups, rest)
    return running.T


def dense_plan(
    source_cells,
    recv_src,
    recv_cell,
    recv_weight,
    enc_w1,
    enc_b1,
    enc_w2,
    enc_b2,
    mix_weight,
    fwd_table,
    inv_table,
):
    lon_count = lax.axis_size("lon")
    lat_count = lax.axis_size("lat")
    slot_count = recv_src.shape[0] // lon_count
    sources = recv_src.reshape(lon_count, slot_count)
    targets = recv_cell.reshape(lon_count, slot_count)
    weights = recv_weight.reshape(lon_count, slot_count)
    lat_total = fwd_table.shape[2]
    lat_dev = lat_total // lat_count
    lon_dev = NLON // lon_count
    cells_dev = lat_dev * lon_dev
    width = enc_w1.shape[0]
    ch_dev = width // lon_count
    orders_total = ORDERS
    ord_dev = fwd_table.shape[0]
    piece = lax.all_gather(source_cells, "lon", axis=1, tiled=True)
    regridded = regrid_all(piece, sources, targets, weights, cells_dev).T
    encoded = dense_encoder(regridded, enc_w1, enc_b1, enc_w2, enc_b2)
    blocked = encoded.reshape(width, lat_dev, 1, lon_dev)
    circles = lax.all_to_all(blocked, "lon", split_axis=0, concat_axis=2, tiled=True).reshape(
        ch_dev * lat_dev, NLON
    )
    natural_order = jnp.arange(orders_total, dtype=jnp.int32)
    dft_basis = build_basis(natural_order, NLON)
    spectra = lax.dot_general(
        dft_basis, circles, (((1,), (1,)), ((), ())), preferred_element_type=jnp.float32
    )
    spectra = spectra.astype(jnp.bfloat16).reshape(orders_total, 2, ch_dev, lat_dev)
    by_order = lax.all_to_all(
        lax.all_to_all(spectra, "lat", split_axis=0, concat_axis=3, tiled=True),
        "lon",
        split_axis=0,
        concat_axis=2,
        tiled=True,
    )
    by_order = by_order.reshape(ord_dev, 2 * width, lat_total)
    coeffs = jnp.einsum(
        "mrt,mlt->mrl", by_order, fwd_table, preferred_element_type=jnp.float32
    ).astype(jnp.bfloat16)
    mix_block = mixing_matrix(mix_weight)
    mixed = jnp.einsum("gr,mrl->mgl", mix_block, coeffs, preferred_element_type=jnp.float32).astype(
        jnp.bfloat16
    )
    synth_in = jnp.einsum(
        "mrl,mtl->mrt", mixed, inv_table, preferred_element_type=jnp.float32
    ).astype(jnp.bfloat16)
    synth_in = synth_in.reshape(ord_dev, 2, width, lat_total)
    returned_modes = lax.all_to_all(
        lax.all_to_all(synth_in, "lon", split_axis=2, concat_axis=0, tiled=True),
        "lat",
        split_axis=3,
        concat_axis=0,
        tiled=True,
    )
    returned_modes = returned_modes.reshape(2 * orders_total, ch_dev * lat_dev)
    synthesis = lax.dot_general(
        returned_modes, dft_basis, (((0,), (0,)), ((), ())), preferred_element_type=jnp.float32
    )
    synthesis = synthesis.astype(jnp.bfloat16).reshape(ch_dev, lat_dev, lon_count, lon_dev)
    regained = lax.all_to_all(synthesis, "lon", split_axis=2, concat_axis=0, tiled=True).reshape(
        width, cells_dev
    )
    return (encoded.astype(jnp.float32) + regained.astype(jnp.float32)).astype(jnp.bfloat16)


def solution(mesh):
    in_specs = (
        P(None, ("lat", "lon")),
        P(("lat", "lon")),
        P(("lat", "lon")),
        P(("lat", "lon")),
        P(),
        P(),
        P(),
        P(),
        P(),
        P(("lat", "lon"), None, None),
        P(("lat", "lon"), None, None),
    )
    out_specs = P(None, ("lat", "lon"))
    lon_count = mesh.shape["lon"]
    lat_count = mesh.shape["lat"]

    def on_device(*arrays):
        slots = arrays[1].shape[0]
        width = arrays[4].shape[0]
        ord_dev, _, lat_total = arrays[9].shape
        lat_dev = lat_total // lat_count
        cells_dev = lat_dev * (NLON // lon_count)
        halves = max(1, width // LANES)
        fits = (
            slots * 4 <= cells_dev
            and width % LANES == 0
            and lon_count % halves == 0
            and lat_dev % (lon_count // halves) == 0
            and lat_dev % 45 == 0
            and 4 * (NLON // lon_count) % TILE == 0
            and lat_dev // (lon_count // halves) < 64
            and ord_dev % ORDER_GROUP == 0
            and lat_total % TILE == 0
        )
        return listed_plan(*arrays) if fits else dense_plan(*arrays)

    return jax.shard_map(
        on_device, mesh=mesh, in_specs=in_specs, out_specs=out_specs, check_vma=False
    )
```
